32 devices in a mesh: groups: 2 (over x), patch: 16 (over z, y, core).
Axes of the slice: x: 2, y: 2, z: 4, core: 2. Of those that a mesh axis runs over, the one named last changes fastest.
Arguments:
- query: bfloat16 [768, 1536], P(('groups', 'patch')), parts along dimension 0, may hold values from -140 to 140
- key_new: bfloat16 [768, 1536], P(('groups', 'patch')), parts along dimension 0, may hold values from -5 to 5
- value_new: bfloat16 [768, 1536], P(('groups', 'patch')), parts along dimension 0, may hold values from -5 to 5
- key_stale: bfloat16 [768, 1536], P('groups'), parts along dimension 0, may hold values from -4.2 to 4.2
- value_stale: bfloat16 [768, 1536], P('groups'), parts along dimension 0, may hold values from -4 to 4
- exponents: int32 [768, 24], P('groups'), parts along dimension 0, may hold values from -2 to 1
- w_out: bfloat16 [1536, 3072], P('patch'), may hold values from -0.15625 to 0.15625
- gate: float32 [6144], P('groups'), parts along dimension 0, may hold values from 0.5 to 4
Outputs:
- branch: bfloat16 [768, 3072], P(('groups', 'patch')), parts along dimension 0
The draws below stay inside these ranges and needn't reach their ends.
There are 2 independent parts, one for each index of `groups`. The reference program is written for one: setup_inputs(seed, part) draws one part's arguments, and reference() takes and returns one part's arrays. A program takes and returns all parts, laid end to end along the dimension named above; an argument that names none is the same for every part. Nothing has to cross between parts.
All inputs are finite; a program needn't handle non-finite values.
Results may differ from the reference program's by a relative error of at most 0.012.
Values may be sent and summed in bfloat16 or wider, within the bound.
No kernel may reach another device: no remote copies, remote signals or barrier semaphores. Data moves between devices by JAX's collectives and lax.ppermute only.
A program may use at most 128 MiB of HBM per device.

```python
import math
import jax
import jax.numpy as jnp
from jax import lax

HEADS = 12
HEAD_DIM = 128
DMODEL = 3072
TOK_DEV = 24
WIDTH = 1536
SEQ = 384


def shared_stale(key):
    return jnp.clip(jax.random.normal(key, (SEQ, WIDTH), jnp.float32), -4.0, 4.0)


def draw_key_stale(key, part):
    base = shared_stale(key)
    return base.astype(jnp.bfloat16)


def draw_key_new(key, part):
    stale = shared_stale(key)
    own = jax.random.fold_in(key, 1)
    noise = jax.random.normal(own, (SEQ, WIDTH), jnp.float32)
    fresh = jnp.clip(0.8 * stale + 0.6 * noise, -5.0, 5.0)
    return fresh.astype(jnp.bfloat16)


def shared_values_base(key):
    return jnp.clip(jax.random.normal(jax.random.fold_in(key, 7), (SEQ, WIDTH), jnp.float32), -4.0, 4.0).astype(jnp.bfloat16)


def draw_value_stale(key, part):
    key = jax.random.fold_in(key, 2)
    return shared_values_base(key)


def draw_value_new(key, part):
    stale = jnp.clip(jax.random.normal(jax.random.fold_in(jax.random.fold_in(key, 2), 7), (SEQ, WIDTH), jnp.float32), -4.0, 4.0)
    own = jax.random.fold_in(key, 3)
    noise = 0.6 * jax.random.normal(own, (SEQ, WIDTH), jnp.float32)
    return jnp.clip(0.8 * stale + noise, -5.0, 5.0).astype(jnp.bfloat16)


def draw_query(key, part):
    own = jax.random.fold_in(key, 4)
    values = jnp.clip(2.0 * jax.random.normal(own, (SEQ, WIDTH), jnp.float32), -8.0, 8.0)
    return values.astype(jnp.bfloat16)


def place_ends(values, key, low, high):
    longest = values.shape.index(max(values.shape))
    spots = []
    for shift in (0, 1):
        where = [jax.random.randint(jax.random.fold_in(key, axis), (), 0, length) for axis, length in enumerate(values.shape)]
        where[longest] = (where[longest] + shift) % values.shape[longest]
        spots.append(tuple(where))
    return values.at[spots[0]].set(low).at[spots[1]].set(high)


def block_levels(rng, dims, cuts, low, largest):
    factor_of = 1.0
    for position, parts in cuts:
        draws = jax.random.uniform(jax.random.fold_in(jax.random.fold_in(rng, 6), position), (parts,), jnp.float32, low / len(cuts), largest / len(cuts))
        factor_of = factor_of * jnp.repeat(jnp.exp(draws), dims[position] // parts).reshape((-1,) + (1,) * (len(dims) - 1 - position))
    return factor_of


def gaussian(rng, shape, width, reach, shards=(), kind=jnp.bfloat16):
    loudness = block_levels(rng, shape, shards, -0.22, 0.18) if shards else 1.0
    values = jax.random.normal(rng, shape, jnp.float32) * width * loudness
    return jnp.minimum(jnp.maximum(values, -reach), reach).astype(kind)


def setup_inputs(seed: int = 0, part: int = 0) -> dict:
    key_list = jax.random.split(jax.random.key(seed), 9)
    part_keys = jax.random.split(jax.random.fold_in(key_list[8], part), 9)
    return {
        "query": draw_query(jax.random.fold_in(jax.random.fold_in(key_list[8], part), 71), part),
        "key_new": draw_key_new(jax.random.fold_in(jax.random.fold_in(key_list[8], part), 71), part),
        "value_new": draw_value_new(jax.random.fold_in(jax.random.fold_in(key_list[8], part), 71), part),
        "key_stale": draw_key_stale(jax.random.fold_in(jax.random.fold_in(key_list[8], part), 71), part),
        "value_stale": draw_value_stale(jax.random.fold_in(jax.random.fold_in(key_list[8], part), 71), part),
        "exponents": place_ends(jax.random.randint(part_keys[5], (SEQ, 2 * HEADS), -2, 2), jax.random.fold_in(part_keys[5], 1), -2, 1).astype(jnp.int32),
        "w_out": gaussian(key_list[6], (WIDTH, DMODEL), WIDTH ** -0.5, 0.15625, ((0, 16),)),
        "gate": jnp.clip(jnp.exp(jax.random.uniform(part_keys[7], (DMODEL,), jnp.float32, math.log(0.5), math.log(4.0))), 0.5, 4.0),
    }


CLIP_LIMIT = 2.0


def encode(fresh, stale, powers):
    count = fresh.shape[0]
    heads = powers.shape[1]
    resid = fresh.astype(jnp.float32).reshape(count, heads, -1) - stale.astype(jnp.float32).reshape(count, heads, -1)
    codes = jnp.clip(resid * jnp.exp2(-powers)[:, :, None], -CLIP_LIMIT, CLIP_LIMIT)
    return codes.reshape(count, -1).astype(jnp.bfloat16)


def decode(codes, stale, powers):
    count = codes.shape[0]
    heads = powers.shape[1]
    shaped = stale.astype(jnp.float32).reshape(count, heads, -1) + jnp.exp2(powers)[:, :, None] * codes.astype(jnp.float32).reshape(count, heads, -1)
    return shaped.reshape(count, -1).astype(jnp.bfloat16)


def reference(query, key_new, value_new, key_stale, value_stale, exponents, w_out, gate):
    powers = exponents.astype(jnp.float32)
    key_powers = powers[:, :HEADS]
    value_powers = powers[:, HEADS:]
    keys = decode(encode(key_new, key_stale, key_powers), key_stale, key_powers)
    values = decode(encode(value_new, value_stale, value_powers), value_stale, value_powers)
    seq = keys.shape[0]
    keys3 = keys.reshape(seq, HEADS, HEAD_DIM).astype(jnp.float32)
    values3 = values.reshape(seq, HEADS, HEAD_DIM).astype(jnp.float32)
    inverse = 1.0 / (HEAD_DIM ** 0.5)
    blocks = query.reshape(seq // TOK_DEV, TOK_DEV, HEADS, HEAD_DIM)

    def attend(block):
        scores = jnp.einsum('qhd,khd->hqk', block.astype(jnp.float32), keys3) * inverse
        peak = jnp.max(scores, axis=2, keepdims=True)
        expo = jnp.exp(scores - peak)
        total = jnp.sum(expo, axis=2)
        weights = expo.astype(jnp.bfloat16)
        numer = jnp.einsum('hqk,khd->qhd', weights.astype(jnp.float32), values3)
        return (numer / jnp.transpose(total)[:, :, None]).astype(jnp.bfloat16)

    attended = lax.map(attend, blocks).reshape(seq, HEADS * HEAD_DIM)
    projected = jnp.dot(attended, w_out, preferred_element_type=jnp.float32)
    return (projected * gate[None, :]).astype(jnp.bfloat16)
```

```python
import functools
import math

import jax
import jax.numpy as jnp
from jax import lax
from jax.experimental import pallas as pl
from jax.experimental.pallas import tpu as pltpu
from jax.sharding import PartitionSpec as P

CLIP_LIMIT = 2.0
VMEM = pl.BlockSpec(memory_space=pltpu.VMEM)
ANY = pl.BlockSpec(memory_space=pl.ANY)


def prepare_kernel(
    groups,
    members,
    query_ref,
    key_ref,
    value_ref,
    kstale_ref,
    vstale_ref,
    expo_ref,
    *rest,
):
    outs = rest[:groups]
    kst, vst, est, packed, sems = rest[groups:]
    rows, width = query_ref.shape
    me = lax.axis_index("patch")
    first = pl.multiple_of((me // 2) * (2 * rows), 2 * rows)
    copies = [
        pltpu.make_async_copy(src.at[pl.ds(first, 2 * rows)], dst, sems.at[i])
        for i, (src, dst) in enumerate(((kstale_ref, kst), (vstale_ref, vst), (expo_ref, est)))
    ]
    for c in copies:
        c.start()
    for c in copies:
        c.wait()
    heads = expo_ref.shape[1] // 2
    dim = width // heads
    odd = me % 2 == 1

    def own(ref, cols):
        both = ref[:, cols].astype(jnp.float32)
        return jnp.where(odd, both[rows:], both[:rows])

    powers = jnp.where(odd, est[rows:, :], est[:rows, :]).astype(jnp.float32)
    scale = jnp.exp2(powers)
    inverse = jnp.exp2(-powers)
    for part, (fresh, stale) in enumerate(((key_ref, kst), (value_ref, vst))):
        for h in range(heads):
            cols = slice(h * dim, (h + 1) * dim)
            col = part * heads + h
            base = own(stale, cols)
            resid = fresh[:, cols].astype(jnp.float32) - base
            codes = jnp.clip(resid * inverse[:, col : col + 1], -CLIP_LIMIT, CLIP_LIMIT)
            codes = codes.astype(jnp.bfloat16).astype(jnp.float32)
            packed[part, :, cols] = (base + scale[:, col : col + 1] * codes).astype(jnp.bfloat16)
    share = width // groups
    for k in range(groups):
        target = (me // members) ^ k
        cols = pl.ds(pl.multiple_of(target * share, share), share)
        outs[k][:, :share] = query_ref[:, cols]
        outs[k][:, share : 2 * share] = packed[0, :, cols]
        outs[k][:, 2 * share :] = packed[1, :, cols]


def prepare(groups, members, query, key_new, value_new, key_stale, value_stale, exponents):
    rows, width = query.shape
    share = width // groups
    return pl.pallas_call(
        functools.partial(prepare_kernel, groups, members),
        out_shape=[jax.ShapeDtypeStruct((rows, 3 * share), jnp.bfloat16)] * groups,
        in_specs=[VMEM] * 3 + [pl.BlockSpec(memory_space=pltpu.HBM)] * 3,
        out_specs=[VMEM] * groups,
        scratch_shapes=[
            pltpu.VMEM((2 * rows, width), jnp.bfloat16),
            pltpu.VMEM((2 * rows, width), jnp.bfloat16),
            pltpu.VMEM((2 * rows, exponents.shape[1]), jnp.int32),
            pltpu.VMEM((2, rows, width), jnp.bfloat16),
            pltpu.SemaphoreType.DMA((3,)),
        ],
        cost_estimate=pl.CostEstimate(flops=10 * rows * width, bytes_accessed=14 * rows * width, transcendentals=0),
    )(query, key_new, value_new, key_stale, value_stale, exponents)


def attend_kernel(groups, members, dim, *refs):
    packs = refs[:groups]
    kvs = refs[groups : groups + members]
    att, kv = refs[groups + members :]
    share = att.shape[1]
    block = kvs[0].shape[0]
    for j in range(members):
        kv[j * block : (j + 1) * block] = kvs[j][...]
    queries = jnp.concatenate([p[:, :share].astype(jnp.float32) for p in packs], axis=0).astype(jnp.bfloat16)
    inverse = 1.0 / dim**0.5
    for h in range(share // dim):
        cols = slice(h * dim, (h + 1) * dim)
        scores = (
            lax.dot_general(queries[:, cols], kv[:, cols], (((1,), (1,)), ((), ())), preferred_element_type=jnp.float32)
            * inverse
        )
        peak = jnp.max(scores, axis=1, keepdims=True)
        expo = jnp.exp(scores - peak)
        total = jnp.sum(expo, axis=1, keepdims=True)
        numer = jnp.dot(
            expo.astype(jnp.bfloat16),
            kv[:, share + h * dim : share + (h + 1) * dim],
            preferred_element_type=jnp.float32,
        )
        att[:, cols] = (numer / total).astype(jnp.bfloat16)


def attend(groups, members, dim, packs, kvs):
    rows = packs[0].shape[0]
    share = packs[0].shape[1] // 3
    block = kvs[0].shape[0]
    return pl.pallas_call(
        functools.partial(attend_kernel, groups, members, dim),
        out_shape=jax.ShapeDtypeStruct((groups * rows, share), jnp.bfloat16),
        in_specs=[VMEM] * (groups + members),
        out_specs=VMEM,
        scratch_shapes=[pltpu.VMEM((members * block, 2 * share), jnp.bfloat16)],
        compiler_params=pltpu.CompilerParams(vmem_limit_bytes=24 * 1024 * 1024),
        cost_estimate=pl.CostEstimate(
            flops=4 * groups * rows * members * block * share,
            bytes_accessed=4 * members * block * share,
            transcendentals=groups * rows * members * block * share // dim,
        ),
    )(*packs, *kvs)


def project_kernel(groups, members, pieces, att, *refs):
    ws = refs[:pieces]
    outs = refs[pieces : pieces + groups]
    wide, sems = refs[pieces + groups :]
    depth = ws[0].shape[0]
    q = lax.axis_index("patch") % members
    copies = []
    for j in range(pieces):
        at = pl.multiple_of((q ^ j) * depth, depth) if pieces > 1 else 0
        copies.append(pltpu.make_async_copy(ws[j], wide.at[pl.ds(at, depth)], sems.at[j]))
    for c in copies:
        c.start()
    for c in copies:
        c.wait()
    rows, width = outs[0].shape
    tile = 512 if width % 512 == 0 else width
    for t in range(width // tile):
        cols = slice(t * tile, (t + 1) * tile)
        part = jnp.dot(att[...], wide[:, cols], preferred_element_type=jnp.float32)
        for k in range(groups):
            outs[k][:, cols] = part[k * rows : (k + 1) * rows].astype(outs[k].dtype)


def project(groups, members, att, ws):
    rows = att.shape[0] // groups
    share = att.shape[1]
    model = ws[0].shape[1]
    return pl.pallas_call(
        functools.partial(project_kernel, groups, members, len(ws)),
        out_shape=[jax.ShapeDtypeStruct((rows, model), jnp.float32)]
        + [jax.ShapeDtypeStruct((rows, model), jnp.bfloat16)] * (groups - 1),
        in_specs=[VMEM] + [ANY] * len(ws),
        out_specs=[VMEM] * groups,
        scratch_shapes=[pltpu.VMEM((share, model), jnp.bfloat16), pltpu.SemaphoreType.DMA((len(ws),))],
        compiler_params=pltpu.CompilerParams(vmem_limit_bytes=24 * 1024 * 1024),
        cost_estimate=pl.CostEstimate(
            flops=2 * groups * rows * share * model, bytes_accessed=2 * share * model, transcendentals=0
        ),
    )(att, *ws)


def per_device(patch, query, key_new, value_new, key_stale, value_stale, exponents, w_out, gate):
    heads = exponents.shape[1] // 2
    dim = query.shape[1] // heads
    groups = math.gcd(patch, heads)
    members = patch // groups
    share = query.shape[1] // groups

    def across(x, k):
        return lax.ppermute(x, "patch", [(p, ((p // members) ^ k) * members + p % members) for p in range(patch)])

    def within(x, j):
        return lax.ppermute(x, "patch", [(p, p ^ j) for p in range(patch)])

    def spread(x, after=None):
        pieces = {0: x}
        bit = members // 2
        while bit:
            for j in list(pieces):
                piece = pieces[j]
                if j and after is not None:
                    piece, _ = lax.optimization_barrier((piece, after))
                pieces[j ^ bit] = within(piece, bit)
            bit //= 2
        return [pieces[j] for j in range(members)]

    packs = prepare(groups, members, query, key_new, value_new, key_stale, value_stale, exponents)
    packs = [packs[0]] + [across(packs[k], k) for k in range(1, groups)]
    kvs = spread(jnp.concatenate([p[:, share:] for p in packs], axis=0))
    att = attend(groups, members, dim, packs, kvs)
    ws = spread(w_out, after=kvs)
    if w_out.shape[0] % 16:
        order = (lax.axis_index("patch") % members) ^ jnp.arange(members)
        ws = [jnp.stack(ws)[order].reshape(-1, w_out.shape[1])]
    parts = project(groups, members, att, ws)
    total = parts[0]
    for k in range(1, groups):
        total = total + across(parts[k], k).astype(jnp.float32)
    return (total * gate[None, :]).astype(jnp.bfloat16)


def solution(mesh):
    return jax.shard_map(
        functools.partial(per_device, mesh.shape["patch"]),
        mesh=mesh,
        in_specs=(
            P(("groups", "patch"), None),
            P(("groups", "patch"), None),
            P(("groups", "patch"), None),
            P("groups", None),
            P("groups", None),
            P("groups", None),
            P("patch", None),
            P("groups"),
        ),
        out_specs=P(("groups", "patch"), None),
        check_vma=False,
    )
```

```python
import functools
import math

import jax
import jax.numpy as jnp
from jax import lax
from jax.experimental import pallas as pl
from jax.experimental.pallas import tpu as pltpu
from jax.sharding import PartitionSpec as P

CLIP_LIMIT = 2.0
VMEM = pl.BlockSpec(memory_space=pltpu.VMEM)
ANY = pl.BlockSpec(memory_space=pl.ANY)
HBM = pl.BlockSpec(memory_space=pltpu.HBM)


def prepare_kernel(groups, query_ref, key_ref, value_ref, power_ref, kstale_ref, vstale_ref, qout, kvout, kst, vst, sems):
    rows, width = query_ref.shape
    me = lax.axis_index("patch")
    first = pl.multiple_of((me // 2) * (2 * rows), 2 * rows)
    copies = [
        pltpu.make_async_copy(src.at[pl.ds(first, 2 * rows)], dst, sems.at[i])
        for i, (src, dst) in enumerate(((kstale_ref, kst), (vstale_ref, vst)))
    ]
    for c in copies:
        c.start()
    heads = power_ref.shape[1] // 2
    dim = width // heads
    share = width // groups
    odd = me % 2 == 1
    powers = power_ref[...].astype(jnp.float32)
    scale = jnp.exp2(powers)
    inverse = jnp.exp2(-powers)
    for z in range(groups):
        qout[z] = query_ref[:, z * share : (z + 1) * share]
    for part, (fresh, stale) in enumerate(((key_ref, kst), (value_ref, vst))):
        copies[part].wait()
        for h in range(heads):
            cols = slice(h * dim, (h + 1) * dim)
            col = part * heads + h
            both = stale[:, cols].astype(jnp.float32)
            base = jnp.where(odd, both[rows:], both[:rows])
            resid = fresh[:, cols].astype(jnp.float32) - base
            codes = jnp.clip(resid * inverse[:, col : col + 1], -CLIP_LIMIT, CLIP_LIMIT)
            codes = codes.astype(jnp.bfloat16).astype(jnp.float32)
            at = part * share + (h * dim) % share
            kvout[h * dim // share, :, at : at + dim] = (base + scale[:, col : col + 1] * codes).astype(jnp.bfloat16)


def prepare(groups, query, key_new, value_new, powers, key_stale, value_stale):
    rows, width = query.shape
    share = width // groups
    return pl.pallas_call(
        functools.partial(prepare_kernel, groups),
        out_shape=[
            jax.ShapeDtypeStruct((groups, rows, share), jnp.bfloat16),
            jax.ShapeDtypeStruct((groups, rows, 2 * share), jnp.bfloat16),
        ],
        in_specs=[VMEM] * 4 + [HBM] * 2,
        out_specs=[VMEM] * 2,
        scratch_shapes=[
            pltpu.VMEM((2 * rows, width), jnp.bfloat16),
            pltpu.VMEM((2 * rows, width), jnp.bfloat16),
            pltpu.SemaphoreType.DMA((2,)),
        ],
        cost_estimate=pl.CostEstimate(flops=10 * rows * width, bytes_accessed=14 * rows * width, transcendentals=0),
    )(query, key_new, value_new, powers, key_stale, value_stale)


def attend_kernel(members, dim, *refs):
    query = refs[0]
    kvs = refs[1 : 1 + members]
    att, kv = refs[1 + members :]
    share = att.shape[1]
    block = kvs[0].shape[0]
    for j in range(members):
        kv[j * block : (j + 1) * block] = kvs[j][...]
    inverse = 1.0 / dim**0.5
    for h in range(share // dim):
        cols = slice(h * dim, (h + 1) * dim)
        scores = (
            lax.dot_general(query[:, cols], kv[:, cols], (((1,), (1,)), ((), ())), preferred_element_type=jnp.float32)
            * inverse
        )
        peak = jnp.max(scores, axis=1, keepdims=True)
        expo = jnp.exp(scores - peak)
        total = jnp.sum(expo, axis=1, keepdims=True)
        numer = jnp.dot(
            expo.astype(jnp.bfloat16),
            kv[:, share + h * dim : share + (h + 1) * dim],
            preferred_element_type=jnp.float32,
        )
        att[:, cols] = (numer / total).astype(jnp.bfloat16)


def attend(members, dim, query, kvs):
    rows, share = query.shape
    block = kvs[0].shape[0]
    return pl.pallas_call(
        functools.partial(attend_kernel, members, dim),
        out_shape=jax.ShapeDtypeStruct((rows, share), jnp.bfloat16),
        in_specs=[VMEM] * (1 + members),
        out_specs=VMEM,
        scratch_shapes=[pltpu.VMEM((members * block, 2 * share), jnp.bfloat16)],
        compiler_params=pltpu.CompilerParams(vmem_limit_bytes=24 * 1024 * 1024),
        cost_estimate=pl.CostEstimate(
            flops=4 * rows * members * block * share,
            bytes_accessed=4 * members * block * share,
            transcendentals=rows * members * block * share // dim,
        ),
    )(query, *kvs)


def project_kernel(groups, members, pieces, att, *refs):
    ws = refs[:pieces]
    out, wide, sems = refs[pieces:]
    depth = ws[0].shape[0]
    q = lax.axis_index("patch") % members
    copies = []
    for j in range(pieces):
        at = pl.multiple_of((q ^ j) * depth, depth) if pieces > 1 else 0
        copies.append(pltpu.make_async_copy(ws[j], wide.at[pl.ds(at, depth)], sems.at[j]))
    for c in copies:
        c.start()
    for c in copies:
        c.wait()
    _, rows, width = out.shape
    tile = 512 if width % 512 == 0 else width
    for t in range(width // tile):
        cols = slice(t * tile, (t + 1) * tile)
        part = jnp.dot(att[...], wide[:, cols], preferred_element_type=jnp.float32)
        for k in range(groups):
            out[k, :, cols] = part[k * rows : (k + 1) * rows].astype(out.dtype)


def project(groups, members, att, ws):
    rows = att.shape[0] // groups
    share = att.shape[1]
    model = ws[0].shape[1]
    return pl.pallas_call(
        functools.partial(project_kernel, groups, members, len(ws)),
        out_shape=jax.ShapeDtypeStruct((groups, rows, model), jnp.bfloat16),
        in_specs=[VMEM] + [ANY] * len(ws),
        out_specs=VMEM,
        scratch_shapes=[pltpu.VMEM((share, model), jnp.bfloat16), pltpu.SemaphoreType.DMA((len(ws),))],
        compiler_params=pltpu.CompilerParams(vmem_limit_bytes=24 * 1024 * 1024),
        cost_estimate=pl.CostEstimate(
            flops=2 * groups * rows * share * model, bytes_accessed=2 * share * model, transcendentals=0
        ),
    )(att, *ws)


def per_device(patch, query, key_new, value_new, key_stale, value_stale, exponents, w_out, gate):
    heads = exponents.shape[1] // 2
    dim = query.shape[1] // heads
    groups = math.gcd(patch, heads)
    members = patch // groups
    share = query.shape[1] // groups

    lines = [[z * members + q for z in range(groups)] for q in range(members)]

    def across(x):
        return lax.all_to_all(x, "patch", 0, 0, axis_index_groups=lines, tiled=True)

    def within(x, j):
        return lax.ppermute(x, "patch", [(p, p ^ j) for p in range(patch)])

    def spread(x, after=None):
        pieces = {0: x}
        bit = members // 2
        while bit:
            for j in list(pieces):
                piece = pieces[j]
                if j and after is not None:
                    piece, _ = lax.optimization_barrier((piece, after))
                pieces[j ^ bit] = within(piece, bit)
            bit //= 2
        return [pieces[j] for j in range(members)]

    rows = query.shape[0]
    powers = lax.dynamic_slice_in_dim(exponents, lax.axis_index("patch") * rows, rows, 0)
    queries, both = prepare(groups, query, key_new, value_new, powers, key_stale, value_stale)
    both = across(both)
    queries = across(queries)
    kvs = spread(both.reshape(groups * rows, 2 * share))
    att = attend(members, dim, queries.reshape(groups * rows, share), kvs)
    ws = spread(w_out, after=kvs)
    if w_out.shape[0] % 16:
        order = (lax.axis_index("patch") % members) ^ jnp.arange(members)
        ws = [jnp.stack(ws)[order].reshape(-1, w_out.shape[1])]
    parts = project(groups, members, att, ws)
    parts = across(parts)
    total = parts[0].astype(jnp.float32)
    for z in range(1, groups):
        total = total + parts[z].astype(jnp.float32)
    return (total * gate[None, :]).astype(jnp.bfloat16)


def solution(mesh):
    return jax.shard_map(
        functools.partial(per_device, mesh.shape["patch"]),
        mesh=mesh,
        in_specs=(
            P(("groups", "patch"), None),
            P(("groups", "patch"), None),
            P(("groups", "patch"), None),
            P("groups", None),
            P("groups", None),
            P("groups", None),
            P("patch", None),
            P("groups"),
        ),
        out_specs=P(("groups", "patch"), None),
        check_vma=False,
    )
```

```python
import functools
import math

import jax
import jax.numpy as jnp
from jax import lax
from jax.experimental import pallas as pl
from jax.experimental.pallas import tpu as pltpu
from jax.sharding import PartitionSpec as P

CLIP_LIMIT = 2.0
VMEM = pl.BlockSpec(memory_space=pltpu.VMEM)
ANY = pl.BlockSpec(memory_space=pl.ANY)
HBM = pl.BlockSpec(memory_space=pltpu.HBM)


def prepare_kernel(groups, members, chunks, *refs):
    sources, (w_ref,) = refs[:6], refs[6:7]
    qouts, kvouts, wouts = refs[7 : 7 + groups], refs[7 + groups : 7 + 2 * groups], refs[7 + 2 * groups :][:chunks]
    query, key_new, value_new, kst, vst, est, packed, sems = refs[7 + 2 * groups + chunks :]
    rows, width = query.shape
    me = lax.axis_index("patch")
    first = pl.multiple_of((me // 2) * (2 * rows), 2 * rows)
    pair = pl.ds(first, 2 * rows)
    views = [sources[0], sources[1], sources[2], sources[3].at[pair], sources[4].at[pair], sources[5]]
    order = (5, 3, 1, 4, 2, 0)
    copies = {
        i: pltpu.make_async_copy(views[i], (query, key_new, value_new, kst, vst, est)[i], sems.at[i]) for i in order
    }
    for i in order:
        copies[i].start()
    part = w_ref.shape[1] // chunks
    moves = [
        pltpu.make_async_copy(w_ref.at[:, pl.ds(i * part, part)], wouts[i], sems.at[6 + i]) for i in range(chunks)
    ]
    for m in moves:
        m.start()
    heads = est.shape[0] // 2
    dim = width // heads
    share = width // groups
    odd = me % 2 == 1
    copies[5].wait()
    spot = lax.broadcasted_iota(jnp.int32, (rows, est.shape[1]), 1) == me * rows + lax.broadcasted_iota(
        jnp.int32, (rows, est.shape[1]), 0
    )
    powers = lax.dot_general(
        spot.astype(jnp.float32).astype(jnp.bfloat16),
        est[...].astype(jnp.float32).astype(jnp.bfloat16),
        (((1,), (1,)), ((), ())),
        preferred_element_type=jnp.float32,
    )
    scale = jnp.exp2(powers)
    inverse = jnp.exp2(-powers)
    for side, (fresh, stale) in enumerate(((key_new, kst), (value_new, vst))):
        copies[1 + side].wait()
        copies[3 + side].wait()
        for h in range(heads):
            cols = slice(h * dim, (h + 1) * dim)
            col = side * heads + h
            both = stale[:, cols].astype(jnp.float32)
            base = jnp.where(odd, both[rows:], both[:rows])
            resid = fresh[:, cols].astype(jnp.float32) - base
            codes = jnp.clip(resid * inverse[:, col : col + 1], -CLIP_LIMIT, CLIP_LIMIT)
            codes = codes.astype(jnp.bfloat16).astype(jnp.float32)
            at = side * share + (h * dim) % share
            packed[h * dim // share, :, at : at + dim] = (base + scale[:, col : col + 1] * codes).astype(jnp.bfloat16)
    copies[0].wait()
    for k in range(groups):
        target = (me // members) ^ k
        kvouts[k][...] = packed[target]
        qouts[k][...] = query[:, pl.ds(pl.multiple_of(target * share, share), share)]
    for m in moves:
        m.wait()


def prepare(groups, members, chunks, query, key_new, value_new, key_stale, value_stale, powers, w_out):
    rows, width = query.shape
    share = width // groups
    depth, model = w_out.shape
    outs = (
        [((rows, share), jnp.bfloat16)] * groups
        + [((rows, 2 * share), jnp.bfloat16)] * groups
        + [((depth, model // chunks), jnp.bfloat16)] * chunks
    )
    result = pl.pallas_call(
        functools.partial(prepare_kernel, groups, members, chunks),
        out_shape=[jax.ShapeDtypeStruct(*o) for o in outs],
        in_specs=[HBM] * 7,
        out_specs=[VMEM] * len(outs),
        scratch_shapes=[pltpu.VMEM((rows, width), jnp.bfloat16)] * 3
        + [pltpu.VMEM((2 * rows, width), jnp.bfloat16)] * 2
        + [
            pltpu.VMEM(powers.shape, jnp.int32),
            pltpu.VMEM((groups, rows, 2 * share), jnp.bfloat16),
            pltpu.SemaphoreType.DMA((6 + chunks,)),
        ],
        compiler_params=pltpu.CompilerParams(vmem_limit_bytes=24 * 1024 * 1024),
        cost_estimate=pl.CostEstimate(
            flops=10 * rows * width, bytes_accessed=14 * rows * width + 4 * depth * model, transcendentals=0
        ),
    )(query, key_new, value_new, key_stale, value_stale, powers, w_out)
    return result[:groups], result[groups : 2 * groups], result[2 * groups :]


def attend_kernel(groups, members, dim, *refs):
    queries = refs[:groups]
    kvs = refs[groups : groups + members]
    att, kv = refs[groups + members :]
    share = att.shape[1]
    block = kvs[0].shape[0]
    for j in range(members):
        kv[j * block : (j + 1) * block] = kvs[j][...]
    query = jnp.concatenate([q[...].astype(jnp.float32) for q in queries], axis=0).astype(jnp.bfloat16)
    inverse = 1.0 / dim**0.5
    for h in range(share // dim):
        cols = slice(h * dim, (h + 1) * dim)
        scores = (
            lax.dot_general(query[:, cols], kv[:, cols], (((1,), (1,)), ((), ())), preferred_element_type=jnp.float32)
            * inverse
        )
        peak = jnp.max(scores, axis=1, keepdims=True)
        expo = jnp.exp(scores - peak)
        total = jnp.sum(expo, axis=1, keepdims=True)
        numer = jnp.dot(
            expo.astype(jnp.bfloat16),
            kv[:, share + h * dim : share + (h + 1) * dim],
            preferred_element_type=jnp.float32,
        )
        att[:, cols] = (numer / total).astype(jnp.bfloat16)


def attend(groups, members, dim, queries, kvs):
    rows, share = queries[0].shape
    block = kvs[0].shape[0]
    return pl.pallas_call(
        functools.partial(attend_kernel, groups, members, dim),
        out_shape=jax.ShapeDtypeStruct((groups * rows, share), jnp.bfloat16),
        in_specs=[VMEM] * (groups + members),
        out_specs=VMEM,
        scratch_shapes=[pltpu.VMEM((members * block, 2 * share), jnp.bfloat16)],
        compiler_params=pltpu.CompilerParams(vmem_limit_bytes=24 * 1024 * 1024),
        cost_estimate=pl.CostEstimate(
            flops=4 * groups * rows * members * block * share,
            bytes_accessed=4 * members * block * share,
            transcendentals=groups * rows * members * block * share // dim,
        ),
    )(*queries, *kvs)


def project_kernel(groups, members, pieces, att, *refs):
    ws = refs[:pieces]
    outs = refs[pieces : pieces + groups]
    wide, sems = refs[pieces + groups :]
    depth = ws[0].shape[0]
    q = lax.axis_index("patch") % members
    copies = []
    for j in range(pieces):
        at = pl.multiple_of((q ^ j) * depth, depth) if pieces > 1 else 0
        copies.append(pltpu.make_async_copy(ws[j], wide.at[pl.ds(at, depth)], sems.at[j]))
    for c in copies:
        c.start()
    for c in copies:
        c.wait()
    rows, width = outs[0].shape
    tile = 512 if width % 512 == 0 else width
    for t in range(width // tile):
        cols = slice(t * tile, (t + 1) * tile)
        part = jnp.dot(att[...], wide[:, cols], preferred_element_type=jnp.float32)
        for k in range(groups):
            outs[k][:, cols] = part[k * rows : (k + 1) * rows].astype(outs[k].dtype)


def project(groups, members, att, ws):
    rows = att.shape[0] // groups
    share = att.shape[1]
    model = ws[0].shape[1]
    return pl.pallas_call(
        functools.partial(project_kernel, groups, members, len(ws)),
        out_shape=[jax.ShapeDtypeStruct((rows, model), jnp.float32)]
        + [jax.ShapeDtypeStruct((rows, model), jnp.bfloat16)] * (groups - 1),
        in_specs=[VMEM] + [ANY] * len(ws),
        out_specs=[VMEM] * groups,
        scratch_shapes=[pltpu.VMEM((share, model), jnp.bfloat16), pltpu.SemaphoreType.DMA((len(ws),))],
        compiler_params=pltpu.CompilerParams(vmem_limit_bytes=24 * 1024 * 1024),
        cost_estimate=pl.CostEstimate(
            flops=2 * groups * rows * share * model, bytes_accessed=2 * share * model, transcendentals=0
        ),
    )(att, *ws)


def after(x, *others):
    return lax.optimization_barrier((x, *others))[0]


def per_device(patch, query, key_new, value_new, key_stale, value_stale, exponents, w_out, gate):
    heads = exponents.shape[1] // 2
    dim = query.shape[1] // heads
    groups = math.gcd(patch, heads)
    members = patch // groups
    chunks = 2

    def across(x, k):
        return lax.ppermute(x, "patch", [(p, ((p // members) ^ k) * members + p % members) for p in range(patch)])

    def within(x, j):
        return lax.ppermute(x, "patch", [(p, p ^ j) for p in range(patch)])

    def spread(pieces, bit):
        while bit:
            for j in list(pieces):
                pieces[j ^ bit] = within(pieces[j], bit)
            bit //= 2
        return [pieces[j] for j in range(members)]

    far = members // 2
    queries, fresh, ws = prepare(
        groups, members, chunks, query, key_new, value_new, key_stale, value_stale, exponents.T, w_out
    )
    fresh = [fresh[0]] + [across(fresh[k], k) for k in range(1, groups)]
    both = jnp.concatenate(fresh, axis=0)
    kvs = spread({0: both}, far)
    queries = [queries[0]] + [across(after(queries[k], both), k) for k in range(1, groups)]
    att = attend(groups, members, dim, queries, kvs)
    sums = []
    done = None
    for c in range(chunks):
        own = ws[c] if c == 0 else after(ws[c], both)
        other = within(own, far)
        if done is not None:
            other = after(other, *done)
        pieces = spread({0: ws[c], far: other}, far // 2)
        if w_out.shape[0] % 16:
            order = (lax.axis_index("patch") % members) ^ jnp.arange(members)
            pieces = [jnp.stack(pieces)[order].reshape(-1, pieces[0].shape[1])]
        done = project(groups, members, att, pieces)
        total = done[0]
        for k in range(1, groups):
            total = total + across(done[k], k).astype(jnp.float32)
        sums.append(total)
    return (jnp.concatenate(sums, axis=1) * gate[None, :]).astype(jnp.bfloat16)


def solution(mesh):
    return jax.shard_map(
        functools.partial(per_device, mesh.shape["patch"]),
        mesh=mesh,
        in_specs=(
            P(("groups", "patch"), None),
            P(("groups", "patch"), None),
            P(("groups", "patch"), None),
            P("groups", None),
            P("groups", None),
            P("groups", None),
            P("patch", None),
            P("groups"),
        ),
        out_specs=P(("groups", "patch"), None),
        check_vma=False,
    )
```

```python
import functools
import math

import jax
import jax.numpy as jnp
from jax import lax
from jax.experimental import pallas as pl
from jax.experimental.pallas import tpu as pltpu
from jax.sharding import PartitionSpec as P

CLIP_LIMIT = 2.0
VMEM = pl.BlockSpec(memory_space=pltpu.VMEM)
ANY = pl.BlockSpec(memory_space=pl.ANY)
HBM = pl.BlockSpec(memory_space=pltpu.HBM)


def prepare_kernel(groups, members, chunks, *refs):
    sources, w_ref = refs[:6], refs[6]
    outs = refs[7:]
    qout, fulls, kvouts, wouts = outs[0], outs[:groups], outs[groups : 2 * groups], outs[2 * groups : 2 * groups + chunks]
    query, key_new, value_new, kst, vst, est, packed, sems = outs[2 * groups + chunks :]
    rows, width = query.shape
    me = lax.axis_index("patch")
    first = pl.multiple_of((me // 2) * (2 * rows), 2 * rows)
    pair = pl.ds(first, 2 * rows)
    views = [sources[0], sources[1], sources[2], sources[3].at[pair], sources[4].at[pair], sources[5]]
    order = (5, 3, 1, 4, 2, 0)
    copies = {
        i: pltpu.make_async_copy(views[i], (query, key_new, value_new, kst, vst, est)[i], sems.at[i]) for i in order
    }
    for i in order:
        copies[i].start()
    part = w_ref.shape[1] // chunks
    moves = [
        pltpu.make_async_copy(w_ref.at[:, pl.ds(i * part, part)], wouts[i], sems.at[6 + i]) for i in range(chunks)
    ]
    for m in moves:
        m.start()
    heads = est.shape[0] // 2
    dim = width // heads
    share = width // groups
    odd = me % 2 == 1
    copies[5].wait()
    spot = lax.broadcasted_iota(jnp.int32, (rows, est.shape[1]), 1) == me * rows + lax.broadcasted_iota(
        jnp.int32, (rows, est.shape[1]), 0
    )
    powers = lax.dot_general(
        spot.astype(jnp.float32).astype(jnp.bfloat16),
        est[...].astype(jnp.float32).astype(jnp.bfloat16),
        (((1,), (1,)), ((), ())),
        preferred_element_type=jnp.float32,
    )
    scale = jnp.exp2(powers)
    inverse = jnp.exp2(-powers)
    for side, (fresh, stale) in enumerate(((key_new, kst), (value_new, vst))):
        copies[1 + side].wait()
        copies[3 + side].wait()
        for h in range(heads):
            cols = slice(h * dim, (h + 1) * dim)
            col = side * heads + h
            both = stale[:, cols].astype(jnp.float32)
            base = jnp.where(odd, both[rows:], both[:rows])
            resid = fresh[:, cols].astype(jnp.float32) - base
            codes = jnp.clip(resid * inverse[:, col : col + 1], -CLIP_LIMIT, CLIP_LIMIT)
            codes = codes.astype(jnp.bfloat16).astype(jnp.float32)
            at = side * share + (h * dim) % share
            packed[h * dim // share, :, at : at + dim] = (base + scale[:, col : col + 1] * codes).astype(jnp.bfloat16)
    copies[0].wait()
    for k in range(groups):
        target = (me // members) ^ k
        kvouts[k][...] = packed[target]
        wanted = query[:, pl.ds(pl.multiple_of(target * share, share), share)]
        if k == 0:
            qout[...] = wanted
        else:
            fulls[k][:, :share] = wanted
            fulls[k][:, share:] = packed[target]
    for m in moves:
        m.wait()


def prepare(groups, members, chunks, query, key_new, value_new, key_stale, value_stale, powers, w_out):
    rows, width = query.shape
    share = width // groups
    depth, model = w_out.shape
    outs = (
        [((rows, share), jnp.bfloat16)]
        + [((rows, 3 * share), jnp.bfloat16)] * (groups - 1)
        + [((rows, 2 * share), jnp.bfloat16)] * groups
        + [((depth, model // chunks), jnp.bfloat16)] * chunks
    )
    sources = (query, key_new, value_new, key_stale, value_stale, powers, w_out)
    result = pl.pallas_call(
        functools.partial(prepare_kernel, groups, members, chunks),
        out_shape=[jax.ShapeDtypeStruct(*o) for o in outs],
        in_specs=[HBM] * 7,
        out_specs=[VMEM] * len(outs),
        scratch_shapes=[pltpu.VMEM((rows, width), jnp.bfloat16)] * 3
        + [pltpu.VMEM((2 * rows, width), jnp.bfloat16)] * 2
        + [
            pltpu.VMEM(powers.shape, jnp.int32),
            pltpu.VMEM((groups, rows, 2 * share), jnp.bfloat16),
            pltpu.SemaphoreType.DMA((6 + chunks,)),
        ],
        compiler_params=pltpu.CompilerParams(vmem_limit_bytes=24 * 1024 * 1024),
        cost_estimate=pl.CostEstimate(
            flops=10 * rows * width, bytes_accessed=14 * rows * width + 4 * depth * model, transcendentals=0
        ),
    )(*(pltpu.with_memory_space_constraint(x, pltpu.HBM) for x in sources))
    return result[:groups], result[groups : 2 * groups], result[2 * groups :]


def attend_kernel(groups, dim, *refs):
    queries = refs[:groups]
    kvs = refs[groups:-2]
    att, kv = refs[-2:]
    share = att.shape[1]
    block = kvs[0].shape[0]
    for j in range(len(kvs)):
        kv[j * block : (j + 1) * block] = kvs[j][...]
    query = jnp.concatenate([q[:, :share].astype(jnp.float32) for q in queries], axis=0).astype(jnp.bfloat16)
    inverse = 1.0 / dim**0.5
    for h in range(share // dim):
        cols = slice(h * dim, (h + 1) * dim)
        scores = (
            lax.dot_general(query[:, cols], kv[:, cols], (((1,), (1,)), ((), ())), preferred_element_type=jnp.float32)
            * inverse
        )
        peak = jnp.max(scores, axis=1, keepdims=True)
        expo = jnp.exp(scores - peak)
        total = jnp.sum(expo, axis=1, keepdims=True)
        numer = jnp.dot(
            expo.astype(jnp.bfloat16),
            kv[:, share + h * dim : share + (h + 1) * dim],
            preferred_element_type=jnp.float32,
        )
        att[:, cols] = (numer / total).astype(jnp.bfloat16)


def attend(groups, dim, queries, kvs):
    rows, share = queries[0].shape
    block = kvs[0].shape[0]
    pieces = len(kvs)
    return pl.pallas_call(
        functools.partial(attend_kernel, groups, dim),
        out_shape=jax.ShapeDtypeStruct((groups * rows, share), jnp.bfloat16),
        in_specs=[VMEM] * (groups + pieces),
        out_specs=VMEM,
        scratch_shapes=[pltpu.VMEM((pieces * block, 2 * share), jnp.bfloat16)],
        compiler_params=pltpu.CompilerParams(vmem_limit_bytes=24 * 1024 * 1024),
        cost_estimate=pl.CostEstimate(
            flops=4 * groups * rows * pieces * block * share,
            bytes_accessed=4 * pieces * block * share,
            transcendentals=groups * rows * pieces * block * share // dim,
        ),
    )(*queries, *kvs)


def project_kernel(groups, members, pieces, att, *refs):
    ws = refs[:pieces]
    outs = refs[pieces : pieces + groups]
    wide, sems = refs[pieces + groups :]
    depth = ws[0].shape[0]
    q = lax.axis_index("patch") % members
    copies = []
    for j in range(pieces):
        at = pl.multiple_of((q ^ j) * depth, depth) if pieces > 1 else 0
        copies.append(pltpu.make_async_copy(ws[j], wide.at[pl.ds(at, depth)], sems.at[j]))
    for c in copies:
        c.start()
    for c in copies:
        c.wait()
    rows, width = outs[0].shape
    tile = 512 if width % 512 == 0 else width
    for t in range(width // tile):
        cols = slice(t * tile, (t + 1) * tile)
        part = jnp.dot(att[...], wide[:, cols], preferred_element_type=jnp.float32)
        for k in range(groups):
            outs[k][:, cols] = part[k * rows : (k + 1) * rows].astype(outs[k].dtype)


def project(groups, members, att, ws):
    rows = att.shape[0] // groups
    share = att.shape[1]
    model = ws[0].shape[1]
    return pl.pallas_call(
        functools.partial(project_kernel, groups, members, len(ws)),
        out_shape=[jax.ShapeDtypeStruct((rows, model), jnp.float32)]
        + [jax.ShapeDtypeStruct((rows, model), jnp.bfloat16)] * (groups - 1),
        in_specs=[VMEM] + [ANY] * len(ws),
        out_specs=[VMEM] * groups,
        scratch_shapes=[pltpu.VMEM((share, model), jnp.bfloat16), pltpu.SemaphoreType.DMA((len(ws),))],
        compiler_params=pltpu.CompilerParams(vmem_limit_bytes=24 * 1024 * 1024),
        cost_estimate=pl.CostEstimate(
            flops=2 * groups * rows * share * model, bytes_accessed=2 * share * model, transcendentals=0
        ),
    )(att, *ws)


def after(x, *others):
    return lax.optimization_barrier((x, *others))[0]


def per_device(patch, query, key_new, value_new, key_stale, value_stale, exponents, w_out, gate):
    heads = exponents.shape[1] // 2
    dim = query.shape[1] // heads
    groups = math.gcd(patch, heads)
    members = patch // groups
    chunks = 2

    def send(x, k, j):
        return lax.ppermute(x, "patch", [(p, ((p // members) ^ k) * members + (p % members) ^ j) for p in range(patch)])

    def spread(pieces, bit):
        while bit:
            for j in list(pieces):
                pieces[j ^ bit] = send(pieces[j], 0, bit)
            bit //= 2
        return [pieces[j] for j in range(members)]

    far = members // 2
    rows = query.shape[0]
    share = query.shape[1] // groups
    result = prepare(groups, members, chunks, query, key_new, value_new, key_stale, value_stale, exponents.T, w_out)
    queries, fresh, ws = result
    others = [send(ws[0], 0, far)]
    queries = list(queries)
    halves = []
    for ks in (range(groups - 1, groups // 2 - 1, -1), range(groups // 2 - 1, -1, -1)):
        half = []
        for k in ks:
            for j in range(members - 2, -1, -2):
                if j:
                    half.append(send(fresh[k], k, j))
                elif k:
                    queries[k] = send(queries[k], k, 0)
                    half.append(queries[k][:, share:])
                else:
                    half.append(fresh[0])
        halves.append(jnp.concatenate(half, axis=0))
    kvs = halves + [send(h, 0, 1) for h in halves]
    for c in range(1, chunks):
        others.append(send(after(ws[c], halves[0]), 0, far))
    att = attend(groups, dim, queries, kvs)
    sums = []
    done = None
    for c in range(chunks):
        other = others[c]
        other = after(other, *(done if c else halves))
        pieces = spread({0: ws[c], far: other}, far // 2)
        if w_out.shape[0] % 16:
            order = (lax.axis_index("patch") % members) ^ jnp.arange(members)
            pieces = [jnp.stack(pieces)[order].reshape(-1, pieces[0].shape[1])]
        done = project(groups, members, att, pieces)
        total = done[0]
        for k in range(1, groups):
            total = total + send(done[k], k, 0).astype(jnp.float32)
        sums.append(total)
    return (jnp.concatenate(sums, axis=1) * gate[None, :]).astype(jnp.bfloat16)


def solution(mesh):
    return jax.shard_map(
        functools.partial(per_device, mesh.shape["patch"]),
        mesh=mesh,
        in_specs=(
            P(("groups", "patch"), None),
            P(("groups", "patch"), None),
            P(("groups", "patch"), None),
            P("groups", None),
            P("groups", None),
            P("groups", None),
            P("patch", None),
            P("groups"),
        ),
        out_specs=P(("groups", "patch"), None),
        check_vma=False,
    )
```

```python
import functools
import math

import jax
import jax.numpy as jnp
from jax import lax
from jax.experimental import pallas as pl
from jax.experimental.pallas import tpu as pltpu
from jax.sharding import PartitionSpec as P

CLIP_LIMIT = 2.0
VMEM = pl.BlockSpec(memory_space=pltpu.VMEM)
ANY = pl.BlockSpec(memory_space=pl.ANY)
HBM = pl.BlockSpec(memory_space=pltpu.HBM)


def prepare_kernel(groups, members, chunks, *refs):
    sources, w_ref = refs[:6], refs[6]
    outs = refs[7:]
    qout, kvout, fulls = outs[0], outs[1], outs[1 : 1 + groups]
    wout, wparts = outs[1 + groups], outs[2 + groups : 2 + groups + chunks]
    query, key_new, value_new, kst, vst, est, packed, sems = outs[2 + groups + chunks :]
    rows, width = query.shape
    me = lax.axis_index("patch")
    first = pl.multiple_of((me // 2) * (2 * rows), 2 * rows)
    pair = pl.ds(first, 2 * rows)
    views = [sources[0], sources[1], sources[2], sources[3].at[pair], sources[4].at[pair], sources[5]]
    order = (5, 3, 1, 4, 2, 0)
    copies = {
        i: pltpu.make_async_copy(views[i], (query, key_new, value_new, kst, vst, est)[i], sems.at[i]) for i in order
    }
    for i in order:
        copies[i].start()
    moves = [pltpu.make_async_copy(w_ref, wout, sems.at[6])]
    for i in range(chunks):
        size, part = wparts[i].shape
        left = sum(w.shape[1] for w in wparts[:i])
        top = pl.multiple_of((lax.axis_index("groups") % 2) * size, size) if size < w_ref.shape[0] else 0
        view = w_ref.at[pl.ds(top, size), pl.ds(left, part)]
        moves.append(pltpu.make_async_copy(view, wparts[i], sems.at[7 + i]))
    for m in moves:
        m.start()
    heads = est.shape[0] // 2
    dim = width // heads
    share = width // groups
    odd = me % 2 == 1
    copies[5].wait()
    spot = lax.broadcasted_iota(jnp.int32, (rows, est.shape[1]), 1) == me * rows + lax.broadcasted_iota(
        jnp.int32, (rows, est.shape[1]), 0
    )
    powers = lax.dot_general(
        spot.astype(jnp.float32).astype(jnp.bfloat16),
        est[...].astype(jnp.float32).astype(jnp.bfloat16),
        (((1,), (1,)), ((), ())),
        preferred_element_type=jnp.float32,
    )
    scale = jnp.exp2(powers)
    inverse = jnp.exp2(-powers)
    for side, (fresh, stale) in enumerate(((key_new, kst), (value_new, vst))):
        copies[1 + side].wait()
        copies[3 + side].wait()
        for h in range(heads):
            cols = slice(h * dim, (h + 1) * dim)
            col = side * heads + h
            both = stale[:, cols].astype(jnp.float32)
            base = jnp.where(odd, both[rows:], both[:rows])
            resid = fresh[:, cols].astype(jnp.float32) - base
            codes = jnp.clip(resid * inverse[:, col : col + 1], -CLIP_LIMIT, CLIP_LIMIT)
            codes = codes.astype(jnp.bfloat16).astype(jnp.float32)
            at = side * share + (h * dim) % share
            packed[h * dim // share, :, at : at + dim] = (base + scale[:, col : col + 1] * codes).astype(jnp.bfloat16)
    copies[0].wait()
    for k in range(groups):
        target = (me // members) ^ k
        wanted = query[:, pl.ds(pl.multiple_of(target * share, share), share)]
        if k == 0:
            qout[...] = wanted
            kvout[...] = packed[target]
        else:
            fulls[k][:, :share] = wanted
            fulls[k][:, share:] = packed[target]
    for m in moves:
        m.wait()


def prepare(groups, members, chunks, split, query, key_new, value_new, key_stale, value_stale, powers, w_out):
    rows, width = query.shape
    share = width // groups
    depth, model = w_out.shape
    outs = (
        [((rows, share), jnp.bfloat16), ((rows, 2 * share), jnp.bfloat16)]
        + [((rows, 3 * share), jnp.bfloat16)] * (groups - 1)
        + [((depth, model), jnp.bfloat16)]
        + [((depth // split, c), jnp.bfloat16) for c in chunks]
    )
    sources = (query, key_new, value_new, key_stale, value_stale, powers, w_out)
    result = pl.pallas_call(
        functools.partial(prepare_kernel, groups, members, len(chunks)),
        out_shape=[jax.ShapeDtypeStruct(*o) for o in outs],
        in_specs=[HBM] * 7,
        out_specs=[VMEM] * len(outs),
        scratch_shapes=[pltpu.VMEM((rows, width), jnp.bfloat16)] * 3
        + [pltpu.VMEM((2 * rows, width), jnp.bfloat16)] * 2
        + [
            pltpu.VMEM(powers.shape, jnp.int32),
            pltpu.VMEM((groups, rows, 2 * share), jnp.bfloat16),
            pltpu.SemaphoreType.DMA((7 + len(chunks),)),
        ],
        compiler_params=pltpu.CompilerParams(vmem_limit_bytes=24 * 1024 * 1024),
        cost_estimate=pl.CostEstimate(
            flops=10 * rows * width, bytes_accessed=14 * rows * width + 4 * depth * model, transcendentals=0
        ),
    )(*(pltpu.with_memory_space_constraint(x, pltpu.HBM) for x in sources))
    return result[0], result[1 : 1 + groups], result[1 + groups], result[2 + groups :]


def attend_kernel(groups, dim, *refs):
    queries = refs[:groups]
    kvs = refs[groups:-2]
    att, kv = refs[-2:]
    share = att.shape[1]
    block = kvs[0].shape[0]
    for j in range(len(kvs)):
        kv[j * block : (j + 1) * block] = kvs[j][...]
    query = jnp.concatenate([q[:, :share].astype(jnp.float32) for q in queries], axis=0).astype(jnp.bfloat16)
    inverse = 1.0 / dim**0.5
    for h in range(share // dim):
        cols = slice(h * dim, (h + 1) * dim)
        scores = (
            lax.dot_general(query[:, cols], kv[:, cols], (((1,), (1,)), ((), ())), preferred_element_type=jnp.float32)
            * inverse
        )
        peak = jnp.max(scores, axis=1, keepdims=True)
        expo = jnp.exp(scores - peak)
        total = jnp.sum(expo, axis=1, keepdims=True)
        numer = jnp.dot(
            expo.astype(jnp.bfloat16),
            kv[:, share + h * dim : share + (h + 1) * dim],
            preferred_element_type=jnp.float32,
        )
        att[:, cols] = (numer / total).astype(jnp.bfloat16)


def attend(groups, dim, queries, kvs):
    rows, share = queries[0].shape
    block = kvs[0].shape[0]
    pieces = len(kvs)
    return pl.pallas_call(
        functools.partial(attend_kernel, groups, dim),
        out_shape=jax.ShapeDtypeStruct((groups * rows, share), jnp.bfloat16),
        in_specs=[VMEM] * (groups + pieces),
        out_specs=VMEM,
        scratch_shapes=[pltpu.VMEM((pieces * block, 2 * share), jnp.bfloat16)],
        compiler_params=pltpu.CompilerParams(vmem_limit_bytes=24 * 1024 * 1024),
        cost_estimate=pl.CostEstimate(
            flops=4 * groups * rows * pieces * block * share,
            bytes_accessed=4 * pieces * block * share,
            transcendentals=groups * rows * pieces * block * share // dim,
        ),
    )(*queries, *kvs)


def project_kernel(groups, members, places, att, *refs):
    ws = refs[: len(places)]
    outs = refs[len(places) : len(places) + groups]
    wide, sems = refs[len(places) + groups :]
    q = lax.axis_index("patch") % members
    side = lax.axis_index("groups") % 2
    copies = []
    for i, (piece, (j, flip, col)) in enumerate(zip(ws, places)):
        size, part = piece.shape
        row = 0
        if j is not None:
            row = (q ^ j) * (size if flip is None else 2 * size)
            if flip is not None:
                row = row + (side ^ flip) * size
            row = pl.multiple_of(row, size)
        view = wide.at[pl.ds(row, size), pl.ds(col, part)]
        copies.append(pltpu.make_async_copy(piece, view, sems.at[i]))
    for c in copies:
        c.start()
    for c in copies:
        c.wait()
    rows, width = outs[0].shape
    tile = 512 if width % 512 == 0 else width
    for t in range(width // tile):
        cols = slice(t * tile, (t + 1) * tile)
        part = jnp.dot(att[...], wide[:, cols], preferred_element_type=jnp.float32)
        for k in range(groups):
            outs[k][:, cols] = part[k * rows : (k + 1) * rows].astype(outs[k].dtype)


def project(groups, members, att, model, pieces, places):
    rows = att.shape[0] // groups
    share = att.shape[1]
    return pl.pallas_call(
        functools.partial(project_kernel, groups, members, places),
        out_shape=[jax.ShapeDtypeStruct((rows, model), jnp.float32)]
        + [jax.ShapeDtypeStruct((rows, model), jnp.bfloat16)] * (groups - 1),
        in_specs=[VMEM] + [ANY] * len(pieces),
        out_specs=[VMEM] * groups,
        scratch_shapes=[pltpu.VMEM((share, model), jnp.bfloat16), pltpu.SemaphoreType.DMA((len(pieces),))],
        compiler_params=pltpu.CompilerParams(vmem_limit_bytes=24 * 1024 * 1024),
        cost_estimate=pl.CostEstimate(
            flops=2 * groups * rows * share * model, bytes_accessed=2 * share * model, transcendentals=0
        ),
    )(att, *pieces)


def after(x, *others):
    if not others:
        return x
    return lax.optimization_barrier((x, *others))[0]


def per_device(parts, patch, query, key_new, value_new, key_stale, value_stale, exponents, w_out, gate):
    heads = exponents.shape[1] // 2
    rows, width = query.shape
    dim = width // heads
    groups = math.gcd(patch, heads)
    members = patch // groups
    share = width // groups
    depth, model = w_out.shape
    far = members // 2
    shared = parts % 2 == 0 and depth % 32 == 0
    chunks = [2 * model // 3, model // 3] if shared and model % 384 == 0 else [model]

    def send(x, k, j):
        return lax.ppermute(x, "patch", [(p, ((p // members) ^ k) * members + (p % members) ^ j) for p in range(patch)])

    def swap(x):
        return lax.ppermute(x, "groups", [(g, g ^ 1) for g in range(parts)])

    def spread(pieces, bit):
        while bit:
            for j in list(pieces):
                pieces[j ^ bit] = send(pieces[j], 0, bit)
            bit //= 2
        return [pieces[j] for j in range(members)]

    own_query, fresh, w_own, w_parts = prepare(
        groups, members, chunks, 2 if shared else 1, query, key_new, value_new, key_stale, value_stale, exponents.T, w_out
    )
    arrived = [send(fresh[k], k, 0) for k in range(1, groups)]
    both = jnp.concatenate([fresh[0]] + [x[:, share:] for x in arrived], axis=0)
    mine = [send(w, 0, far) for w in w_parts] if shared else []
    both = after(both, *mine)
    kvs = spread({0: both}, far)
    att = attend(groups, dim, [own_query] + arrived, kvs)

    if shared:
        pieces, places = [w_own], [(0, None, 0)]
        others = []
        for c, w in enumerate(mine):
            left = sum(chunks[:c])
            others += [(w, (far, 0, left)), (swap(w), (far, 1, left))]
        bit = 1
        while bit < far:
            pieces, places = (
                pieces + [send(after(x, both), 0, bit) for x in pieces],
                places + [(p[0] ^ bit, p[1], p[2]) for p in places],
            )
            others = others + [(send(after(x, *(kvs if p[1] else [both])), 0, bit), (p[0] ^ bit, p[1], p[2])) for x, p in others]
            bit *= 2
        pieces = pieces + [x for x, _ in others]
        places = places + [p for _, p in others]
    else:
        order = (lax.axis_index("patch") % members) ^ jnp.arange(members)
        pieces = [jnp.stack(spread({0: w_parts[0]}, far))[order].reshape(-1, model)]
        places = [(None, None, 0)]
    sums = project(groups, members, att, model, pieces, places)
    total = sums[0]
    for k in range(1, groups):
        total = total + send(sums[k], k, 0).astype(jnp.float32)
    return (total * gate[None, :]).astype(jnp.bfloat16)


def solution(mesh):
    return jax.shard_map(
        functools.partial(per_device, mesh.shape["groups"], mesh.shape["patch"]),
        mesh=mesh,
        in_specs=(
            P(("groups", "patch"), None),
            P(("groups", "patch"), None),
            P(("groups", "patch"), None),
            P("groups", None),
            P("groups", None),
            P("groups", None),
            P("patch", None),
            P("groups"),
        ),
        out_specs=P(("groups", "patch"), None),
        check_vma=False,
    )
```

```python
import functools
import math

import jax
import jax.numpy as jnp
from jax import lax
from jax.experimental import pallas as pl
from jax.experimental.pallas import tpu as pltpu
from jax.sharding import PartitionSpec as P

CLIP_LIMIT = 2.0
VMEM = pl.BlockSpec(memory_space=pltpu.VMEM)
ANY = pl.BlockSpec(memory_space=pl.ANY)
HBM = pl.BlockSpec(memory_space=pltpu.HBM)


def prepare_kernel(groups, members, chunks, *refs):
    sources, w_ref = refs[:6], refs[6]
    outs = refs[7:]
    qout, kvout, fulls = outs[0], outs[1], outs[1 : 1 + groups]
    wout, wparts = outs[1 + groups], outs[2 + groups : 2 + groups + chunks]
    query, key_new, value_new, kst, vst, est, packed, sems = outs[2 + groups + chunks :]
    rows, width = query.shape
    me = lax.axis_index("patch")
    first = pl.multiple_of((me // 2) * (2 * rows), 2 * rows)
    pair = pl.ds(first, 2 * rows)
    views = [sources[0], sources[1], sources[2], sources[3].at[pair], sources[4].at[pair], sources[5]]
    order = (5, 3, 1, 4, 2, 0)
    copies = {
        i: pltpu.make_async_copy(views[i], (query, key_new, value_new, kst, vst, est)[i], sems.at[i]) for i in order
    }
    for i in order:
        copies[i].start()
    moves = [pltpu.make_async_copy(w_ref, wout, sems.at[6])]
    for i in range(chunks):
        size, part = wparts[i].shape
        left = sum(w.shape[1] for w in wparts[:i])
        top = pl.multiple_of((lax.axis_index("groups") % 2) * size, size) if size < w_ref.shape[0] else 0
        view = w_ref.at[pl.ds(top, size), pl.ds(left, part)]
        moves.append(pltpu.make_async_copy(view, wparts[i], sems.at[7 + i]))
    for m in moves:
        m.start()
    heads = est.shape[0] // 2
    dim = width // heads
    share = width // groups
    odd = me % 2 == 1
    copies[5].wait()
    spot = lax.broadcasted_iota(jnp.int32, (rows, est.shape[1]), 1) == me * rows + lax.broadcasted_iota(
        jnp.int32, (rows, est.shape[1]), 0
    )
    powers = lax.dot_general(
        spot.astype(jnp.float32).astype(jnp.bfloat16),
        est[...].astype(jnp.float32).astype(jnp.bfloat16),
        (((1,), (1,)), ((), ())),
        preferred_element_type=jnp.float32,
    )
    scale = jnp.exp2(powers)
    inverse = jnp.exp2(-powers)
    for side, (fresh, stale) in enumerate(((key_new, kst), (value_new, vst))):
        copies[1 + side].wait()
        copies[3 + side].wait()
        for h in range(heads):
            cols = slice(h * dim, (h + 1) * dim)
            col = side * heads + h
            both = stale[:, cols].astype(jnp.float32)
            base = jnp.where(odd, both[rows:], both[:rows])
            resid = fresh[:, cols].astype(jnp.float32) - base
            codes = jnp.clip(resid * inverse[:, col : col + 1], -CLIP_LIMIT, CLIP_LIMIT)
            codes = codes.astype(jnp.bfloat16).astype(jnp.float32)
            at = side * share + (h * dim) % share
            packed[h * dim // share, :, at : at + dim] = (base + scale[:, col : col + 1] * codes).astype(jnp.bfloat16)
    copies[0].wait()
    for k in range(groups):
        target = (me // members) ^ k
        wanted = query[:, pl.ds(pl.multiple_of(target * share, share), share)]
        if k == 0:
            qout[...] = wanted
            kvout[...] = packed[target]
        else:
            fulls[k][:, :share] = wanted
            fulls[k][:, share:] = packed[target]
    for m in moves:
        m.wait()


def prepare(groups, members, chunks, split, query, key_new, value_new, key_stale, value_stale, powers, w_out):
    rows, width = query.shape
    share = width // groups
    depth, model = w_out.shape
    outs = (
        [((rows, share), jnp.bfloat16), ((rows, 2 * share), jnp.bfloat16)]
        + [((rows, 3 * share), jnp.bfloat16)] * (groups - 1)
        + [((depth, model), jnp.bfloat16)]
        + [((depth // split, c), jnp.bfloat16) for c in chunks]
    )
    sources = (query, key_new, value_new, key_stale, value_stale, powers, w_out)
    result = pl.pallas_call(
        functools.partial(prepare_kernel, groups, members, len(chunks)),
        out_shape=[jax.ShapeDtypeStruct(*o) for o in outs],
        in_specs=[HBM] * 7,
        out_specs=[VMEM] * len(outs),
        scratch_shapes=[pltpu.VMEM((rows, width), jnp.bfloat16)] * 3
        + [pltpu.VMEM((2 * rows, width), jnp.bfloat16)] * 2
        + [
            pltpu.VMEM(powers.shape, jnp.int32),
            pltpu.VMEM((groups, rows, 2 * share), jnp.bfloat16),
            pltpu.SemaphoreType.DMA((7 + len(chunks),)),
        ],
        compiler_params=pltpu.CompilerParams(vmem_limit_bytes=24 * 1024 * 1024),
        cost_estimate=pl.CostEstimate(
            flops=10 * rows * width, bytes_accessed=14 * rows * width + 4 * depth * model, transcendentals=0
        ),
    )(*(pltpu.with_memory_space_constraint(x, pltpu.HBM) for x in sources))
    return result[0], result[1 : 1 + groups], result[1 + groups], result[2 + groups :]


def attend_kernel(groups, dim, *refs):
    queries = refs[:groups]
    kvs = refs[groups:-2]
    att, kv = refs[-2:]
    share = att.shape[1]
    block = kvs[0].shape[0]
    for j in range(len(kvs)):
        kv[j * block : (j + 1) * block] = kvs[j][...]
    query = jnp.concatenate([q[:, :share].astype(jnp.float32) for q in queries], axis=0).astype(jnp.bfloat16)
    inverse = 1.0 / dim**0.5
    for h in range(share // dim):
        cols = slice(h * dim, (h + 1) * dim)
        scores = (
            lax.dot_general(query[:, cols], kv[:, cols], (((1,), (1,)), ((), ())), preferred_element_type=jnp.float32)
            * inverse
        )
        peak = jnp.max(scores, axis=1, keepdims=True)
        expo = jnp.exp(scores - peak)
        total = jnp.sum(expo, axis=1, keepdims=True)
        numer = jnp.dot(
            expo.astype(jnp.bfloat16),
            kv[:, share + h * dim : share + (h + 1) * dim],
            preferred_element_type=jnp.float32,
        )
        att[:, cols] = (numer / total).astype(jnp.bfloat16)


def attend(groups, dim, queries, kvs):
    rows, share = queries[-1].shape
    block = kvs[0].shape[0]
    pieces = len(kvs)
    return pl.pallas_call(
        functools.partial(attend_kernel, groups, dim),
        out_shape=jax.ShapeDtypeStruct((groups * rows, share), jnp.bfloat16),
        in_specs=[VMEM] * (groups + pieces),
        out_specs=VMEM,
        scratch_shapes=[pltpu.VMEM((pieces * block, 2 * share), jnp.bfloat16)],
        compiler_params=pltpu.CompilerParams(vmem_limit_bytes=24 * 1024 * 1024),
        cost_estimate=pl.CostEstimate(
            flops=4 * groups * rows * pieces * block * share,
            bytes_accessed=4 * pieces * block * share,
            transcendentals=groups * rows * pieces * block * share // dim,
        ),
    )(*queries, *kvs)


def project_kernel(groups, members, places, att, *refs):
    ws = refs[: len(places)]
    outs = refs[len(places) : len(places) + groups]
    wide, sems = refs[len(places) + groups :]
    q = lax.axis_index("patch") % members
    side = lax.axis_index("groups") % 2
    copies = []
    for i, (piece, (j, flip, col)) in enumerate(zip(ws, places)):
        size, part = piece.shape
        row = 0
        if j is not None:
            row = (q ^ j) * (size if flip is None else 2 * size)
            if flip is not None:
                row = row + (side ^ flip) * size
            row = pl.multiple_of(row, size)
        view = wide.at[pl.ds(row, size), pl.ds(col, part)]
        copies.append(pltpu.make_async_copy(piece, view, sems.at[i]))
    for c in copies:
        c.start()
    for c in copies:
        c.wait()
    rows, width = outs[0].shape
    tile = 512 if width % 512 == 0 else width
    for t in range(width // tile):
        cols = slice(t * tile, (t + 1) * tile)
        part = jnp.dot(att[...], wide[:, cols], preferred_element_type=jnp.float32)
        for i in range(groups):
            outs[i][:, cols] = part[i * rows : (i + 1) * rows].astype(outs[i].dtype)


def project(groups, members, att, model, pieces, places):
    rows = att.shape[0] // groups
    share = att.shape[1]
    return pl.pallas_call(
        functools.partial(project_kernel, groups, members, places),
        out_shape=[jax.ShapeDtypeStruct((rows, model), jnp.bfloat16)] * (groups - 1)
        + [jax.ShapeDtypeStruct((rows, model), jnp.float32)],
        in_specs=[VMEM] + [ANY] * len(pieces),
        out_specs=[VMEM] * groups,
        scratch_shapes=[pltpu.VMEM((share, model), jnp.bfloat16), pltpu.SemaphoreType.DMA((len(pieces),))],
        compiler_params=pltpu.CompilerParams(vmem_limit_bytes=24 * 1024 * 1024),
        cost_estimate=pl.CostEstimate(
            flops=2 * groups * rows * share * model, bytes_accessed=2 * share * model, transcendentals=0
        ),
    )(att, *pieces)


def after(x, *others):
    if not others:
        return x
    return lax.optimization_barrier((x, *others))[0]


def per_device(parts, patch, query, key_new, value_new, key_stale, value_stale, exponents, w_out, gate):
    heads = exponents.shape[1] // 2
    rows, width = query.shape
    dim = width // heads
    groups = math.gcd(patch, heads)
    members = patch // groups
    share = width // groups
    depth, model = w_out.shape
    far = members // 2
    shared = parts % 2 == 0 and depth % 32 == 0
    chunks = [2 * model // 3, model // 3] if shared and model % 384 == 0 else [model]

    def send(x, k, j):
        return lax.ppermute(x, "patch", [(p, ((p // members) ^ k) * members + (p % members) ^ j) for p in range(patch)])

    def swap(x):
        return lax.ppermute(x, "groups", [(g, g ^ 1) for g in range(parts)])

    def spread(pieces, bit):
        while bit:
            for j in list(pieces):
                pieces[j ^ bit] = send(pieces[j], 0, bit)
            bit //= 2
        return [pieces[j] for j in range(members)]

    own_query, fresh, w_own, w_parts = prepare(
        groups, members, chunks, 2 if shared else 1, query, key_new, value_new, key_stale, value_stale, exponents.T, w_out
    )
    order = range(groups - 1, 0, -1)
    arrived = [send(fresh[k], k, 0) for k in order]
    both = jnp.concatenate([x[:, share:] for x in arrived] + [fresh[0]], axis=0)
    mine = [send(w, 0, far) for w in w_parts] if shared else []
    both = after(both, *mine)
    swapped = [swap(w) for w in mine]
    pieces = {0: both}
    bit = far
    while bit:
        for j in list(pieces):
            relay = after(pieces[j], *swapped[:1]) if j else both
            pieces[j ^ bit] = send(relay, 0, bit)
        bit //= 2
    kvs = [pieces[j] for j in range(members)]
    kvs[-1] = after(kvs[-1], *swapped)
    att = attend(groups, dim, arrived + [own_query], kvs)

    if shared:
        pieces, places = [w_own], [(0, None, 0)]
        others = []
        for c, w in enumerate(mine):
            left = sum(chunks[:c])
            others += [(w, (far, 0, left)), (swapped[c], (far, 1, left))]
        bit = 1
        while bit < far:
            pieces, places = (
                pieces + [send(after(x, both), 0, bit) for x in pieces],
                places + [(p[0] ^ bit, p[1], p[2]) for p in places],
            )
            others = others + [(send(after(x, both), 0, bit), (p[0] ^ bit, p[1], p[2])) for x, p in others]
            bit *= 2
        pieces = pieces + [x for x, _ in others]
        places = places + [p for _, p in others]
    else:
        spots = (lax.axis_index("patch") % members) ^ jnp.arange(members)
        pieces = [jnp.stack(spread({0: w_parts[0]}, far))[spots].reshape(-1, model)]
        places = [(None, None, 0)]
    sums = project(groups, members, att, model, pieces, places)
    total = sums[-1]
    for k, part in zip(order, sums):
        total = total + send(part, k, 0).astype(jnp.float32)
    return (total * gate[None, :]).astype(jnp.bfloat16)


def solution(mesh):
    return jax.shard_map(
        functools.partial(per_device, mesh.shape["groups"], mesh.shape["patch"]),
        mesh=mesh,
        in_specs=(
            P(("groups", "patch"), None),
            P(("groups", "patch"), None),
            P(("groups", "patch"), None),
            P("groups", None),
            P("groups", None),
            P("groups", None),
            P("patch", None),
            P("groups"),
        ),
        out_specs=P(("groups", "patch"), None),
        check_vma=False,
    )
```

```python
import functools
import math

import jax
import jax.numpy as jnp
from jax import lax
from jax.experimental import pallas as pl
from jax.experimental.pallas import tpu as pltpu
from jax.sharding import PartitionSpec as P

CLIP_LIMIT = 2.0
VMEM = pl.BlockSpec(memory_space=pltpu.VMEM)
ANY = pl.BlockSpec(memory_space=pl.ANY)
HBM = pl.BlockSpec(memory_space=pltpu.HBM)


def prepare_kernel(groups, members, chunks, *refs):
    sources, w_ref = refs[:6], refs[6]
    outs = refs[7:]
    qout, fulls, kvouts, wout = outs[0], outs[:groups], outs[groups : 2 * groups], outs[2 * groups]
    wparts = outs[2 * groups + 1 : 2 * groups + 1 + chunks]
    query, key_new, value_new, kst, vst, est, packed, sems = outs[2 * groups + 1 + chunks :]
    rows, width = query.shape
    me = lax.axis_index("patch")
    first = pl.multiple_of((me // 2) * (2 * rows), 2 * rows)
    pair = pl.ds(first, 2 * rows)
    views = [sources[0], sources[1], sources[2], sources[3].at[pair], sources[4].at[pair], sources[5]]
    order = (5, 3, 1, 4, 2, 0)
    copies = {
        i: pltpu.make_async_copy(views[i], (query, key_new, value_new, kst, vst, est)[i], sems.at[i]) for i in order
    }
    for i in order:
        copies[i].start()
    moves = [pltpu.make_async_copy(w_ref, wout, sems.at[6])]
    for i in range(chunks):
        size, part = wparts[i].shape
        left = sum(w.shape[1] for w in wparts[:i])
        top = pl.multiple_of((lax.axis_index("groups") % 2) * size, size) if size < w_ref.shape[0] else 0
        view = w_ref.at[pl.ds(top, size), pl.ds(left, part)]
        moves.append(pltpu.make_async_copy(view, wparts[i], sems.at[7 + i]))
    for m in moves:
        m.start()
    heads = est.shape[0] // 2
    dim = width // heads
    share = width // groups
    odd = me % 2 == 1
    copies[5].wait()
    spot = lax.broadcasted_iota(jnp.int32, (rows, est.shape[1]), 1) == me * rows + lax.broadcasted_iota(
        jnp.int32, (rows, est.shape[1]), 0
    )
    powers = lax.dot_general(
        spot.astype(jnp.float32).astype(jnp.bfloat16),
        est[...].astype(jnp.float32).astype(jnp.bfloat16),
        (((1,), (1,)), ((), ())),
        preferred_element_type=jnp.float32,
    )
    scale = jnp.exp2(powers)
    inverse = jnp.exp2(-powers)
    for side, (fresh, stale) in enumerate(((key_new, kst), (value_new, vst))):
        copies[1 + side].wait()
        copies[3 + side].wait()
        for h in range(heads):
            cols = slice(h * dim, (h + 1) * dim)
            col = side * heads + h
            both = stale[:, cols].astype(jnp.float32)
            base = jnp.where(odd, both[rows:], both[:rows])
            resid = fresh[:, cols].astype(jnp.float32) - base
            codes = jnp.clip(resid * inverse[:, col : col + 1], -CLIP_LIMIT, CLIP_LIMIT)
            codes = codes.astype(jnp.bfloat16).astype(jnp.float32)
            at = side * share + (h * dim) % share
            packed[h * dim // share, :, at : at + dim] = (base + scale[:, col : col + 1] * codes).astype(jnp.bfloat16)
    copies[0].wait()
    for k in range(groups):
        target = (me // members) ^ k
        wanted = query[:, pl.ds(pl.multiple_of(target * share, share), share)]
        kvouts[k][...] = packed[target]
        if k == 0:
            qout[...] = wanted
        else:
            fulls[k][:, :share] = wanted
            fulls[k][:, share:] = packed[target]
    for m in moves:
        m.wait()


def prepare(groups, members, chunks, split, query, key_new, value_new, key_stale, value_stale, powers, w_out):
    rows, width = query.shape
    share = width // groups
    depth, model = w_out.shape
    outs = (
        [((rows, share), jnp.bfloat16)]
        + [((rows, 3 * share), jnp.bfloat16)] * (groups - 1)
        + [((rows, 2 * share), jnp.bfloat16)] * groups
        + [((depth, model), jnp.bfloat16)]
        + [((depth // (split if i == 0 else 1), c), jnp.bfloat16) for i, c in enumerate(chunks)]
    )
    sources = (query, key_new, value_new, key_stale, value_stale, powers, w_out)
    result = pl.pallas_call(
        functools.partial(prepare_kernel, groups, members, len(chunks)),
        out_shape=[jax.ShapeDtypeStruct(*o) for o in outs],
        in_specs=[HBM] * 7,
        out_specs=[VMEM] * len(outs),
        scratch_shapes=[pltpu.VMEM((rows, width), jnp.bfloat16)] * 3
        + [pltpu.VMEM((2 * rows, width), jnp.bfloat16)] * 2
        + [
            pltpu.VMEM(powers.shape, jnp.int32),
            pltpu.VMEM((groups, rows, 2 * share), jnp.bfloat16),
            pltpu.SemaphoreType.DMA((7 + len(chunks),)),
        ],
        compiler_params=pltpu.CompilerParams(vmem_limit_bytes=24 * 1024 * 1024),
        cost_estimate=pl.CostEstimate(
            flops=10 * rows * width, bytes_accessed=14 * rows * width + 4 * depth * model, transcendentals=0
        ),
    )(*(pltpu.with_memory_space_constraint(x, pltpu.HBM) for x in sources))
    return result[:groups], result[groups : 2 * groups], result[2 * groups], result[2 * groups + 1 :]


def attend_kernel(groups, dim, *refs):
    queries = refs[:groups]
    kvs = refs[groups:-2]
    att, kv = refs[-2:]
    share = att.shape[1]
    block = kvs[0].shape[0]
    for j in range(len(kvs)):
        kv[j * block : (j + 1) * block] = kvs[j][...]
    query = jnp.concatenate([q[:, :share].astype(jnp.float32) for q in queries], axis=0).astype(jnp.bfloat16)
    inverse = 1.0 / dim**0.5
    for h in range(share // dim):
        cols = slice(h * dim, (h + 1) * dim)
        scores = (
            lax.dot_general(query[:, cols], kv[:, cols], (((1,), (1,)), ((), ())), preferred_element_type=jnp.float32)
            * inverse
        )
        peak = jnp.max(scores, axis=1, keepdims=True)
        expo = jnp.exp(scores - peak)
        total = jnp.sum(expo, axis=1, keepdims=True)
        numer = jnp.dot(
            expo.astype(jnp.bfloat16),
            kv[:, share + h * dim : share + (h + 1) * dim],
            preferred_element_type=jnp.float32,
        )
        att[:, cols] = (numer / total).astype(jnp.bfloat16)


def attend(groups, dim, queries, kvs):
    rows, share = queries[-1].shape
    block = kvs[0].shape[0]
    pieces = len(kvs)
    return pl.pallas_call(
        functools.partial(attend_kernel, groups, dim),
        out_shape=jax.ShapeDtypeStruct((groups * rows, share), jnp.bfloat16),
        in_specs=[VMEM] * (groups + pieces),
        out_specs=VMEM,
        scratch_shapes=[pltpu.VMEM((pieces * block, 2 * share), jnp.bfloat16)],
        compiler_params=pltpu.CompilerParams(vmem_limit_bytes=24 * 1024 * 1024),
        cost_estimate=pl.CostEstimate(
            flops=4 * groups * rows * pieces * block * share,
            bytes_accessed=4 * pieces * block * share,
            transcendentals=groups * rows * pieces * block * share // dim,
        ),
    )(*queries, *kvs)


def project_kernel(groups, members, places, att, *refs):
    ws = refs[: len(places)]
    outs = refs[len(places) : len(places) + groups]
    wide, sems = refs[len(places) + groups :]
    q = lax.axis_index("patch") % members
    side = lax.axis_index("groups") % 2
    copies = []
    for i, (piece, (j, flip, col)) in enumerate(zip(ws, places)):
        size, part = piece.shape
        row = 0
        if j is not None:
            row = (q ^ j) * (size if flip is None else 2 * size)
            if flip is not None:
                row = row + (side ^ flip) * size
            row = pl.multiple_of(row, size)
        view = wide.at[pl.ds(row, size), pl.ds(col, part)]
        copies.append(pltpu.make_async_copy(piece, view, sems.at[i]))
    for c in copies:
        c.start()
    for c in copies:
        c.wait()
    rows, width = outs[0].shape
    tile = 512 if width % 512 == 0 else width
    for t in range(width // tile):
        cols = slice(t * tile, (t + 1) * tile)
        part = jnp.dot(att[...], wide[:, cols], preferred_element_type=jnp.float32)
        for i in range(groups):
            outs[i][:, cols] = part[i * rows : (i + 1) * rows].astype(outs[i].dtype)


def project(groups, members, att, model, pieces, places):
    rows = att.shape[0] // groups
    share = att.shape[1]
    return pl.pallas_call(
        functools.partial(project_kernel, groups, members, places),
        out_shape=[jax.ShapeDtypeStruct((rows, model), jnp.bfloat16)] * (groups - 1)
        + [jax.ShapeDtypeStruct((rows, model), jnp.float32)],
        in_specs=[VMEM] + [ANY] * len(pieces),
        out_specs=[VMEM] * groups,
        scratch_shapes=[pltpu.VMEM((share, model), jnp.bfloat16), pltpu.SemaphoreType.DMA((len(pieces),))],
        compiler_params=pltpu.CompilerParams(vmem_limit_bytes=24 * 1024 * 1024),
        cost_estimate=pl.CostEstimate(
            flops=2 * groups * rows * share * model, bytes_accessed=2 * share * model, transcendentals=0
        ),
    )(att, *pieces)


def after(x, *others):
    if not others:
        return x
    return lax.optimization_barrier((x, *others))[0]


def per_device(parts, patch, query, key_new, value_new, key_stale, value_stale, exponents, w_out, gate):
    heads = exponents.shape[1] // 2
    rows, width = query.shape
    dim = width // heads
    groups = math.gcd(patch, heads)
    members = patch // groups
    share = width // groups
    depth, model = w_out.shape
    far = members // 2
    shared = parts % 2 == 0 and depth % 32 == 0
    chunks = [2 * model // 3, model // 3] if shared and model % 384 == 0 else [model]

    def send(x, k, j):
        return lax.ppermute(x, "patch", [(p, ((p // members) ^ k) * members + (p % members) ^ j) for p in range(patch)])

    def swap(x):
        return lax.ppermute(x, "groups", [(g, g ^ 1) for g in range(parts)])

    def spread(pieces, bit):
        while bit:
            for j in list(pieces):
                pieces[j ^ bit] = send(pieces[j], 0, bit)
            bit //= 2
        return [pieces[j] for j in range(members)]

    full, fresh, w_own, w_parts = prepare(
        groups, members, chunks, 2 if shared else 1, query, key_new, value_new, key_stale, value_stale, exponents.T, w_out
    )
    order = range(groups - 1, 0, -1)
    arrived = [send(full[k], k, 0) for k in order]
    mine = [send(w, 0, far) for w in w_parts] if shared else []
    arrived[0] = after(arrived[0], *mine[:1])
    swapped = swap(mine[0]) if shared else fresh[0]
    fresh = [after(x, arrived[0]) for x in fresh]
    side = [send(fresh[k], k, j) for j in range(2, members, 2) for k in [*order, 0]]
    side[0] = after(side[0], swapped)
    both = jnp.concatenate([x[:, share:] for x in arrived] + [fresh[0]] + side, axis=0)
    both = after(both, *mine)
    theirs = after(send(both, 0, 1), swapped)
    att = attend(groups, dim, arrived + [full[0]], [both, theirs])

    if shared:
        pieces, places = [w_own], [(0, None, 0)]
        others = []
        others += [(mine[0], (far, 0, 0)), (swapped, (far, 1, 0)), (mine[1], (far, None, chunks[0]))]
        bit = 1
        while bit < far:
            pieces, places = (
                pieces + [send(after(x, both), 0, bit) for x in pieces],
                places + [(p[0] ^ bit, p[1], p[2]) for p in places],
            )
            others = others + [(send(after(x, both), 0, bit), (p[0] ^ bit, p[1], p[2])) for x, p in others]
            bit *= 2
        pieces = pieces + [x for x, _ in others]
        places = places + [p for _, p in others]
    else:
        spots = (lax.axis_index("patch") % members) ^ jnp.arange(members)
        pieces = [jnp.stack(spread({0: w_parts[0]}, far))[spots].reshape(-1, model)]
        places = [(None, None, 0)]
    sums = project(groups, members, att, model, pieces, places)
    total = sums[-1]
    for k, part in zip(order, sums):
        total = total + send(part, k, 0).astype(jnp.float32)
    return (total * gate[None, :]).astype(jnp.bfloat16)


def solution(mesh):
    return jax.shard_map(
        functools.partial(per_device, mesh.shape["groups"], mesh.shape["patch"]),
        mesh=mesh,
        in_specs=(
            P(("groups", "patch"), None),
            P(("groups", "patch"), None),
            P(("groups", "patch"), None),
            P("groups", None),
            P("groups", None),
            P("groups", None),
            P("patch", None),
            P("groups"),
        ),
        out_specs=P(("groups", "patch"), None),
        check_vma=False,
    )
```

```python
import functools
import math

import jax
import jax.numpy as jnp
from jax import lax
from jax.experimental import pallas as pl
from jax.experimental.pallas import tpu as pltpu
from jax.sharding import PartitionSpec as P

CLIP_LIMIT = 2.0
VMEM = pl.BlockSpec(memory_space=pltpu.VMEM)
ANY = pl.BlockSpec(memory_space=pl.ANY)
HBM = pl.BlockSpec(memory_space=pltpu.HBM)


def prepare_kernel(groups, members, chunks, *refs):
    sources, w_ref = refs[:6], refs[6]
    outs = refs[7:]
    qout, kvout, fulls = outs[0], outs[1], outs[1 : 1 + groups]
    wout, wparts = outs[1 + groups], outs[2 + groups : 2 + groups + chunks]
    query, key_new, value_new, kst, vst, est, packed, sems = outs[2 + groups + chunks :]
    rows, width = query.shape
    me = lax.axis_index("patch")
    first = pl.multiple_of((me // 2) * (2 * rows), 2 * rows)
    pair = pl.ds(first, 2 * rows)
    views = [sources[0], sources[1], sources[2], sources[3].at[pair], sources[4].at[pair], sources[5]]
    order = (5, 3, 1, 4, 2, 0)
    copies = {
        i: pltpu.make_async_copy(views[i], (query, key_new, value_new, kst, vst, est)[i], sems.at[i]) for i in order
    }
    for i in order:
        copies[i].start()
    moves = [pltpu.make_async_copy(w_ref, wout, sems.at[6])]
    for i in range(chunks):
        size, part = wparts[i].shape
        left = sum(w.shape[1] for w in wparts[:i])
        top = pl.multiple_of((lax.axis_index("groups") % 2) * size, size) if size < w_ref.shape[0] else 0
        view = w_ref.at[pl.ds(top, size), pl.ds(left, part)]
        moves.append(pltpu.make_async_copy(view, wparts[i], sems.at[7 + i]))
    for m in moves:
        m.start()
    heads = est.shape[0] // 2
    dim = width // heads
    share = width // groups
    odd = me % 2 == 1
    copies[5].wait()
    spot = lax.broadcasted_iota(jnp.int32, (rows, est.shape[1]), 1) == me * rows + lax.broadcasted_iota(
        jnp.int32, (rows, est.shape[1]), 0
    )
    powers = lax.dot_general(
        spot.astype(jnp.float32).astype(jnp.bfloat16),
        est[...].astype(jnp.float32).astype(jnp.bfloat16),
        (((1,), (1,)), ((), ())),
        preferred_element_type=jnp.float32,
    )
    scale = jnp.exp2(powers)
    inverse = jnp.exp2(-powers)
    for side, (fresh, stale) in enumerate(((key_new, kst), (value_new, vst))):
        copies[1 + side].wait()
        copies[3 + side].wait()
        for h in range(heads):
            cols = slice(h * dim, (h + 1) * dim)
            col = side * heads + h
            both = stale[:, cols].astype(jnp.float32)
            base = jnp.where(odd, both[rows:], both[:rows])
            resid = fresh[:, cols].astype(jnp.float32) - base
            codes = jnp.clip(resid * inverse[:, col : col + 1], -CLIP_LIMIT, CLIP_LIMIT)
            codes = codes.astype(jnp.bfloat16).astype(jnp.float32)
            at = side * share + (h * dim) % share
            packed[h * dim // share, :, at : at + dim] = (base + scale[:, col : col + 1] * codes).astype(jnp.bfloat16)
    copies[0].wait()
    for k in range(groups):
        target = (me // members) ^ k
        wanted = query[:, pl.ds(pl.multiple_of(target * share, share), share)]
        if k == 0:
            qout[...] = wanted
            kvout[...] = packed[target]
        else:
            fulls[k][:, :share] = wanted
            fulls[k][:, share:] = packed[target]
    for m in moves:
        m.wait()


def prepare(groups, members, chunks, split, query, key_new, value_new, key_stale, value_stale, powers, w_out):
    rows, width = query.shape
    share = width // groups
    depth, model = w_out.shape
    outs = (
        [((rows, share), jnp.bfloat16), ((rows, 2 * share), jnp.bfloat16)]
        + [((rows, 3 * share), jnp.bfloat16)] * (groups - 1)
        + [((depth, model), jnp.bfloat16)]
        + [((depth // split, c), jnp.bfloat16) for c in chunks]
    )
    sources = (query, key_new, value_new, key_stale, value_stale, powers, w_out)
    result = pl.pallas_call(
        functools.partial(prepare_kernel, groups, members, len(chunks)),
        out_shape=[jax.ShapeDtypeStruct(*o) for o in outs],
        in_specs=[HBM] * 7,
        out_specs=[VMEM] * len(outs),
        scratch_shapes=[pltpu.VMEM((rows, width), jnp.bfloat16)] * 3
        + [pltpu.VMEM((2 * rows, width), jnp.bfloat16)] * 2
        + [
            pltpu.VMEM(powers.shape, jnp.int32),
            pltpu.VMEM((groups, rows, 2 * share), jnp.bfloat16),
            pltpu.SemaphoreType.DMA((7 + len(chunks),)),
        ],
        compiler_params=pltpu.CompilerParams(vmem_limit_bytes=24 * 1024 * 1024),
        cost_estimate=pl.CostEstimate(
            flops=10 * rows * width, bytes_accessed=14 * rows * width + 4 * depth * model, transcendentals=0
        ),
    )(*(pltpu.with_memory_space_constraint(x, pltpu.HBM) for x in sources))
    return result[0], result[1 : 1 + groups], result[1 + groups], result[2 + groups :]


def attend_kernel(groups, dim, *refs):
    queries = refs[:groups]
    kvs = refs[groups:-2]
    att, kv = refs[-2:]
    share = att.shape[1]
    block = kvs[0].shape[0]
    for j in range(len(kvs)):
        kv[j * block : (j + 1) * block] = kvs[j][...]
    query = jnp.concatenate([q[:, :share].astype(jnp.float32) for q in queries], axis=0).astype(jnp.bfloat16)
    inverse = 1.0 / dim**0.5
    for h in range(share // dim):
        cols = slice(h * dim, (h + 1) * dim)
        scores = (
            lax.dot_general(query[:, cols], kv[:, cols], (((1,), (1,)), ((), ())), preferred_element_type=jnp.float32)
            * inverse
        )
        peak = jnp.max(scores, axis=1, keepdims=True)
        expo = jnp.exp(scores - peak)
        total = jnp.sum(expo, axis=1, keepdims=True)
        numer = jnp.dot(
            expo.astype(jnp.bfloat16),
            kv[:, share + h * dim : share + (h + 1) * dim],
            preferred_element_type=jnp.float32,
        )
        att[:, cols] = (numer / total).astype(jnp.bfloat16)


def attend(groups, dim, queries, kvs):
    rows, share = queries[-1].shape
    block = kvs[0].shape[0]
    pieces = len(kvs)
    return pl.pallas_call(
        functools.partial(attend_kernel, groups, dim),
        out_shape=jax.ShapeDtypeStruct((groups * rows, share), jnp.bfloat16),
        in_specs=[VMEM] * (groups + pieces),
        out_specs=VMEM,
        scratch_shapes=[pltpu.VMEM((pieces * block, 2 * share), jnp.bfloat16)],
        compiler_params=pltpu.CompilerParams(vmem_limit_bytes=24 * 1024 * 1024),
        cost_estimate=pl.CostEstimate(
            flops=4 * groups * rows * pieces * block * share,
            bytes_accessed=4 * pieces * block * share,
            transcendentals=groups * rows * pieces * block * share // dim,
        ),
    )(*queries, *kvs)


def project_kernel(groups, members, places, att, *refs):
    ws = refs[: len(places)]
    outs = refs[len(places) : len(places) + groups]
    wide, sems = refs[len(places) + groups :]
    q = lax.axis_index("patch") % members
    side = lax.axis_index("groups") % 2
    copies = []
    for i, (piece, (j, flip, col)) in enumerate(zip(ws, places)):
        size, part = piece.shape
        row = 0
        if j is not None:
            row = (q ^ j) * (size if flip is None else 2 * size)
            if flip is not None:
                row = row + (side ^ flip) * size
            row = pl.multiple_of(row, size)
        view = wide.at[pl.ds(row, size), pl.ds(col, part)]
        copies.append(pltpu.make_async_copy(piece, view, sems.at[i]))
    for c in copies:
        c.start()
    for c in copies:
        c.wait()
    rows, width = outs[0].shape
    tile = 512 if width % 512 == 0 else width
    for t in range(width // tile):
        cols = slice(t * tile, (t + 1) * tile)
        part = jnp.dot(att[...], wide[:, cols], preferred_element_type=jnp.float32)
        for i in range(groups):
            outs[i][:, cols] = part[i * rows : (i + 1) * rows].astype(outs[i].dtype)


def project(groups, members, att, model, pieces, places):
    rows = att.shape[0] // groups
    share = att.shape[1]
    return pl.pallas_call(
        functools.partial(project_kernel, groups, members, places),
        out_shape=[jax.ShapeDtypeStruct((rows, model), jnp.bfloat16)] * (groups - 1)
        + [jax.ShapeDtypeStruct((rows, model), jnp.float32)],
        in_specs=[VMEM] + [ANY] * len(pieces),
        out_specs=[VMEM] * groups,
        scratch_shapes=[pltpu.VMEM((share, model), jnp.bfloat16), pltpu.SemaphoreType.DMA((len(pieces),))],
        compiler_params=pltpu.CompilerParams(vmem_limit_bytes=24 * 1024 * 1024),
        cost_estimate=pl.CostEstimate(
            flops=2 * groups * rows * share * model, bytes_accessed=2 * share * model, transcendentals=0
        ),
    )(att, *pieces)


def after(x, *others):
    if not others:
        return x
    return lax.optimization_barrier((x, *others))[0]


def per_device(parts, patch, query, key_new, value_new, key_stale, value_stale, exponents, w_out, gate):
    heads = exponents.shape[1] // 2
    rows, width = query.shape
    dim = width // heads
    groups = math.gcd(patch, heads)
    members = patch // groups
    share = width // groups
    depth, model = w_out.shape
    far = members // 2
    shared = parts % 2 == 0 and depth % 32 == 0
    chunks = [model]

    def send(x, k, j):
        return lax.ppermute(x, "patch", [(p, ((p // members) ^ k) * members + (p % members) ^ j) for p in range(patch)])

    def swap(x):
        return lax.ppermute(x, "groups", [(g, g ^ 1) for g in range(parts)])

    def spread(pieces, bit):
        while bit:
            for j in list(pieces):
                pieces[j ^ bit] = send(pieces[j], 0, bit)
            bit //= 2
        return [pieces[j] for j in range(members)]

    own_query, fresh, w_own, w_parts = prepare(
        groups, members, chunks, 2 if shared else 1, query, key_new, value_new, key_stale, value_stale, exponents.T, w_out
    )
    order = range(groups - 1, 0, -1)
    arrived = [send(fresh[k], k, 0) for k in order]
    both = jnp.concatenate([x[:, share:] for x in arrived] + [fresh[0]], axis=0)
    mine = [send(w, 0, far) for w in w_parts] if shared else []
    both = after(both, *mine)
    swapped = [swap(w) for w in mine]
    pieces = {0: both}
    bit = far
    while bit:
        for j in list(pieces):
            pieces[j ^ bit] = send(pieces[j], 0, bit)
        bit //= 2
    kvs = [pieces[j] for j in range(members)]
    att = attend(groups, dim, arrived + [own_query], kvs)

    if shared:
        pieces, places = [w_own], [(0, None, 0)]
        others = []
        for c, w in enumerate(mine):
            left = sum(chunks[:c])
            others += [(w, (far, 0, left)), (swapped[c], (far, 1, left))]
        bit = 1
        while bit < far:
            pieces, places = (
                pieces + [send(after(x, both), 0, bit) for x in pieces],
                places + [(p[0] ^ bit, p[1], p[2]) for p in places],
            )
            others = others + [(send(after(x, *(kvs if p[1] else [both])), 0, bit), (p[0] ^ bit, p[1], p[2])) for x, p in others]
            bit *= 2
        pieces = pieces + [x for x, _ in others]
        places = places + [p for _, p in others]
    else:
        spots = (lax.axis_index("patch") % members) ^ jnp.arange(members)
        pieces = [jnp.stack(spread({0: w_parts[0]}, far))[spots].reshape(-1, model)]
        places = [(None, None, 0)]
    sums = project(groups, members, att, model, pieces, places)
    total = sums[-1]
    for k, part in zip(order, sums):
        total = total + send(part, k, 0).astype(jnp.float32)
    return (total * gate[None, :]).astype(jnp.bfloat16)


def solution(mesh):
    return jax.shard_map(
        functools.partial(per_device, mesh.shape["groups"], mesh.shape["patch"]),
        mesh=mesh,
        in_specs=(
            P(("groups", "patch"), None),
            P(("groups", "patch"), None),
            P(("groups", "patch"), None),
            P("groups", None),
            P("groups", None),
            P("groups", None),
            P("patch", None),
            P("groups"),
        ),
        out_specs=P(("groups", "patch"), None),
        check_vma=False,
    )
```

```python
import functools
import math

import jax
import jax.numpy as jnp
from jax import lax
from jax.experimental import pallas as pl
from jax.experimental.pallas import tpu as pltpu
from jax.sharding import PartitionSpec as P

CLIP_LIMIT = 2.0
VMEM = pl.BlockSpec(memory_space=pltpu.VMEM)
ANY = pl.BlockSpec(memory_space=pl.ANY)
HBM = pl.BlockSpec(memory_space=pltpu.HBM)


def prepare_kernel(groups, members, *refs):
    sources, w_ref = refs[:6], refs[6]
    outs = refs[7:]
    qout, kvout, fulls = outs[0], outs[1], outs[1 : 1 + groups]
    wout, wpart = outs[1 + groups], outs[2 + groups]
    query, key_new, value_new, kst, vst, est, packed, sems = outs[3 + groups :]
    rows, width = query.shape
    me = lax.axis_index("patch")
    first = pl.multiple_of((me // 2) * (2 * rows), 2 * rows)
    pair = pl.ds(first, 2 * rows)
    views = [sources[0], sources[1], sources[2], sources[3].at[pair], sources[4].at[pair], sources[5]]
    order = (5, 3, 1, 4, 2, 0)
    copies = {
        i: pltpu.make_async_copy(views[i], (query, key_new, value_new, kst, vst, est)[i], sems.at[i]) for i in order
    }
    for i in order:
        copies[i].start()
    size = wpart.shape[0]
    top = pl.multiple_of((lax.axis_index("groups") % 2) * size, size) if size < w_ref.shape[0] else 0
    moves = [
        pltpu.make_async_copy(w_ref.at[pl.ds(top, size)], wpart, sems.at[7]),
        pltpu.make_async_copy(w_ref, wout, sems.at[6]),
    ]
    for m in moves:
        m.start()
    heads = est.shape[0] // 2
    dim = width // heads
    share = width // groups
    odd = me % 2 == 1
    copies[5].wait()
    spot = lax.broadcasted_iota(jnp.int32, (rows, est.shape[1]), 1) == me * rows + lax.broadcasted_iota(
        jnp.int32, (rows, est.shape[1]), 0
    )
    powers = lax.dot_general(
        spot.astype(jnp.float32).astype(jnp.bfloat16),
        est[...].astype(jnp.float32).astype(jnp.bfloat16),
        (((1,), (1,)), ((), ())),
        preferred_element_type=jnp.float32,
    )
    scale = jnp.exp2(powers)
    inverse = jnp.exp2(-powers)
    for side, (fresh, stale) in enumerate(((key_new, kst), (value_new, vst))):
        copies[1 + side].wait()
        copies[3 + side].wait()
        for h in range(heads):
            cols = slice(h * dim, (h + 1) * dim)
            col = side * heads + h
            both = stale[:, cols].astype(jnp.float32)
            base = jnp.where(odd, both[rows:], both[:rows])
            resid = fresh[:, cols].astype(jnp.float32) - base
            codes = jnp.clip(resid * inverse[:, col : col + 1], -CLIP_LIMIT, CLIP_LIMIT)
            codes = codes.astype(jnp.bfloat16).astype(jnp.float32)
            at = side * share + (h * dim) % share
            packed[h * dim // share, :, at : at + dim] = (base + scale[:, col : col + 1] * codes).astype(jnp.bfloat16)
    copies[0].wait()
    for k in range(groups):
        target = (me // members) ^ k
        wanted = query[:, pl.ds(pl.multiple_of(target * share, share), share)]
        if k == 0:
            qout[...] = wanted
            kvout[...] = packed[target]
        else:
            fulls[k][:, :share] = wanted
            fulls[k][:, share:] = packed[target]
    for m in moves:
        m.wait()


def prepare(groups, members, split, query, key_new, value_new, key_stale, value_stale, powers, w_out):
    rows, width = query.shape
    share = width // groups
    depth, model = w_out.shape
    outs = (
        [((rows, share), jnp.bfloat16), ((rows, 2 * share), jnp.bfloat16)]
        + [((rows, 3 * share), jnp.bfloat16)] * (groups - 1)
        + [((depth, model), jnp.bfloat16), ((depth // split, model), jnp.bfloat16)]
    )
    sources = (query, key_new, value_new, key_stale, value_stale, powers, w_out)
    result = pl.pallas_call(
        functools.partial(prepare_kernel, groups, members),
        out_shape=[jax.ShapeDtypeStruct(*o) for o in outs],
        in_specs=[HBM] * 7,
        out_specs=[VMEM] * len(outs),
        scratch_shapes=[pltpu.VMEM((rows, width), jnp.bfloat16)] * 3
        + [pltpu.VMEM((2 * rows, width), jnp.bfloat16)] * 2
        + [
            pltpu.VMEM(powers.shape, jnp.int32),
            pltpu.VMEM((groups, rows, 2 * share), jnp.bfloat16),
            pltpu.SemaphoreType.DMA((8,)),
        ],
        compiler_params=pltpu.CompilerParams(vmem_limit_bytes=24 * 1024 * 1024),
        cost_estimate=pl.CostEstimate(
            flops=10 * rows * width, bytes_accessed=14 * rows * width + 4 * depth * model, transcendentals=0
        ),
    )(*(pltpu.with_memory_space_constraint(x, pltpu.HBM) for x in sources))
    return result[0], result[1 : 1 + groups], result[-2], result[-1]


def attend_kernel(groups, dim, *refs):
    queries = refs[:groups]
    kvs = refs[groups:-2]
    att, kv = refs[-2:]
    share = att.shape[1]
    block = kvs[0].shape[0]
    for j in range(len(kvs)):
        kv[j * block : (j + 1) * block] = kvs[j][...]
    query = jnp.concatenate([q[:, :share].astype(jnp.float32) for q in queries], axis=0).astype(jnp.bfloat16)
    inverse = 1.0 / dim**0.5
    for h in range(share // dim):
        cols = slice(h * dim, (h + 1) * dim)
        scores = (
            lax.dot_general(query[:, cols], kv[:, cols], (((1,), (1,)), ((), ())), preferred_element_type=jnp.float32)
            * inverse
        )
        peak = jnp.max(scores, axis=1, keepdims=True)
        expo = jnp.exp(scores - peak)
        total = jnp.sum(expo, axis=1, keepdims=True)
        numer = jnp.dot(
            expo.astype(jnp.bfloat16),
            kv[:, share + h * dim : share + (h + 1) * dim],
            preferred_element_type=jnp.float32,
        )
        att[:, cols] = (numer / total).astype(jnp.bfloat16)


def attend(groups, dim, queries, kvs):
    rows, share = queries[-1].shape
    block = kvs[0].shape[0]
    pieces = len(kvs)
    return pl.pallas_call(
        functools.partial(attend_kernel, groups, dim),
        out_shape=jax.ShapeDtypeStruct((groups * rows, share), jnp.bfloat16),
        in_specs=[VMEM] * (groups + pieces),
        out_specs=VMEM,
        scratch_shapes=[pltpu.VMEM((pieces * block, 2 * share), jnp.bfloat16)],
        compiler_params=pltpu.CompilerParams(vmem_limit_bytes=24 * 1024 * 1024),
        cost_estimate=pl.CostEstimate(
            flops=4 * groups * rows * pieces * block * share,
            bytes_accessed=4 * pieces * block * share,
            transcendentals=groups * rows * pieces * block * share // dim,
        ),
    )(*queries, *kvs)


def project_kernel(groups, members, places, att, *refs):
    ws = refs[: len(places)]
    outs = refs[len(places) : len(places) + groups]
    wide, sems = refs[len(places) + groups :]
    rows, width = outs[0].shape
    q = lax.axis_index("patch") % members
    side = lax.axis_index("groups") % 2
    copies = []
    for i, (piece, (j, flip, left)) in enumerate(zip(ws, places)):
        size = piece.shape[0]
        row = 0
        if j is not None:
            row = (q ^ j) * (size if flip is None else 2 * size)
            if flip is not None:
                row = row + (side ^ flip) * size
            row = pl.multiple_of(row, size)
        copies.append(pltpu.make_async_copy(piece.at[:, pl.ds(left, width)], wide.at[pl.ds(row, size)], sems.at[i]))
    for c in copies:
        c.start()
    for c in copies:
        c.wait()
    tile = 512 if width % 512 == 0 else width
    for t in range(width // tile):
        cols = slice(t * tile, (t + 1) * tile)
        part = jnp.dot(att[...], wide[:, cols], preferred_element_type=jnp.float32)
        for i in range(groups):
            outs[i][:, cols] = part[i * rows : (i + 1) * rows].astype(outs[i].dtype)


def project(groups, members, att, width, pieces, places):
    rows = att.shape[0] // groups
    share = att.shape[1]
    return pl.pallas_call(
        functools.partial(project_kernel, groups, members, places),
        out_shape=[jax.ShapeDtypeStruct((rows, width), jnp.bfloat16)] * (groups - 1)
        + [jax.ShapeDtypeStruct((rows, width), jnp.float32)],
        in_specs=[VMEM] + [ANY] * len(pieces),
        out_specs=[VMEM] * groups,
        scratch_shapes=[pltpu.VMEM((share, width), jnp.bfloat16), pltpu.SemaphoreType.DMA((len(pieces),))],
        compiler_params=pltpu.CompilerParams(vmem_limit_bytes=24 * 1024 * 1024),
        cost_estimate=pl.CostEstimate(
            flops=2 * groups * rows * share * width, bytes_accessed=2 * share * width, transcendentals=0
        ),
    )(att, *pieces)


def after(x, *others):
    if not others:
        return x
    return lax.optimization_barrier((x, *others))[0]


def per_device(parts, patch, query, key_new, value_new, key_stale, value_stale, exponents, w_out, gate):
    heads = exponents.shape[1] // 2
    rows, width = query.shape
    dim = width // heads
    groups = math.gcd(patch, heads)
    members = patch // groups
    share = width // groups
    depth, model = w_out.shape
    far = members // 2
    shared = parts % 2 == 0 and members == 4 and depth % 32 == 0
    half = model // 2

    def send(x, k, j):
        return lax.ppermute(x, "patch", [(p, ((p // members) ^ k) * members + (p % members) ^ j) for p in range(patch)])

    def swap(x):
        return lax.ppermute(x, "groups", [(g, g ^ 1) for g in range(parts)])

    def spread(pieces, bit):
        while bit:
            for j in list(pieces):
                pieces[j ^ bit] = send(pieces[j], 0, bit)
            bit //= 2
        return [pieces[j] for j in range(members)]

    own_query, fresh, w_own, w_part = prepare(
        groups, members, 2 if shared else 1, query, key_new, value_new, key_stale, value_stale, exponents.T, w_out
    )
    order = range(groups - 1, 0, -1)
    arrived = [send(fresh[k], k, 0) for k in order]
    both = jnp.concatenate([x[:, share:] for x in arrived] + [fresh[0]], axis=0)
    if shared:
        y_part = send(w_part, 0, 2)
        both = after(both, y_part)
    kvs = spread({0: both}, far)
    att = attend(groups, dim, arrived + [own_query], kvs)

    jobs = []
    if shared:
        w_core = send(after(w_own, both), 0, 1)
        y_core = send(after(y_part, both), 0, 1)
        x_part = swap(y_part)
        edges = (0, half, model)
        for left, right in zip(edges, edges[1:]):
            x_core = send(after(x_part, att)[:, left:right], 0, 1)
            pieces = [w_own, w_core, y_part, x_part, y_core, x_core]
            places = [(0, None, left), (1, None, left), (2, 0, left), (2, 1, left), (3, 0, left), (3, 1, 0)]
            jobs.append((right - left, pieces, places))
    else:
        spots = (lax.axis_index("patch") % members) ^ jnp.arange(members)
        jobs.append((model, [jnp.stack(spread({0: w_own}, far))[spots].reshape(-1, model)], [(None, None, 0)]))
    totals = []
    for width, pieces, places in jobs:
        sums = project(groups, members, att, width, pieces, places)
        total = sums[-1]
        for k, part in zip(order, sums):
            total = total + send(part, k, 0).astype(jnp.float32)
        totals.append(total)
    return (jnp.concatenate(totals, axis=1) * gate[None, :]).astype(jnp.bfloat16)


def solution(mesh):
    return jax.shard_map(
        functools.partial(per_device, mesh.shape["groups"], mesh.shape["patch"]),
        mesh=mesh,
        in_specs=(
            P(("groups", "patch"), None),
            P(("groups", "patch"), None),
            P(("groups", "patch"), None),
            P("groups", None),
            P("groups", None),
            P("groups", None),
            P("patch", None),
            P("groups"),
        ),
        out_specs=P(("groups", "patch"), None),
        check_vma=False,
    )
```

```python
import functools
import math

import jax
import jax.numpy as jnp
from jax import lax
from jax.experimental import pallas as pl
from jax.experimental.pallas import tpu as pltpu
from jax.sharding import PartitionSpec as P

CLIP_LIMIT = 2.0
VMEM = pl.BlockSpec(memory_space=pltpu.VMEM)
ANY = pl.BlockSpec(memory_space=pl.ANY)
HBM = pl.BlockSpec(memory_space=pltpu.HBM)


def prepare_kernel(groups, members, *refs):
    sources, w_ref = refs[:6], refs[6]
    outs = refs[7:]
    qout, kvout, fulls = outs[0], outs[1], outs[1 : 1 + groups]
    wout, wpart = outs[1 + groups], outs[2 + groups]
    query, key_new, value_new, kst, vst, est, packed, sems = outs[3 + groups :]
    rows, width = query.shape
    me = lax.axis_index("patch")
    first = pl.multiple_of((me // 2) * (2 * rows), 2 * rows)
    pair = pl.ds(first, 2 * rows)
    views = [sources[0], sources[1], sources[2], sources[3].at[pair], sources[4].at[pair], sources[5]]
    order = (5, 3, 1, 4, 2, 0)
    copies = {
        i: pltpu.make_async_copy(views[i], (query, key_new, value_new, kst, vst, est)[i], sems.at[i]) for i in order
    }
    for i in order:
        copies[i].start()
    size = wpart.shape[0]
    top = pl.multiple_of((lax.axis_index("groups") % 2) * size, size) if size < w_ref.shape[0] else 0
    moves = [
        pltpu.make_async_copy(w_ref.at[pl.ds(top, size)], wpart, sems.at[7]),
        pltpu.make_async_copy(w_ref, wout, sems.at[6]),
    ]
    for m in moves:
        m.start()
    heads = est.shape[0] // 2
    dim = width // heads
    share = width // groups
    odd = me % 2 == 1
    copies[5].wait()
    spot = lax.broadcasted_iota(jnp.int32, (rows, est.shape[1]), 1) == me * rows + lax.broadcasted_iota(
        jnp.int32, (rows, est.shape[1]), 0
    )
    powers = lax.dot_general(
        spot.astype(jnp.float32).astype(jnp.bfloat16),
        est[...].astype(jnp.float32).astype(jnp.bfloat16),
        (((1,), (1,)), ((), ())),
        preferred_element_type=jnp.float32,
    )
    scale = jnp.exp2(powers)
    inverse = jnp.exp2(-powers)
    for side, (fresh, stale) in enumerate(((key_new, kst), (value_new, vst))):
        copies[1 + side].wait()
        copies[3 + side].wait()
        for h in range(heads):
            cols = slice(h * dim, (h + 1) * dim)
            col = side * heads + h
            both = stale[:, cols].astype(jnp.float32)
            base = jnp.where(odd, both[rows:], both[:rows])
            resid = fresh[:, cols].astype(jnp.float32) - base
            codes = jnp.clip(resid * inverse[:, col : col + 1], -CLIP_LIMIT, CLIP_LIMIT)
            codes = codes.astype(jnp.bfloat16).astype(jnp.float32)
            at = side * share + (h * dim) % share
            packed[h * dim // share, :, at : at + dim] = (base + scale[:, col : col + 1] * codes).astype(jnp.bfloat16)
    copies[0].wait()
    for k in range(groups):
        target = (me // members) ^ k
        wanted = query[:, pl.ds(pl.multiple_of(target * share, share), share)]
        if k == 0:
            qout[...] = wanted
            kvout[...] = packed[target]
        else:
            fulls[k][:, :share] = wanted
            fulls[k][:, share:] = packed[target]
    for m in moves:
        m.wait()


def prepare(groups, members, split, query, key_new, value_new, key_stale, value_stale, powers, w_out):
    rows, width = query.shape
    share = width // groups
    depth, model = w_out.shape
    outs = (
        [((rows, share), jnp.bfloat16), ((rows, 2 * share), jnp.bfloat16)]
        + [((rows, 3 * share), jnp.bfloat16)] * (groups - 1)
        + [((depth, model), jnp.bfloat16), ((depth // split, model), jnp.bfloat16)]
    )
    sources = (query, key_new, value_new, key_stale, value_stale, powers, w_out)
    result = pl.pallas_call(
        functools.partial(prepare_kernel, groups, members),
        out_shape=[jax.ShapeDtypeStruct(*o) for o in outs],
        in_specs=[HBM] * 7,
        out_specs=[VMEM] * len(outs),
        scratch_shapes=[pltpu.VMEM((rows, width), jnp.bfloat16)] * 3
        + [pltpu.VMEM((2 * rows, width), jnp.bfloat16)] * 2
        + [
            pltpu.VMEM(powers.shape, jnp.int32),
            pltpu.VMEM((groups, rows, 2 * share), jnp.bfloat16),
            pltpu.SemaphoreType.DMA((8,)),
        ],
        compiler_params=pltpu.CompilerParams(vmem_limit_bytes=24 * 1024 * 1024),
        cost_estimate=pl.CostEstimate(
            flops=10 * rows * width, bytes_accessed=14 * rows * width + 4 * depth * model, transcendentals=0
        ),
    )(*(pltpu.with_memory_space_constraint(x, pltpu.HBM) for x in sources))
    return result[0], result[1 : 1 + groups], result[-2], result[-1]


def attend_kernel(groups, dim, *refs):
    queries = refs[:groups]
    kvs = refs[groups:-2]
    att, kv = refs[-2:]
    share = att.shape[1]
    block = kvs[0].shape[0]
    for j in range(len(kvs)):
        kv[j * block : (j + 1) * block] = kvs[j][...]
    query = jnp.concatenate([q[:, :share].astype(jnp.float32) for q in queries], axis=0).astype(jnp.bfloat16)
    inverse = 1.0 / dim**0.5
    for h in range(share // dim):
        cols = slice(h * dim, (h + 1) * dim)
        scores = (
            lax.dot_general(query[:, cols], kv[:, cols], (((1,), (1,)), ((), ())), preferred_element_type=jnp.float32)
            * inverse
        )
        peak = jnp.max(scores, axis=1, keepdims=True)
        expo = jnp.exp(scores - peak)
        total = jnp.sum(expo, axis=1, keepdims=True)
        numer = jnp.dot(
            expo.astype(jnp.bfloat16),
            kv[:, share + h * dim : share + (h + 1) * dim],
            preferred_element_type=jnp.float32,
        )
        att[:, cols] = (numer / total).astype(jnp.bfloat16)


def attend(groups, dim, queries, kvs):
    rows, share = queries[-1].shape
    block = kvs[0].shape[0]
    pieces = len(kvs)
    return pl.pallas_call(
        functools.partial(attend_kernel, groups, dim),
        out_shape=jax.ShapeDtypeStruct((groups * rows, share), jnp.bfloat16),
        in_specs=[VMEM] * (groups + pieces),
        out_specs=VMEM,
        scratch_shapes=[pltpu.VMEM((pieces * block, 2 * share), jnp.bfloat16)],
        compiler_params=pltpu.CompilerParams(vmem_limit_bytes=24 * 1024 * 1024),
        cost_estimate=pl.CostEstimate(
            flops=4 * groups * rows * pieces * block * share,
            bytes_accessed=4 * pieces * block * share,
            transcendentals=groups * rows * pieces * block * share // dim,
        ),
    )(*queries, *kvs)


def project_kernel(groups, members, places, att, *refs):
    ws = refs[: len(places)]
    outs = refs[len(places) : len(places) + groups]
    wide, sems = refs[len(places) + groups :]
    rows, width = outs[0].shape
    q = lax.axis_index("patch") % members
    side = lax.axis_index("groups") % 2
    copies = []
    for i, (piece, (j, flip, left)) in enumerate(zip(ws, places)):
        size = piece.shape[0]
        row = 0
        if j is not None:
            row = (q ^ j) * (size if flip is None else 2 * size)
            if flip is not None:
                row = row + (side ^ flip) * size
            row = pl.multiple_of(row, size)
        copies.append(pltpu.make_async_copy(piece.at[:, pl.ds(left, width)], wide.at[pl.ds(row, size)], sems.at[i]))
    for c in copies:
        c.start()
    for c in copies:
        c.wait()
    tile = 512 if width % 512 == 0 else width
    for t in range(width // tile):
        cols = slice(t * tile, (t + 1) * tile)
        part = jnp.dot(att[...], wide[:, cols], preferred_element_type=jnp.float32)
        for i in range(groups):
            outs[i][:, cols] = part[i * rows : (i + 1) * rows].astype(outs[i].dtype)


def project(groups, members, att, width, pieces, places):
    rows = att.shape[0] // groups
    share = att.shape[1]
    return pl.pallas_call(
        functools.partial(project_kernel, groups, members, places),
        out_shape=[jax.ShapeDtypeStruct((rows, width), jnp.bfloat16)] * (groups - 1)
        + [jax.ShapeDtypeStruct((rows, width), jnp.float32)],
        in_specs=[VMEM] + [ANY] * len(pieces),
        out_specs=[VMEM] * groups,
        scratch_shapes=[pltpu.VMEM((share, width), jnp.bfloat16), pltpu.SemaphoreType.DMA((len(pieces),))],
        compiler_params=pltpu.CompilerParams(vmem_limit_bytes=24 * 1024 * 1024),
        cost_estimate=pl.CostEstimate(
            flops=2 * groups * rows * share * width, bytes_accessed=2 * share * width, transcendentals=0
        ),
    )(att, *pieces)


def after(x, *others):
    if not others:
        return x
    return lax.optimization_barrier((x, *others))[0]


def per_device(parts, patch, query, key_new, value_new, key_stale, value_stale, exponents, w_out, gate):
    heads = exponents.shape[1] // 2
    rows, width = query.shape
    dim = width // heads
    groups = math.gcd(patch, heads)
    members = patch // groups
    share = width // groups
    depth, model = w_out.shape
    far = members // 2
    shared = parts % 2 == 0 and members == 4 and depth % 32 == 0
    half = model // 2

    def send(x, k, j):
        return lax.ppermute(x, "patch", [(p, ((p // members) ^ k) * members + (p % members) ^ j) for p in range(patch)])

    def swap(x):
        return lax.ppermute(x, "groups", [(g, g ^ 1) for g in range(parts)])

    def spread(pieces, bit):
        while bit:
            for j in list(pieces):
                pieces[j ^ bit] = send(pieces[j], 0, bit)
            bit //= 2
        return [pieces[j] for j in range(members)]

    own_query, fresh, w_own, w_part = prepare(
        groups, members, 2 if shared else 1, query, key_new, value_new, key_stale, value_stale, exponents.T, w_out
    )
    order = range(groups - 1, 0, -1)
    arrived = [send(fresh[k], k, 0) for k in order]
    both = jnp.concatenate([x[:, share:] for x in arrived] + [fresh[0]], axis=0)
    if shared:
        y_part = send(w_part, 0, 2)
        both = after(both, y_part)
    kvs = spread({0: both}, far)
    att = attend(groups, dim, arrived + [own_query], kvs)

    jobs = []
    if shared:
        w_core = send(after(w_own, both), 0, 1)
        y_core = send(after(y_part, both), 0, 1)
        x_part = swap(y_part)
        edges = (0, half, model)
        for left, right in zip(edges, edges[1:]):
            x_core = send(after(x_part, kvs[far])[:, left:right], 0, 1)
            pieces = [w_own, w_core, y_part, x_part, y_core, x_core]
            places = [(0, None, left), (1, None, left), (2, 0, left), (2, 1, left), (3, 0, left), (3, 1, 0)]
            jobs.append((right - left, pieces, places))
    else:
        spots = (lax.axis_index("patch") % members) ^ jnp.arange(members)
        jobs.append((model, [jnp.stack(spread({0: w_own}, far))[spots].reshape(-1, model)], [(None, None, 0)]))
    totals = []
    for width, pieces, places in jobs:
        sums = project(groups, members, att, width, pieces, places)
        att = after(att, *sums)
        total = sums[-1]
        for k, part in zip(order, sums):
            total = total + send(part, k, 0).astype(jnp.float32)
        totals.append(total)
    return (jnp.concatenate(totals, axis=1) * gate[None, :]).astype(jnp.bfloat16)


def solution(mesh):
    return jax.shard_map(
        functools.partial(per_device, mesh.shape["groups"], mesh.shape["patch"]),
        mesh=mesh,
        in_specs=(
            P(("groups", "patch"), None),
            P(("groups", "patch"), None),
            P(("groups", "patch"), None),
            P("groups", None),
            P("groups", None),
            P("groups", None),
            P("patch", None),
            P("groups"),
        ),
        out_specs=P(("groups", "patch"), None),
        check_vma=False,
    )
```

```python
import functools
import math

import jax
import jax.numpy as jnp
from jax import lax
from jax.experimental import pallas as pl
from jax.experimental.pallas import tpu as pltpu
from jax.sharding import PartitionSpec as P

CLIP_LIMIT = 2.0
VMEM = pl.BlockSpec(memory_space=pltpu.VMEM)
ANY = pl.BlockSpec(memory_space=pl.ANY)
HBM = pl.BlockSpec(memory_space=pltpu.HBM)


def prepare_kernel(groups, members, *refs):
    sources, w_ref = refs[:6], refs[6]
    outs = refs[7:]
    qout, kvout, fulls = outs[0], outs[1], outs[1 : 1 + groups]
    wout = outs[1 + groups]
    query, key_new, value_new, kst, vst, est, packed, sems = outs[2 + groups :]
    rows, width = query.shape
    me = lax.axis_index("patch")
    first = pl.multiple_of((me // 2) * (2 * rows), 2 * rows)
    pair = pl.ds(first, 2 * rows)
    views = [sources[0], sources[1], sources[2], sources[3].at[pair], sources[4].at[pair], sources[5]]
    order = (5, 3, 1, 4, 2, 0)
    copies = {
        i: pltpu.make_async_copy(views[i], (query, key_new, value_new, kst, vst, est)[i], sems.at[i]) for i in order
    }
    for i in order:
        copies[i].start()
    move = pltpu.make_async_copy(w_ref, wout, sems.at[6])
    move.start()
    heads = est.shape[0] // 2
    dim = width // heads
    share = width // groups
    odd = me % 2 == 1
    copies[5].wait()
    spot = lax.broadcasted_iota(jnp.int32, (rows, est.shape[1]), 1) == me * rows + lax.broadcasted_iota(
        jnp.int32, (rows, est.shape[1]), 0
    )
    powers = lax.dot_general(
        spot.astype(jnp.float32).astype(jnp.bfloat16),
        est[...].astype(jnp.float32).astype(jnp.bfloat16),
        (((1,), (1,)), ((), ())),
        preferred_element_type=jnp.float32,
    )
    scale = jnp.exp2(powers)
    inverse = jnp.exp2(-powers)
    for side, (fresh, stale) in enumerate(((key_new, kst), (value_new, vst))):
        copies[1 + side].wait()
        copies[3 + side].wait()
        for h in range(heads):
            cols = slice(h * dim, (h + 1) * dim)
            col = side * heads + h
            both = stale[:, cols].astype(jnp.float32)
            base = jnp.where(odd, both[rows:], both[:rows])
            resid = fresh[:, cols].astype(jnp.float32) - base
            codes = jnp.clip(resid * inverse[:, col : col + 1], -CLIP_LIMIT, CLIP_LIMIT)
            codes = codes.astype(jnp.bfloat16).astype(jnp.float32)
            at = side * share + (h * dim) % share
            packed[h * dim // share, :, at : at + dim] = (base + scale[:, col : col + 1] * codes).astype(jnp.bfloat16)
    copies[0].wait()
    for k in range(groups):
        target = (me // members) ^ k
        wanted = query[:, pl.ds(pl.multiple_of(target * share, share), share)]
        if k == 0:
            qout[...] = wanted
            kvout[...] = packed[target]
        else:
            fulls[k][:, :share] = wanted
            fulls[k][:, share:] = packed[target]
    move.wait()


def prepare(groups, members, query, key_new, value_new, key_stale, value_stale, powers, w_out):
    rows, width = query.shape
    share = width // groups
    depth, model = w_out.shape
    outs = (
        [((rows, share), jnp.bfloat16), ((rows, 2 * share), jnp.bfloat16)]
        + [((rows, 3 * share), jnp.bfloat16)] * (groups - 1)
        + [((depth, model), jnp.bfloat16)]
    )
    sources = (query, key_new, value_new, key_stale, value_stale, powers, w_out)
    result = pl.pallas_call(
        functools.partial(prepare_kernel, groups, members),
        out_shape=[jax.ShapeDtypeStruct(*o) for o in outs],
        in_specs=[HBM] * 7,
        out_specs=[VMEM] * len(outs),
        scratch_shapes=[pltpu.VMEM((rows, width), jnp.bfloat16)] * 3
        + [pltpu.VMEM((2 * rows, width), jnp.bfloat16)] * 2
        + [
            pltpu.VMEM(powers.shape, jnp.int32),
            pltpu.VMEM((groups, rows, 2 * share), jnp.bfloat16),
            pltpu.SemaphoreType.DMA((7,)),
        ],
        compiler_params=pltpu.CompilerParams(vmem_limit_bytes=24 * 1024 * 1024),
        cost_estimate=pl.CostEstimate(
            flops=10 * rows * width, bytes_accessed=14 * rows * width + 4 * depth * model, transcendentals=0
        ),
    )(*(pltpu.with_memory_space_constraint(x, pltpu.HBM) for x in sources))
    return result[0], result[1 : 1 + groups], result[-1]


def attend_kernel(groups, dim, *refs):
    queries = refs[:groups]
    kvs = refs[groups:-2]
    att, kv = refs[-2:]
    share = att.shape[1]
    block = kvs[0].shape[0]
    for j in range(len(kvs)):
        kv[j * block : (j + 1) * block] = kvs[j][...]
    query = jnp.concatenate([q[:, :share].astype(jnp.float32) for q in queries], axis=0).astype(jnp.bfloat16)
    inverse = 1.0 / dim**0.5
    for h in range(share // dim):
        cols = slice(h * dim, (h + 1) * dim)
        scores = (
            lax.dot_general(query[:, cols], kv[:, cols], (((1,), (1,)), ((), ())), preferred_element_type=jnp.float32)
            * inverse
        )
        peak = jnp.max(scores, axis=1, keepdims=True)
        expo = jnp.exp(scores - peak)
        total = jnp.sum(expo, axis=1, keepdims=True)
        numer = jnp.dot(
            expo.astype(jnp.bfloat16),
            kv[:, share + h * dim : share + (h + 1) * dim],
            preferred_element_type=jnp.float32,
        )
        att[:, cols] = (numer / total).astype(jnp.bfloat16)


def attend(groups, dim, queries, kvs):
    rows, share = queries[-1].shape
    block = kvs[0].shape[0]
    pieces = len(kvs)
    return pl.pallas_call(
        functools.partial(attend_kernel, groups, dim),
        out_shape=jax.ShapeDtypeStruct((groups * rows, share), jnp.bfloat16),
        in_specs=[VMEM] * (groups + pieces),
        out_specs=VMEM,
        scratch_shapes=[pltpu.VMEM((pieces * block, 2 * share), jnp.bfloat16)],
        compiler_params=pltpu.CompilerParams(vmem_limit_bytes=24 * 1024 * 1024),
        cost_estimate=pl.CostEstimate(
            flops=4 * groups * rows * pieces * block * share,
            bytes_accessed=4 * pieces * block * share,
            transcendentals=groups * rows * pieces * block * share // dim,
        ),
    )(*queries, *kvs)


def project_kernel(groups, members, places, att, *refs):
    ws = refs[: len(places)]
    outs = refs[len(places) : len(places) + groups]
    wide, sems = refs[len(places) + groups :]
    rows, width = outs[0].shape
    q = lax.axis_index("patch") % members
    side = lax.axis_index("groups") % 2
    copies = []
    for i, (piece, (j, flip, left)) in enumerate(zip(ws, places)):
        size = piece.shape[0]
        row = 0
        if j is not None:
            row = (q ^ j) * (size if flip is None else 2 * size)
            if flip is not None:
                row = row + (side ^ flip) * size
            row = pl.multiple_of(row, size)
        copies.append(pltpu.make_async_copy(piece.at[:, pl.ds(left, width)], wide.at[pl.ds(row, size)], sems.at[i]))
    for c in copies:
        c.start()
    for c in copies:
        c.wait()
    tile = 512 if width % 512 == 0 else width
    for t in range(width // tile):
        cols = slice(t * tile, (t + 1) * tile)
        part = jnp.dot(att[...], wide[:, cols], preferred_element_type=jnp.float32)
        for i in range(groups):
            outs[i][:, cols] = part[i * rows : (i + 1) * rows].astype(outs[i].dtype)


def project(groups, members, att, width, pieces, places):
    rows = att.shape[0] // groups
    share = att.shape[1]
    return pl.pallas_call(
        functools.partial(project_kernel, groups, members, places),
        out_shape=[jax.ShapeDtypeStruct((rows, width), jnp.bfloat16)] * (groups - 1)
        + [jax.ShapeDtypeStruct((rows, width), jnp.float32)],
        in_specs=[VMEM] + [ANY] * len(pieces),
        out_specs=[VMEM] * groups,
        scratch_shapes=[pltpu.VMEM((share, width), jnp.bfloat16), pltpu.SemaphoreType.DMA((len(pieces),))],
        compiler_params=pltpu.CompilerParams(vmem_limit_bytes=24 * 1024 * 1024),
        cost_estimate=pl.CostEstimate(
            flops=2 * groups * rows * share * width, bytes_accessed=2 * share * width, transcendentals=0
        ),
    )(att, *pieces)


def after(x, *others):
    if not others:
        return x
    return lax.optimization_barrier((x, *others))[0]


def per_device(parts, patch, query, key_new, value_new, key_stale, value_stale, exponents, w_out, gate):
    heads = exponents.shape[1] // 2
    rows, width = query.shape
    dim = width // heads
    groups = math.gcd(patch, heads)
    members = patch // groups
    share = width // groups
    depth, model = w_out.shape
    far = members // 2
    shared = parts % 2 == 0 and members == 4 and depth % 32 == 0
    half = model // 2

    def send(x, k, j):
        return lax.ppermute(x, "patch", [(p, ((p // members) ^ k) * members + (p % members) ^ j) for p in range(patch)])

    def swap(x):
        return lax.ppermute(x, "groups", [(g, g ^ 1) for g in range(parts)])

    def spread(pieces, bit):
        while bit:
            for j in list(pieces):
                pieces[j ^ bit] = send(pieces[j], 0, bit)
            bit //= 2
        return [pieces[j] for j in range(members)]

    if shared:
        side = lax.axis_index("groups") & 1
        w_part = lax.dynamic_slice_in_dim(w_out, side * (depth // 2), depth // 2, 0)
        y_part = send(w_part, 0, far)
    own_query, fresh, w_own = prepare(
        groups, members, query, key_new, value_new, key_stale, value_stale, exponents.T, w_out
    )
    order = range(groups - 1, 0, -1)
    arrived = [send(fresh[k], k, 0) for k in order]
    both = jnp.concatenate([x[:, share:] for x in arrived] + [fresh[0]], axis=0)
    if shared:
        both = after(both, y_part)
    kvs = spread({0: both}, far)
    att = attend(groups, dim, arrived + [own_query], kvs)

    jobs = []
    if shared:
        w_core = send(after(w_own, both), 0, 1)
        y_core = send(after(y_part, both), 0, 1)
        x_part = swap(y_part)
        edges = (0, half, model)
        for left, right in zip(edges, edges[1:]):
            x_core = send(after(x_part, kvs[far])[:, left:right], 0, 1)
            pieces = [w_own, w_core, y_part, x_part, y_core, x_core]
            places = [(0, None, left), (1, None, left), (2, 0, left), (2, 1, left), (3, 0, left), (3, 1, 0)]
            jobs.append((right - left, pieces, places))
    else:
        spots = (lax.axis_index("patch") % members) ^ jnp.arange(members)
        jobs.append((model, [jnp.stack(spread({0: w_own}, far))[spots].reshape(-1, model)], [(None, None, 0)]))
    totals = []
    for width, pieces, places in jobs:
        sums = project(groups, members, att, width, pieces, places)
        att = after(att, *sums)
        total = sums[-1]
        for k, part in zip(order, sums):
            total = total + send(part, k, 0).astype(jnp.float32)
        totals.append(total)
    return (jnp.concatenate(totals, axis=1) * gate[None, :]).astype(jnp.bfloat16)


def solution(mesh):
    return jax.shard_map(
        functools.partial(per_device, mesh.shape["groups"], mesh.shape["patch"]),
        mesh=mesh,
        in_specs=(
            P(("groups", "patch"), None),
            P(("groups", "patch"), None),
            P(("groups", "patch"), None),
            P("groups", None),
            P("groups", None),
            P("groups", None),
            P("patch", None),
            P("groups"),
        ),
        out_specs=P(("groups", "patch"), None),
        check_vma=False,
    )
```

```python
import functools
import math

import jax
import jax.numpy as jnp
from jax import lax
from jax.experimental import pallas as pl
from jax.experimental.pallas import tpu as pltpu
from jax.sharding import PartitionSpec as P

CLIP_LIMIT = 2.0
VMEM = pl.BlockSpec(memory_space=pltpu.VMEM)
ANY = pl.BlockSpec(memory_space=pl.ANY)
HBM = pl.BlockSpec(memory_space=pltpu.HBM)


def prepare_kernel(groups, members, *refs):
    sources, w_ref = refs[:6], refs[6]
    outs = refs[7:]
    qout, kvout, fulls = outs[0], outs[1], outs[1 : 1 + groups]
    wout = outs[1 + groups]
    query, key_new, value_new, kst, vst, est, packed, sems = outs[2 + groups :]
    rows, width = query.shape
    me = lax.axis_index("patch")
    first = pl.multiple_of((me // 2) * (2 * rows), 2 * rows)
    pair = pl.ds(first, 2 * rows)
    views = [sources[0], sources[1], sources[2], sources[3].at[pair], sources[4].at[pair], sources[5]]
    order = (5, 3, 1, 4, 2, 0)
    copies = {
        i: pltpu.make_async_copy(views[i], (query, key_new, value_new, kst, vst, est)[i], sems.at[i]) for i in order
    }
    for i in order:
        copies[i].start()
    move = pltpu.make_async_copy(w_ref, wout, sems.at[6])
    move.start()
    heads = est.shape[0] // 2
    dim = width // heads
    share = width // groups
    odd = me % 2 == 1
    copies[5].wait()
    spot = lax.broadcasted_iota(jnp.int32, (rows, est.shape[1]), 1) == me * rows + lax.broadcasted_iota(
        jnp.int32, (rows, est.shape[1]), 0
    )
    powers = lax.dot_general(
        spot.astype(jnp.float32).astype(jnp.bfloat16),
        est[...].astype(jnp.float32).astype(jnp.bfloat16),
        (((1,), (1,)), ((), ())),
        preferred_element_type=jnp.float32,
    )
    scale = jnp.exp2(powers)
    inverse = jnp.exp2(-powers)
    for side, (fresh, stale) in enumerate(((key_new, kst), (value_new, vst))):
        copies[1 + side].wait()
        copies[3 + side].wait()
        for h in range(heads):
            cols = slice(h * dim, (h + 1) * dim)
            col = side * heads + h
            both = stale[:, cols].astype(jnp.float32)
            base = jnp.where(odd, both[rows:], both[:rows])
            resid = fresh[:, cols].astype(jnp.float32) - base
            codes = jnp.clip(resid * inverse[:, col : col + 1], -CLIP_LIMIT, CLIP_LIMIT)
            codes = codes.astype(jnp.bfloat16).astype(jnp.float32)
            at = side * share + (h * dim) % share
            packed[h * dim // share, :, at : at + dim] = (base + scale[:, col : col + 1] * codes).astype(jnp.bfloat16)
    copies[0].wait()
    for k in range(groups):
        target = (me // members) ^ k
        wanted = query[:, pl.ds(pl.multiple_of(target * share, share), share)]
        if k == 0:
            qout[...] = wanted
            kvout[...] = packed[target]
        else:
            fulls[k][:, :share] = wanted
            fulls[k][:, share:] = packed[target]
    move.wait()


def prepare(groups, members, query, key_new, value_new, key_stale, value_stale, powers, w_out):
    rows, width = query.shape
    share = width // groups
    depth, model = w_out.shape
    outs = (
        [((rows, share), jnp.bfloat16), ((rows, 2 * share), jnp.bfloat16)]
        + [((rows, 3 * share), jnp.bfloat16)] * (groups - 1)
        + [((depth, model), jnp.bfloat16)]
    )
    sources = (query, key_new, value_new, key_stale, value_stale, powers, w_out)
    result = pl.pallas_call(
        functools.partial(prepare_kernel, groups, members),
        out_shape=[jax.ShapeDtypeStruct(*o) for o in outs],
        in_specs=[HBM] * 7,
        out_specs=[VMEM] * len(outs),
        scratch_shapes=[pltpu.VMEM((rows, width), jnp.bfloat16)] * 3
        + [pltpu.VMEM((2 * rows, width), jnp.bfloat16)] * 2
        + [
            pltpu.VMEM(powers.shape, jnp.int32),
            pltpu.VMEM((groups, rows, 2 * share), jnp.bfloat16),
            pltpu.SemaphoreType.DMA((7,)),
        ],
        compiler_params=pltpu.CompilerParams(vmem_limit_bytes=24 * 1024 * 1024),
        cost_estimate=pl.CostEstimate(
            flops=10 * rows * width, bytes_accessed=14 * rows * width + 4 * depth * model, transcendentals=0
        ),
    )(*(pltpu.with_memory_space_constraint(x, pltpu.HBM) for x in sources))
    return result[0], result[1 : 1 + groups], result[-1]


def attend_kernel(groups, dim, *refs):
    queries = refs[:groups]
    kvs = refs[groups:-2]
    att, kv = refs[-2:]
    share = att.shape[1]
    block = kvs[0].shape[0]
    for j in range(len(kvs)):
        kv[j * block : (j + 1) * block] = kvs[j][...]
    query = jnp.concatenate([q[:, :share].astype(jnp.float32) for q in queries], axis=0).astype(jnp.bfloat16)
    inverse = 1.0 / dim**0.5
    for h in range(share // dim):
        cols = slice(h * dim, (h + 1) * dim)
        scores = (
            lax.dot_general(query[:, cols], kv[:, cols], (((1,), (1,)), ((), ())), preferred_element_type=jnp.float32)
            * inverse
        )
        peak = jnp.max(scores, axis=1, keepdims=True)
        expo = jnp.exp(scores - peak)
        total = jnp.sum(expo, axis=1, keepdims=True)
        numer = jnp.dot(
            expo.astype(jnp.bfloat16),
            kv[:, share + h * dim : share + (h + 1) * dim],
            preferred_element_type=jnp.float32,
        )
        att[:, cols] = (numer / total).astype(jnp.bfloat16)


def attend(groups, dim, queries, kvs):
    rows, share = queries[-1].shape
    block = kvs[0].shape[0]
    pieces = len(kvs)
    return pl.pallas_call(
        functools.partial(attend_kernel, groups, dim),
        out_shape=jax.ShapeDtypeStruct((groups * rows, share), jnp.bfloat16),
        in_specs=[VMEM] * (groups + pieces),
        out_specs=VMEM,
        scratch_shapes=[pltpu.VMEM((pieces * block, 2 * share), jnp.bfloat16)],
        compiler_params=pltpu.CompilerParams(vmem_limit_bytes=24 * 1024 * 1024),
        cost_estimate=pl.CostEstimate(
            flops=4 * groups * rows * pieces * block * share,
            bytes_accessed=4 * pieces * block * share,
            transcendentals=groups * rows * pieces * block * share // dim,
        ),
    )(*queries, *kvs)


def project_kernel(groups, members, left, places, att, *refs):
    ws = refs[: 2 * len(places)]
    outs = refs[2 * len(places) : 2 * len(places) + groups]
    wide, sems = refs[2 * len(places) + groups :]
    rows, width = outs[0].shape
    me = lax.axis_index("patch")
    direct = ((me ^ lax.axis_index("groups")) & 1) == 0
    waits = []
    for i, j in enumerate(places):
        depth = ws[2 * i].shape[0]
        row = 0 if j is None else pl.multiple_of(((me % members) ^ j) * depth, depth)
        views = [w if w.shape[1] == width else w.at[:, pl.ds(left, width)] for w in ws[2 * i : 2 * i + 2]]
        copies = [pltpu.make_async_copy(v, wide.at[pl.ds(row, depth)], sems.at[i]) for v in views]
        pl.when(direct)(copies[0].start)
        pl.when(jnp.logical_not(direct))(copies[1].start)
        waits.append(copies[0])
    for c in waits:
        c.wait()
    tile = 512 if width % 512 == 0 else width
    for t in range(width // tile):
        cols = slice(t * tile, (t + 1) * tile)
        part = jnp.dot(att[...], wide[:, cols], preferred_element_type=jnp.float32)
        for i in range(groups):
            outs[i][:, cols] = part[i * rows : (i + 1) * rows].astype(outs[i].dtype)


def project(groups, members, att, width, left, pieces):
    rows = att.shape[0] // groups
    share = att.shape[1]
    places = [p[0] for p in pieces]
    ws = [w for p in pieces for w in p[1:]]
    return pl.pallas_call(
        functools.partial(project_kernel, groups, members, left, places),
        out_shape=[jax.ShapeDtypeStruct((rows, width), jnp.bfloat16)] * (groups - 1)
        + [jax.ShapeDtypeStruct((rows, width), jnp.float32)],
        in_specs=[VMEM] + [ANY] * len(ws),
        out_specs=[VMEM] * groups,
        scratch_shapes=[pltpu.VMEM((share, width), jnp.bfloat16), pltpu.SemaphoreType.DMA((len(places),))],
        compiler_params=pltpu.CompilerParams(vmem_limit_bytes=24 * 1024 * 1024),
        cost_estimate=pl.CostEstimate(
            flops=2 * groups * rows * share * width, bytes_accessed=2 * share * width, transcendentals=0
        ),
    )(att, *ws)


def after(x, *others):
    if not others:
        return x
    return lax.optimization_barrier((x, *others))[0]


def per_device(parts, patch, query, key_new, value_new, key_stale, value_stale, exponents, w_out, gate):
    heads = exponents.shape[1] // 2
    rows, width = query.shape
    dim = width // heads
    groups = math.gcd(patch, heads)
    members = patch // groups
    share = width // groups
    depth, model = w_out.shape
    far = members // 2
    shared = parts % 2 == 0 and members == 4 and depth % 32 == 0
    half = model // 2

    def send(x, k, j):
        return lax.ppermute(x, "patch", [(p, ((p // members) ^ k) * members + (p % members) ^ j) for p in range(patch)])

    def swap(x):
        return lax.ppermute(x, "groups", [(g, g ^ 1) for g in range(parts)])

    def spread(pieces, bit):
        while bit:
            for j in list(pieces):
                pieces[j ^ bit] = send(pieces[j], 0, bit)
            bit //= 2
        return [pieces[j] for j in range(members)]

    def relay(x, direct, move):
        everyone = [(g, p) for g in range(parts) for p in range(patch) if ((g ^ p) & 1 == 0) == direct]
        pairs = [(g * patch + p, move(g, p)[0] * patch + move(g, p)[1]) for g, p in everyone]
        return lax.ppermute(x, ("groups", "patch"), pairs)

    if shared:
        w_far = relay(w_out, True, lambda g, p: (g, p ^ 2))
    own_query, fresh, w_own = prepare(
        groups, members, query, key_new, value_new, key_stale, value_stale, exponents.T, w_out
    )
    order = range(groups - 1, 0, -1)
    arrived = [send(fresh[k], k, 0) for k in order]
    both = jnp.concatenate([x[:, share:] for x in arrived] + [fresh[0]], axis=0)
    if shared:
        both = after(both, w_far)
    kvs = spread({0: both}, far)
    att = attend(groups, dim, arrived + [own_query], kvs)

    jobs = []
    if shared:
        w_core = send(after(w_own, both), 0, 1)
        w_diagonal = relay(after(w_far, both), True, lambda g, p: (g, p ^ 1))
        w_swapped = relay(after(w_far, *arrived), True, lambda g, p: (g ^ 1, p))
        for left in (0, half):
            crossed = relay(after(w_swapped, *kvs)[:, left : left + half], False, lambda g, p: (g, p ^ 1))
            pieces = [(0, w_own, w_own), (1, w_core, w_core), (2, w_far, w_swapped), (3, crossed, w_diagonal)]
            jobs.append((half, left, pieces))
    else:
        spots = (lax.axis_index("patch") % members) ^ jnp.arange(members)
        whole = jnp.stack(spread({0: w_own}, far))[spots].reshape(-1, model)
        jobs.append((model, 0, [(None, whole, whole)]))
    totals = []
    for width, left, pieces in jobs:
        sums = project(groups, members, att, width, left, pieces)
        att = after(att, *sums)
        total = sums[-1]
        for k, part in zip(order, sums):
            total = total + send(part, k, 0).astype(jnp.float32)
        totals.append(total)
    return (jnp.concatenate(totals, axis=1) * gate[None, :]).astype(jnp.bfloat16)


def solution(mesh):
    return jax.shard_map(
        functools.partial(per_device, mesh.shape["groups"], mesh.shape["patch"]),
        mesh=mesh,
        in_specs=(
            P(("groups", "patch"), None),
            P(("groups", "patch"), None),
            P(("groups", "patch"), None),
            P("groups", None),
            P("groups", None),
            P("groups", None),
            P("patch", None),
            P("groups"),
        ),
        out_specs=P(("groups", "patch"), None),
        check_vma=False,
    )
```

```python
import functools
import math

import jax
import jax.numpy as jnp
from jax import lax
from jax.experimental import pallas as pl
from jax.experimental.pallas import tpu as pltpu
from jax.sharding import PartitionSpec as P

CLIP_LIMIT = 2.0
VMEM = pl.BlockSpec(memory_space=pltpu.VMEM)
HBM = pl.BlockSpec(memory_space=pltpu.HBM)


def prepare_kernel(groups, members, *refs):
    sources, w_ref = refs[:6], refs[6]
    outs = refs[7:]
    qout, kvout, fulls = outs[0], outs[1], outs[1 : 1 + groups]
    wout = outs[1 + groups]
    query, key_new, value_new, kst, vst, est, packed, sems = outs[2 + groups :]
    rows, width = query.shape
    me = lax.axis_index("patch")
    first = pl.multiple_of((me // 2) * (2 * rows), 2 * rows)
    pair = pl.ds(first, 2 * rows)
    views = [sources[0], sources[1], sources[2], sources[3].at[pair], sources[4].at[pair], sources[5]]
    order = (5, 3, 1, 4, 2, 0)
    copies = {
        i: pltpu.make_async_copy(views[i], (query, key_new, value_new, kst, vst, est)[i], sems.at[i]) for i in order
    }
    for i in order:
        copies[i].start()
    move = pltpu.make_async_copy(w_ref, wout, sems.at[6])
    move.start()
    heads = est.shape[0] // 2
    dim = width // heads
    share = width // groups
    odd = me % 2 == 1
    copies[5].wait()
    spot = lax.broadcasted_iota(jnp.int32, (rows, est.shape[1]), 1) == me * rows + lax.broadcasted_iota(
        jnp.int32, (rows, est.shape[1]), 0
    )
    powers = lax.dot_general(
        spot.astype(jnp.float32).astype(jnp.bfloat16),
        est[...].astype(jnp.float32).astype(jnp.bfloat16),
        (((1,), (1,)), ((), ())),
        preferred_element_type=jnp.float32,
    )
    scale = jnp.exp2(powers)
    inverse = jnp.exp2(-powers)
    for side, (fresh, stale) in enumerate(((key_new, kst), (value_new, vst))):
        copies[1 + side].wait()
        copies[3 + side].wait()
        for h in range(heads):
            cols = slice(h * dim, (h + 1) * dim)
            col = side * heads + h
            both = stale[:, cols].astype(jnp.float32)
            base = jnp.where(odd, both[rows:], both[:rows])
            resid = fresh[:, cols].astype(jnp.float32) - base
            codes = jnp.clip(resid * inverse[:, col : col + 1], -CLIP_LIMIT, CLIP_LIMIT)
            codes = codes.astype(jnp.bfloat16).astype(jnp.float32)
            at = side * share + (h * dim) % share
            packed[h * dim // share, :, at : at + dim] = (base + scale[:, col : col + 1] * codes).astype(jnp.bfloat16)
    copies[0].wait()
    for k in range(groups):
        target = (me // members) ^ k
        wanted = query[:, pl.ds(pl.multiple_of(target * share, share), share)]
        if k == 0:
            qout[...] = wanted
            kvout[...] = packed[target]
        else:
            fulls[k][:, :share] = wanted
            fulls[k][:, share:] = packed[target]
    move.wait()


def prepare(groups, members, query, key_new, value_new, key_stale, value_stale, powers, w_out):
    rows, width = query.shape
    share = width // groups
    depth, model = w_out.shape
    outs = (
        [((rows, share), jnp.bfloat16), ((rows, 2 * share), jnp.bfloat16)]
        + [((rows, 3 * share), jnp.bfloat16)] * (groups - 1)
        + [((depth, model), jnp.bfloat16)]
    )
    sources = (query, key_new, value_new, key_stale, value_stale, powers, w_out)
    result = pl.pallas_call(
        functools.partial(prepare_kernel, groups, members),
        out_shape=[jax.ShapeDtypeStruct(*o) for o in outs],
        in_specs=[HBM] * 7,
        out_specs=[VMEM] * len(outs),
        scratch_shapes=[pltpu.VMEM((rows, width), jnp.bfloat16)] * 3
        + [pltpu.VMEM((2 * rows, width), jnp.bfloat16)] * 2
        + [
            pltpu.VMEM(powers.shape, jnp.int32),
            pltpu.VMEM((groups, rows, 2 * share), jnp.bfloat16),
            pltpu.SemaphoreType.DMA((7,)),
        ],
        compiler_params=pltpu.CompilerParams(vmem_limit_bytes=24 * 1024 * 1024),
        cost_estimate=pl.CostEstimate(
            flops=10 * rows * width, bytes_accessed=14 * rows * width + 4 * depth * model, transcendentals=0
        ),
    )(*(pltpu.with_memory_space_constraint(x, pltpu.HBM) for x in sources))
    return result[0], result[1 : 1 + groups], result[-1]


def share_kernel(w_ref, out_ref, sem):
    size = out_ref.shape[0]
    top = pl.multiple_of((lax.axis_index("groups") & 1) * size, size)
    copy = pltpu.make_async_copy(w_ref.at[pl.ds(top, size)], out_ref, sem)
    copy.start()
    copy.wait()


def share_rows(w_out):
    depth, model = w_out.shape
    return pl.pallas_call(
        share_kernel,
        out_shape=jax.ShapeDtypeStruct((depth // 2, model), w_out.dtype),
        in_specs=[HBM],
        out_specs=VMEM,
        scratch_shapes=[pltpu.SemaphoreType.DMA],
        compiler_params=pltpu.CompilerParams(vmem_limit_bytes=24 * 1024 * 1024),
        cost_estimate=pl.CostEstimate(flops=0, bytes_accessed=2 * depth * model, transcendentals=0),
    )(pltpu.with_memory_space_constraint(w_out, pltpu.HBM))


def attend_kernel(groups, dim, *refs):
    queries = refs[:groups]
    kvs = refs[groups:-2]
    att, kv = refs[-2:]
    share = att.shape[1]
    block = kvs[0].shape[0]
    for j in range(len(kvs)):
        kv[j * block : (j + 1) * block] = kvs[j][...]
    query = jnp.concatenate([q[:, :share].astype(jnp.float32) for q in queries], axis=0).astype(jnp.bfloat16)
    inverse = 1.0 / dim**0.5
    for h in range(share // dim):
        cols = slice(h * dim, (h + 1) * dim)
        scores = (
            lax.dot_general(query[:, cols], kv[:, cols], (((1,), (1,)), ((), ())), preferred_element_type=jnp.float32)
            * inverse
        )
        peak = jnp.max(scores, axis=1, keepdims=True)
        expo = jnp.exp(scores - peak)
        total = jnp.sum(expo, axis=1, keepdims=True)
        numer = jnp.dot(
            expo.astype(jnp.bfloat16),
            kv[:, share + h * dim : share + (h + 1) * dim],
            preferred_element_type=jnp.float32,
        )
        att[:, cols] = (numer / total).astype(jnp.bfloat16)


def attend(groups, dim, queries, kvs):
    rows, share = queries[-1].shape
    block = kvs[0].shape[0]
    pieces = len(kvs)
    return pl.pallas_call(
        functools.partial(attend_kernel, groups, dim),
        out_shape=jax.ShapeDtypeStruct((groups * rows, share), jnp.bfloat16),
        in_specs=[VMEM] * (groups + pieces),
        out_specs=VMEM,
        scratch_shapes=[pltpu.VMEM((pieces * block, 2 * share), jnp.bfloat16)],
        compiler_params=pltpu.CompilerParams(vmem_limit_bytes=24 * 1024 * 1024),
        cost_estimate=pl.CostEstimate(
            flops=4 * groups * rows * pieces * block * share,
            bytes_accessed=4 * pieces * block * share,
            transcendentals=groups * rows * pieces * block * share // dim,
        ),
    )(*queries, *kvs)


def project_kernel(groups, members, places, att, *refs):
    ws = refs[: len(places)]
    outs = refs[len(places) : len(places) + groups]
    wide = refs[-1]
    rows, width = outs[0].shape
    q = lax.axis_index("patch") % members
    side = lax.axis_index("groups") & 1
    for piece, (j, flip, left) in zip(ws, places):
        size = piece.shape[0]
        row = 0
        if j is not None:
            row = (q ^ j) * (size if flip is None else 2 * size)
            if flip is not None:
                row = row + (side ^ flip) * size
            row = pl.multiple_of(row, size)
        wide[pl.ds(row, size), :] = piece[:, left : left + width]
    tile = 256 if width % 256 == 0 else width
    for t in range(width // tile):
        cols = slice(t * tile, (t + 1) * tile)
        part = jnp.dot(att[...], wide[:, cols], preferred_element_type=jnp.float32)
        for i in range(groups):
            outs[i][:, cols] = part[i * rows : (i + 1) * rows].astype(outs[i].dtype)


def project(groups, members, att, width, pieces, places):
    rows = att.shape[0] // groups
    share = att.shape[1]
    return pl.pallas_call(
        functools.partial(project_kernel, groups, members, places),
        out_shape=[jax.ShapeDtypeStruct((rows, width), jnp.bfloat16)] * (groups - 1)
        + [jax.ShapeDtypeStruct((rows, width), jnp.float32)],
        in_specs=[VMEM] * (1 + len(pieces)),
        out_specs=[VMEM] * groups,
        scratch_shapes=[pltpu.VMEM((share, width), jnp.bfloat16)],
        compiler_params=pltpu.CompilerParams(vmem_limit_bytes=24 * 1024 * 1024),
        cost_estimate=pl.CostEstimate(
            flops=2 * groups * rows * share * width, bytes_accessed=2 * share * width, transcendentals=0
        ),
    )(att, *pieces)


def after(x, *others):
    if not others:
        return x
    return lax.optimization_barrier((x, *others))[0]


def per_device(parts, patch, query, key_new, value_new, key_stale, value_stale, exponents, w_out, gate):
    heads = exponents.shape[1] // 2
    rows, width = query.shape
    dim = width // heads
    groups = math.gcd(patch, heads)
    members = patch // groups
    share = width // groups
    depth, model = w_out.shape
    far = members // 2
    shared = parts % 2 == 0 and members == 4 and depth % 32 == 0
    first = model // 2

    def send(x, k, j):
        return lax.ppermute(x, "patch", [(p, ((p // members) ^ k) * members + (p % members) ^ j) for p in range(patch)])

    def swap(x):
        return lax.ppermute(x, "groups", [(g, g ^ 1) for g in range(parts)])

    def spread(pieces, bit):
        while bit:
            for j in list(pieces):
                pieces[j ^ bit] = send(pieces[j], 0, bit)
            bit //= 2
        return [pieces[j] for j in range(members)]

    if shared:
        w_part = share_rows(w_out)
        y_part = send(w_part, 0, far)
    own_query, fresh, w_own = prepare(
        groups, members, query, key_new, value_new, key_stale, value_stale, exponents.T, w_out
    )
    order = range(groups - 1, 0, -1)
    arrived = [send(fresh[k], k, 0) for k in order]
    both = jnp.concatenate([x[:, share:] for x in arrived] + [fresh[0]], axis=0)
    if shared:
        both = after(both, y_part)
    kvs = spread({0: both}, far)
    att = attend(groups, dim, arrived + [own_query], kvs)

    jobs = []
    if shared:
        w_core = send(after(w_own, both), 0, 1)
        y_core = send(after(y_part, both), 0, 1)
        x_part = swap(y_part)
        edges = (0, first, model)
        for left, right in zip(edges, edges[1:]):
            x_core = send(after(x_part, kvs[far])[:, left:right], 0, 1)
            pieces = [w_own, w_core, y_part, x_part, y_core, x_core]
            places = [(0, None, left), (1, None, left), (2, 0, left), (2, 1, left), (3, 0, left), (3, 1, 0)]
            jobs.append((right - left, pieces, places))
    else:
        spots = (lax.axis_index("patch") % members) ^ jnp.arange(members)
        jobs.append((model, [jnp.stack(spread({0: w_own}, far))[spots].reshape(-1, model)], [(None, None, 0)]))
    totals = []
    for width, pieces, places in jobs:
        sums = project(groups, members, att, width, pieces, places)
        att = after(att, *sums)
        total = sums[-1]
        for k, part in zip(order, sums):
            total = total + send(part, k, 0).astype(jnp.float32)
        totals.append(total)
    return (jnp.concatenate(totals, axis=1) * gate[None, :]).astype(jnp.bfloat16)


def solution(mesh):
    return jax.shard_map(
        functools.partial(per_device, mesh.shape["groups"], mesh.shape["patch"]),
        mesh=mesh,
        in_specs=(
            P(("groups", "patch"), None),
            P(("groups", "patch"), None),
            P(("groups", "patch"), None),
            P("groups", None),
            P("groups", None),
            P("groups", None),
            P("patch", None),
            P("groups"),
        ),
        out_specs=P(("groups", "patch"), None),
        check_vma=False,
    )
```

```python
import functools
import math

import jax
import jax.numpy as jnp
from jax import lax
from jax.experimental import pallas as pl
from jax.experimental.pallas import tpu as pltpu
from jax.sharding import PartitionSpec as P

CLIP_LIMIT = 2.0
VMEM = pl.BlockSpec(memory_space=pltpu.VMEM)
HBM = pl.BlockSpec(memory_space=pltpu.HBM)


def prepare_kernel(groups, members, *refs):
    sources, w_ref = refs[:6], refs[6]
    outs = refs[7:]
    qout, kvout, fulls = outs[0], outs[1], outs[1 : 1 + groups]
    wout = outs[1 + groups]
    query, key_new, value_new, kst, vst, est, packed, sems = outs[2 + groups :]
    rows, width = query.shape
    me = lax.axis_index("patch")
    first = pl.multiple_of((me // 2) * (2 * rows), 2 * rows)
    pair = pl.ds(first, 2 * rows)
    views = [sources[0], sources[1], sources[2], sources[3].at[pair], sources[4].at[pair], sources[5]]
    order = (5, 3, 1, 4, 2, 0)
    copies = {
        i: pltpu.make_async_copy(views[i], (query, key_new, value_new, kst, vst, est)[i], sems.at[i]) for i in order
    }
    for i in order:
        copies[i].start()
    size = wout.shape[0]
    top = pl.multiple_of((lax.axis_index("groups") & 1) * size, size) if size < w_ref.shape[0] else 0
    move = pltpu.make_async_copy(w_ref.at[pl.ds(top, size)], wout, sems.at[6])
    move.start()
    heads = est.shape[0] // 2
    dim = width // heads
    share = width // groups
    odd = me % 2 == 1
    copies[5].wait()
    spot = lax.broadcasted_iota(jnp.int32, (rows, est.shape[1]), 1) == me * rows + lax.broadcasted_iota(
        jnp.int32, (rows, est.shape[1]), 0
    )
    powers = lax.dot_general(
        spot.astype(jnp.float32).astype(jnp.bfloat16),
        est[...].astype(jnp.float32).astype(jnp.bfloat16),
        (((1,), (1,)), ((), ())),
        preferred_element_type=jnp.float32,
    )
    scale = jnp.exp2(powers)
    inverse = jnp.exp2(-powers)
    for side, (fresh, stale) in enumerate(((key_new, kst), (value_new, vst))):
        copies[1 + side].wait()
        copies[3 + side].wait()
        for h in range(heads):
            cols = slice(h * dim, (h + 1) * dim)
            col = side * heads + h
            both = stale[:, cols].astype(jnp.float32)
            base = jnp.where(odd, both[rows:], both[:rows])
            resid = fresh[:, cols].astype(jnp.float32) - base
            codes = jnp.clip(resid * inverse[:, col : col + 1], -CLIP_LIMIT, CLIP_LIMIT)
            codes = codes.astype(jnp.bfloat16).astype(jnp.float32)
            at = side * share + (h * dim) % share
            packed[h * dim // share, :, at : at + dim] = (base + scale[:, col : col + 1] * codes).astype(jnp.bfloat16)
    copies[0].wait()
    for k in range(groups):
        target = (me // members) ^ k
        wanted = query[:, pl.ds(pl.multiple_of(target * share, share), share)]
        if k == 0:
            qout[...] = wanted
            kvout[...] = packed[target]
        else:
            fulls[k][:, :share] = wanted
            fulls[k][:, share:] = packed[target]
    move.wait()


def prepare(groups, members, split, query, key_new, value_new, key_stale, value_stale, powers, w_out):
    rows, width = query.shape
    share = width // groups
    depth, model = w_out.shape
    outs = (
        [((rows, share), jnp.bfloat16), ((rows, 2 * share), jnp.bfloat16)]
        + [((rows, 3 * share), jnp.bfloat16)] * (groups - 1)
        + [((depth // split, model), jnp.bfloat16)]
    )
    sources = (query, key_new, value_new, key_stale, value_stale, powers, w_out)
    result = pl.pallas_call(
        functools.partial(prepare_kernel, groups, members),
        out_shape=[jax.ShapeDtypeStruct(*o) for o in outs],
        in_specs=[HBM] * 7,
        out_specs=[VMEM] * len(outs),
        scratch_shapes=[pltpu.VMEM((rows, width), jnp.bfloat16)] * 3
        + [pltpu.VMEM((2 * rows, width), jnp.bfloat16)] * 2
        + [
            pltpu.VMEM(powers.shape, jnp.int32),
            pltpu.VMEM((groups, rows, 2 * share), jnp.bfloat16),
            pltpu.SemaphoreType.DMA((7,)),
        ],
        compiler_params=pltpu.CompilerParams(vmem_limit_bytes=24 * 1024 * 1024),
        cost_estimate=pl.CostEstimate(
            flops=10 * rows * width, bytes_accessed=14 * rows * width + 4 * (depth // split) * model, transcendentals=0
        ),
    )(*(pltpu.with_memory_space_constraint(x, pltpu.HBM) for x in sources))
    return result[0], result[1 : 1 + groups], result[-1]


def attend_kernel(groups, dim, *refs):
    queries = refs[:groups]
    kvs = refs[groups:-5]
    w_ref, att, w_own, kv, sem = refs[-5:]
    copy = pltpu.make_async_copy(w_ref, w_own, sem)
    copy.start()
    share = att.shape[1]
    block = kvs[0].shape[0]
    for j in range(len(kvs)):
        kv[j * block : (j + 1) * block] = kvs[j][...]
    query = jnp.concatenate([q[:, :share].astype(jnp.float32) for q in queries], axis=0).astype(jnp.bfloat16)
    inverse = 1.0 / dim**0.5
    for h in range(share // dim):
        cols = slice(h * dim, (h + 1) * dim)
        scores = (
            lax.dot_general(query[:, cols], kv[:, cols], (((1,), (1,)), ((), ())), preferred_element_type=jnp.float32)
            * inverse
        )
        peak = jnp.max(scores, axis=1, keepdims=True)
        expo = jnp.exp(scores - peak)
        total = jnp.sum(expo, axis=1, keepdims=True)
        numer = jnp.dot(
            expo.astype(jnp.bfloat16),
            kv[:, share + h * dim : share + (h + 1) * dim],
            preferred_element_type=jnp.float32,
        )
        att[:, cols] = (numer / total).astype(jnp.bfloat16)
    copy.wait()


def attend(groups, dim, queries, kvs, w_out):
    rows, share = queries[-1].shape
    block = kvs[0].shape[0]
    pieces = len(kvs)
    return pl.pallas_call(
        functools.partial(attend_kernel, groups, dim),
        out_shape=[
            jax.ShapeDtypeStruct((groups * rows, share), jnp.bfloat16),
            jax.ShapeDtypeStruct(w_out.shape, w_out.dtype),
        ],
        in_specs=[VMEM] * (groups + pieces) + [HBM],
        out_specs=[VMEM] * 2,
        scratch_shapes=[pltpu.VMEM((pieces * block, 2 * share), jnp.bfloat16), pltpu.SemaphoreType.DMA],
        compiler_params=pltpu.CompilerParams(vmem_limit_bytes=24 * 1024 * 1024),
        cost_estimate=pl.CostEstimate(
            flops=4 * groups * rows * pieces * block * share,
            bytes_accessed=4 * pieces * block * share,
            transcendentals=groups * rows * pieces * block * share // dim,
        ),
    )(*queries, *kvs, pltpu.with_memory_space_constraint(w_out, pltpu.HBM))


def project_kernel(groups, members, places, att, *refs):
    ws = refs[: len(places)]
    outs = refs[len(places) : len(places) + groups]
    wide = refs[-1]
    rows, width = outs[0].shape
    q = lax.axis_index("patch") % members
    side = lax.axis_index("groups") & 1
    for piece, (j, flip, left) in zip(ws, places):
        size = piece.shape[0]
        row = 0
        if j is not None:
            row = (q ^ j) * (size if flip is None else 2 * size)
            if flip is not None:
                row = row + (side ^ flip) * size
            row = pl.multiple_of(row, size)
        wide[pl.ds(row, size), :] = piece[:, left : left + width]
    tile = 256 if width % 256 == 0 else width
    for t in range(width // tile):
        cols = slice(t * tile, (t + 1) * tile)
        part = jnp.dot(att[...], wide[:, cols], preferred_element_type=jnp.float32)
        for i in range(groups):
            outs[i][:, cols] = part[i * rows : (i + 1) * rows].astype(outs[i].dtype)


def project(groups, members, att, width, pieces, places):
    rows = att.shape[0] // groups
    share = att.shape[1]
    return pl.pallas_call(
        functools.partial(project_kernel, groups, members, places),
        out_shape=[jax.ShapeDtypeStruct((rows, width), jnp.bfloat16)] * (groups - 1)
        + [jax.ShapeDtypeStruct((rows, width), jnp.float32)],
        in_specs=[VMEM] * (1 + len(pieces)),
        out_specs=[VMEM] * groups,
        scratch_shapes=[pltpu.VMEM((share, width), jnp.bfloat16)],
        compiler_params=pltpu.CompilerParams(vmem_limit_bytes=24 * 1024 * 1024),
        cost_estimate=pl.CostEstimate(
            flops=2 * groups * rows * share * width, bytes_accessed=2 * share * width, transcendentals=0
        ),
    )(att, *pieces)


def after(x, *others):
    if not others:
        return x
    return lax.optimization_barrier((x, *others))[0]


def per_device(parts, patch, query, key_new, value_new, key_stale, value_stale, exponents, w_out, gate):
    heads = exponents.shape[1] // 2
    rows, width = query.shape
    dim = width // heads
    groups = math.gcd(patch, heads)
    members = patch // groups
    share = width // groups
    depth, model = w_out.shape
    far = members // 2
    shared = parts % 2 == 0 and members == 4 and depth % 32 == 0
    first = model // 2

    def send(x, k, j):
        return lax.ppermute(x, "patch", [(p, ((p // members) ^ k) * members + (p % members) ^ j) for p in range(patch)])

    def swap(x):
        return lax.ppermute(x, "groups", [(g, g ^ 1) for g in range(parts)])

    def spread(pieces, bit):
        while bit:
            for j in list(pieces):
                pieces[j ^ bit] = send(pieces[j], 0, bit)
            bit //= 2
        return [pieces[j] for j in range(members)]

    own_query, fresh, w_part = prepare(
        groups, members, 2 if shared else 1, query, key_new, value_new, key_stale, value_stale, exponents.T, w_out
    )
    order = range(groups - 1, 0, -1)
    arrived = [send(fresh[k], k, 0) for k in order]
    both = jnp.concatenate([x[:, share:] for x in arrived] + [fresh[0]], axis=0)
    if shared:
        y_part = send(w_part, 0, 2)
        both = after(both, y_part)
    kvs = spread({0: both}, far)
    att, w_own = attend(groups, dim, arrived + [own_query], kvs, w_out)

    jobs = []
    if shared:
        w_core = send(after(w_out, both), 0, 1)
        y_core = send(after(y_part, both), 0, 1)
        x_part = swap(y_part)
        edges = (0, first, model)
        for left, right in zip(edges, edges[1:]):
            x_core = send(after(x_part, kvs[far])[:, left:right], 0, 1)
            pieces = [w_own, w_core, y_part, x_part, y_core, x_core]
            places = [(0, None, left), (1, None, left), (2, 0, left), (2, 1, left), (3, 0, left), (3, 1, 0)]
            jobs.append((right - left, pieces, places))
    else:
        spots = (lax.axis_index("patch") % members) ^ jnp.arange(members)
        jobs.append((model, [jnp.stack(spread({0: w_out}, far))[spots].reshape(-1, model)], [(None, None, 0)]))
    totals = []
    for width, pieces, places in jobs:
        sums = project(groups, members, att, width, pieces, places)
        att = after(att, *sums)
        total = sums[-1]
        for k, part in zip(order, sums):
            total = total + send(part, k, 0).astype(jnp.float32)
        totals.append(total)
    return (jnp.concatenate(totals, axis=1) * gate[None, :]).astype(jnp.bfloat16)


def solution(mesh):
    return jax.shard_map(
        functools.partial(per_device, mesh.shape["groups"], mesh.shape["patch"]),
        mesh=mesh,
        in_specs=(
            P(("groups", "patch"), None),
            P(("groups", "patch"), None),
            P(("groups", "patch"), None),
            P("groups", None),
            P("groups", None),
            P("groups", None),
            P("patch", None),
            P("groups"),
        ),
        out_specs=P(("groups", "patch"), None),
        check_vma=False,
    )
```

```python
import functools
import math

import jax
import jax.numpy as jnp
from jax import lax
from jax.experimental import pallas as pl
from jax.experimental.pallas import tpu as pltpu
from jax.sharding import PartitionSpec as P

CLIP_LIMIT = 2.0
VMEM = pl.BlockSpec(memory_space=pltpu.VMEM)
HBM = pl.BlockSpec(memory_space=pltpu.HBM)


def prepare_kernel(groups, members, *refs):
    sources = refs[:6]
    outs = refs[6:]
    qout, kvout, fulls = outs[0], outs[1], outs[1 : 1 + groups]
    query, key_new, value_new, kst, vst, est, packed, sems = outs[1 + groups :]
    rows, width = query.shape
    me = lax.axis_index("patch")
    first = pl.multiple_of((me // 2) * (2 * rows), 2 * rows)
    pair = pl.ds(first, 2 * rows)
    views = [sources[0], sources[1], sources[2], sources[3].at[pair], sources[4].at[pair], sources[5]]
    order = (5, 3, 1, 4, 2, 0)
    copies = {
        i: pltpu.make_async_copy(views[i], (query, key_new, value_new, kst, vst, est)[i], sems.at[i]) for i in order
    }
    for i in order:
        copies[i].start()
    heads = est.shape[0] // 2
    dim = width // heads
    share = width // groups
    odd = me % 2 == 1
    copies[5].wait()
    spot = lax.broadcasted_iota(jnp.int32, (rows, est.shape[1]), 1) == me * rows + lax.broadcasted_iota(
        jnp.int32, (rows, est.shape[1]), 0
    )
    powers = lax.dot_general(
        spot.astype(jnp.float32).astype(jnp.bfloat16),
        est[...].astype(jnp.float32).astype(jnp.bfloat16),
        (((1,), (1,)), ((), ())),
        preferred_element_type=jnp.float32,
    )
    scale = jnp.exp2(powers)
    inverse = jnp.exp2(-powers)
    for side, (fresh, stale) in enumerate(((key_new, kst), (value_new, vst))):
        copies[1 + side].wait()
        copies[3 + side].wait()
        for h in range(heads):
            cols = slice(h * dim, (h + 1) * dim)
            col = side * heads + h
            both = stale[:, cols].astype(jnp.float32)
            base = jnp.where(odd, both[rows:], both[:rows])
            resid = fresh[:, cols].astype(jnp.float32) - base
            codes = jnp.clip(resid * inverse[:, col : col + 1], -CLIP_LIMIT, CLIP_LIMIT)
            codes = codes.astype(jnp.bfloat16).astype(jnp.float32)
            at = side * share + (h * dim) % share
            packed[h * dim // share, :, at : at + dim] = (base + scale[:, col : col + 1] * codes).astype(jnp.bfloat16)
    copies[0].wait()
    for k in range(groups):
        target = (me // members) ^ k
        wanted = query[:, pl.ds(pl.multiple_of(target * share, share), share)]
        if k == 0:
            qout[...] = wanted
            kvout[...] = packed[target]
        else:
            fulls[k][:, :share] = wanted
            fulls[k][:, share:] = packed[target]


def prepare(groups, members, query, key_new, value_new, key_stale, value_stale, powers):
    rows, width = query.shape
    share = width // groups
    outs = (
        [((rows, share), jnp.bfloat16), ((rows, 2 * share), jnp.bfloat16)]
        + [((rows, 3 * share), jnp.bfloat16)] * (groups - 1)
    )
    sources = (query, key_new, value_new, key_stale, value_stale, powers)
    result = pl.pallas_call(
        functools.partial(prepare_kernel, groups, members),
        out_shape=[jax.ShapeDtypeStruct(*o) for o in outs],
        in_specs=[HBM] * 6,
        out_specs=[VMEM] * len(outs),
        scratch_shapes=[pltpu.VMEM((rows, width), jnp.bfloat16)] * 3
        + [pltpu.VMEM((2 * rows, width), jnp.bfloat16)] * 2
        + [
            pltpu.VMEM(powers.shape, jnp.int32),
            pltpu.VMEM((groups, rows, 2 * share), jnp.bfloat16),
            pltpu.SemaphoreType.DMA((6,)),
        ],
        compiler_params=pltpu.CompilerParams(vmem_limit_bytes=24 * 1024 * 1024),
        cost_estimate=pl.CostEstimate(
            flops=10 * rows * width, bytes_accessed=14 * rows * width, transcendentals=0
        ),
    )(*(pltpu.with_memory_space_constraint(x, pltpu.HBM) for x in sources))
    return result[0], result[1:]


def share_kernel(w_ref, out_ref, sems):
    size, model = out_ref.shape
    top = (lax.axis_index("groups") & 1) * size
    copies = []
    for i in range(sems.shape[0]):
        cols = pl.ds(i * (model // sems.shape[0]), model // sems.shape[0])
        source = w_ref.at[pl.ds(pl.multiple_of(top, size), size), cols]
        copies.append(pltpu.make_async_copy(source, out_ref.at[:, cols], sems.at[i]))
    for c in copies:
        c.start()
    for c in copies:
        c.wait()


def share_rows(w_out):
    depth, model = w_out.shape
    return pl.pallas_call(
        share_kernel,
        out_shape=jax.ShapeDtypeStruct((depth // 2, model), w_out.dtype),
        in_specs=[HBM],
        out_specs=VMEM,
        scratch_shapes=[pltpu.SemaphoreType.DMA((4,))],
        compiler_params=pltpu.CompilerParams(vmem_limit_bytes=24 * 1024 * 1024),
        cost_estimate=pl.CostEstimate(flops=0, bytes_accessed=2 * depth * model, transcendentals=0),
    )(pltpu.with_memory_space_constraint(w_out, pltpu.HBM))


def attend_kernel(groups, dim, *refs):
    queries = refs[:groups]
    kvs = refs[groups:-2]
    att, kv = refs[-2:]
    share = att.shape[1]
    block = kvs[0].shape[0]
    for j in range(len(kvs)):
        kv[j * block : (j + 1) * block] = kvs[j][...]
    query = jnp.concatenate([q[:, :share].astype(jnp.float32) for q in queries], axis=0).astype(jnp.bfloat16)
    inverse = 1.0 / dim**0.5
    for h in range(share // dim):
        cols = slice(h * dim, (h + 1) * dim)
        scores = (
            lax.dot_general(query[:, cols], kv[:, cols], (((1,), (1,)), ((), ())), preferred_element_type=jnp.float32)
            * inverse
        )
        peak = jnp.max(scores, axis=1, keepdims=True)
        expo = jnp.exp(scores - peak)
        total = jnp.sum(expo, axis=1, keepdims=True)
        numer = jnp.dot(
            expo.astype(jnp.bfloat16),
            kv[:, share + h * dim : share + (h + 1) * dim],
            preferred_element_type=jnp.float32,
        )
        att[:, cols] = (numer / total).astype(jnp.bfloat16)


def attend(groups, dim, queries, kvs):
    rows, share = queries[-1].shape
    block = kvs[0].shape[0]
    pieces = len(kvs)
    return pl.pallas_call(
        functools.partial(attend_kernel, groups, dim),
        out_shape=jax.ShapeDtypeStruct((groups * rows, share), jnp.bfloat16),
        in_specs=[VMEM] * (groups + pieces),
        out_specs=VMEM,
        scratch_shapes=[pltpu.VMEM((pieces * block, 2 * share), jnp.bfloat16)],
        compiler_params=pltpu.CompilerParams(vmem_limit_bytes=24 * 1024 * 1024),
        cost_estimate=pl.CostEstimate(
            flops=4 * groups * rows * pieces * block * share,
            bytes_accessed=4 * pieces * block * share,
            transcendentals=groups * rows * pieces * block * share // dim,
        ),
    )(*queries, *kvs)


def project_kernel(groups, members, places, att, *refs):
    ws = refs[: len(places)]
    outs = refs[len(places) : len(places) + groups]
    wide = refs[-1]
    rows, width = outs[0].shape
    q = lax.axis_index("patch") % members
    side = lax.axis_index("groups") & 1
    for piece, (j, flip, left) in zip(ws, places):
        size = piece.shape[0]
        row = 0
        if j is not None:
            row = (q ^ j) * (size if flip is None else 2 * size)
            if flip is not None:
                row = row + (side ^ flip) * size
            row = pl.multiple_of(row, size)
        wide[pl.ds(row, size), :] = piece[:, left : left + width]
    tile = 256 if width % 256 == 0 else width
    for t in range(width // tile):
        cols = slice(t * tile, (t + 1) * tile)
        part = jnp.dot(att[...], wide[:, cols], preferred_element_type=jnp.float32)
        for i in range(groups):
            outs[i][:, cols] = part[i * rows : (i + 1) * rows].astype(outs[i].dtype)


def project(groups, members, att, width, pieces, places):
    rows = att.shape[0] // groups
    share = att.shape[1]
    return pl.pallas_call(
        functools.partial(project_kernel, groups, members, places),
        out_shape=[jax.ShapeDtypeStruct((rows, width), jnp.bfloat16)] * (groups - 1)
        + [jax.ShapeDtypeStruct((rows, width), jnp.float32)],
        in_specs=[VMEM] * (1 + len(pieces)),
        out_specs=[VMEM] * groups,
        scratch_shapes=[pltpu.VMEM((share, width), jnp.bfloat16)],
        compiler_params=pltpu.CompilerParams(vmem_limit_bytes=24 * 1024 * 1024),
        cost_estimate=pl.CostEstimate(
            flops=2 * groups * rows * share * width, bytes_accessed=2 * share * width, transcendentals=0
        ),
    )(att, *pieces)


def after(x, *others):
    if not others:
        return x
    return lax.optimization_barrier((x, *others))[0]


def per_device(parts, patch, query, key_new, value_new, key_stale, value_stale, exponents, w_out, gate):
    heads = exponents.shape[1] // 2
    rows, width = query.shape
    dim = width // heads
    groups = math.gcd(patch, heads)
    members = patch // groups
    share = width // groups
    depth, model = w_out.shape
    far = members // 2
    shared = parts % 2 == 0 and members == 4 and depth % 32 == 0
    first = model // 2

    def send(x, k, j):
        return lax.ppermute(x, "patch", [(p, ((p // members) ^ k) * members + (p % members) ^ j) for p in range(patch)])

    def swap(x):
        return lax.ppermute(x, "groups", [(g, g ^ 1) for g in range(parts)])

    def spread(pieces, bit):
        while bit:
            for j in list(pieces):
                pieces[j ^ bit] = send(pieces[j], 0, bit)
            bit //= 2
        return [pieces[j] for j in range(members)]

    if shared:
        w_part = share_rows(w_out)
        y_part = send(w_part, 0, far)
    own_query, fresh = prepare(groups, members, query, key_new, value_new, key_stale, value_stale, exponents.T)
    w_own = w_out
    order = range(groups - 1, 0, -1)
    arrived = [send(fresh[k], k, 0) for k in order]
    both = jnp.concatenate([x[:, share:] for x in arrived] + [fresh[0]], axis=0)
    if shared:
        both = after(both, y_part)
    kvs = spread({0: both}, far)
    att = attend(groups, dim, arrived + [own_query], kvs)

    jobs = []
    if shared:
        w_core = send(after(w_own, both), 0, 1)
        y_core = send(after(y_part, both), 0, 1)
        x_part = swap(y_part)
        edges = (0, first, model)
        for left, right in zip(edges, edges[1:]):
            x_core = send(after(x_part, kvs[far])[:, left:right], 0, 1)
            pieces = [w_own, w_core, y_part, x_part, y_core, x_core]
            places = [(0, None, left), (1, None, left), (2, 0, left), (2, 1, left), (3, 0, left), (3, 1, 0)]
            jobs.append((right - left, pieces, places))
    else:
        spots = (lax.axis_index("patch") % members) ^ jnp.arange(members)
        jobs.append((model, [jnp.stack(spread({0: w_own}, far))[spots].reshape(-1, model)], [(None, None, 0)]))
    totals = []
    for width, pieces, places in jobs:
        sums = project(groups, members, att, width, pieces, places)
        att = after(att, *sums)
        total = sums[-1]
        for k, part in zip(order, sums):
            total = total + send(part, k, 0).astype(jnp.float32)
        totals.append(total)
    return (jnp.concatenate(totals, axis=1) * gate[None, :]).astype(jnp.bfloat16)


def solution(mesh):
    return jax.shard_map(
        functools.partial(per_device, mesh.shape["groups"], mesh.shape["patch"]),
        mesh=mesh,
        in_specs=(
            P(("groups", "patch"), None),
            P(("groups", "patch"), None),
            P(("groups", "patch"), None),
            P("groups", None),
            P("groups", None),
            P("groups", None),
            P("patch", None),
            P("groups"),
        ),
        out_specs=P(("groups", "patch"), None),
        check_vma=False,
    )
```

```python
import functools
import math

import jax
import jax.numpy as jnp
from jax import lax
from jax.experimental import pallas as pl
from jax.experimental.pallas import tpu as pltpu
from jax.sharding import PartitionSpec as P

CLIP_LIMIT = 2.0
VMEM = pl.BlockSpec(memory_space=pltpu.VMEM)
HBM = pl.BlockSpec(memory_space=pltpu.HBM)


def prepare_kernel(groups, members, *refs):
    sources = refs[:6]
    outs = refs[6:]
    qout, kvout, fulls = outs[0], outs[1], outs[1 : 1 + groups]
    query, key_new, value_new, kst, vst, est, packed, sems = outs[1 + groups :]
    rows, width = query.shape
    me = lax.axis_index("patch")
    first = pl.multiple_of((me // 2) * (2 * rows), 2 * rows)
    pair = pl.ds(first, 2 * rows)
    views = [sources[0], sources[1], sources[2], sources[3].at[pair], sources[4].at[pair], sources[5]]
    order = (5, 3, 1, 4, 2, 0)
    copies = {
        i: pltpu.make_async_copy(views[i], (query, key_new, value_new, kst, vst, est)[i], sems.at[i]) for i in order
    }
    for i in order:
        copies[i].start()
    heads = est.shape[0] // 2
    dim = width // heads
    share = width // groups
    odd = me % 2 == 1
    copies[5].wait()
    spot = lax.broadcasted_iota(jnp.int32, (rows, est.shape[1]), 1) == me * rows + lax.broadcasted_iota(
        jnp.int32, (rows, est.shape[1]), 0
    )
    powers = lax.dot_general(
        spot.astype(jnp.float32).astype(jnp.bfloat16),
        est[...].astype(jnp.float32).astype(jnp.bfloat16),
        (((1,), (1,)), ((), ())),
        preferred_element_type=jnp.float32,
    )
    scale = jnp.exp2(powers)
    inverse = jnp.exp2(-powers)
    for side, (fresh, stale) in enumerate(((key_new, kst), (value_new, vst))):
        copies[1 + side].wait()
        copies[3 + side].wait()
        for h in range(heads):
            cols = slice(h * dim, (h + 1) * dim)
            col = side * heads + h
            both = stale[:, cols].astype(jnp.float32)
            base = jnp.where(odd, both[rows:], both[:rows])
            resid = fresh[:, cols].astype(jnp.float32) - base
            codes = jnp.clip(resid * inverse[:, col : col + 1], -CLIP_LIMIT, CLIP_LIMIT)
            codes = codes.astype(jnp.bfloat16).astype(jnp.float32)
            at = side * share + (h * dim) % share
            packed[h * dim // share, :, at : at + dim] = (base + scale[:, col : col + 1] * codes).astype(jnp.bfloat16)
    copies[0].wait()
    for k in range(groups):
        target = (me // members) ^ k
        wanted = query[:, pl.ds(pl.multiple_of(target * share, share), share)]
        if k == 0:
            qout[...] = wanted
            kvout[...] = packed[target]
        else:
            fulls[k][:, :share] = wanted
            fulls[k][:, share:] = packed[target]


def prepare(groups, members, query, key_new, value_new, key_stale, value_stale, powers):
    rows, width = query.shape
    share = width // groups
    outs = (
        [((rows, share), jnp.bfloat16), ((rows, 2 * share), jnp.bfloat16)]
        + [((rows, 3 * share), jnp.bfloat16)] * (groups - 1)
    )
    sources = (query, key_new, value_new, key_stale, value_stale, powers)
    result = pl.pallas_call(
        functools.partial(prepare_kernel, groups, members),
        out_shape=[jax.ShapeDtypeStruct(*o) for o in outs],
        in_specs=[HBM] * 6,
        out_specs=[VMEM] * len(outs),
        scratch_shapes=[pltpu.VMEM((rows, width), jnp.bfloat16)] * 3
        + [pltpu.VMEM((2 * rows, width), jnp.bfloat16)] * 2
        + [
            pltpu.VMEM(powers.shape, jnp.int32),
            pltpu.VMEM((groups, rows, 2 * share), jnp.bfloat16),
            pltpu.SemaphoreType.DMA((6,)),
        ],
        compiler_params=pltpu.CompilerParams(vmem_limit_bytes=24 * 1024 * 1024),
        cost_estimate=pl.CostEstimate(
            flops=10 * rows * width, bytes_accessed=14 * rows * width, transcendentals=0
        ),
    )(*(pltpu.with_memory_space_constraint(x, pltpu.HBM) for x in sources))
    return result[0], result[1:]


def share_kernel(w_ref, out_ref, sems):
    size, model = out_ref.shape
    top = (lax.axis_index("groups") & 1) * size
    copies = []
    for i in range(sems.shape[0]):
        cols = pl.ds(i * (model // sems.shape[0]), model // sems.shape[0])
        source = w_ref.at[pl.ds(pl.multiple_of(top, size), size), cols]
        copies.append(pltpu.make_async_copy(source, out_ref.at[:, cols], sems.at[i]))
    for c in copies:
        c.start()
    for c in copies:
        c.wait()


def share_rows(w_out):
    depth, model = w_out.shape
    return pl.pallas_call(
        share_kernel,
        out_shape=jax.ShapeDtypeStruct((depth // 2, model), w_out.dtype),
        in_specs=[HBM],
        out_specs=VMEM,
        scratch_shapes=[pltpu.SemaphoreType.DMA((4,))],
        compiler_params=pltpu.CompilerParams(vmem_limit_bytes=24 * 1024 * 1024),
        cost_estimate=pl.CostEstimate(flops=0, bytes_accessed=2 * depth * model, transcendentals=0),
    )(pltpu.with_memory_space_constraint(w_out, pltpu.HBM))


def attend_kernel(groups, dim, *refs):
    queries = refs[:groups]
    kvs = refs[groups:-2]
    att, kv = refs[-2:]
    share = att.shape[1]
    block = kvs[0].shape[0]
    for j in range(len(kvs)):
        kv[j * block : (j + 1) * block] = kvs[j][...]
    query = jnp.concatenate([q[:, :share].astype(jnp.float32) for q in queries], axis=0).astype(jnp.bfloat16)
    inverse = 1.0 / dim**0.5
    for h in range(share // dim):
        cols = slice(h * dim, (h + 1) * dim)
        scores = (
            lax.dot_general(query[:, cols], kv[:, cols], (((1,), (1,)), ((), ())), preferred_element_type=jnp.float32)
            * inverse
        )
        peak = jnp.max(scores, axis=1, keepdims=True)
        expo = jnp.exp(scores - peak)
        total = jnp.sum(expo, axis=1, keepdims=True)
        numer = jnp.dot(
            expo.astype(jnp.bfloat16),
            kv[:, share + h * dim : share + (h + 1) * dim],
            preferred_element_type=jnp.float32,
        )
        att[:, cols] = (numer / total).astype(jnp.bfloat16)


def attend(groups, dim, queries, kvs):
    rows = queries[0].shape[0]
    share = min(q.shape[1] for q in queries)
    block = kvs[0].shape[0]
    pieces = len(kvs)
    return pl.pallas_call(
        functools.partial(attend_kernel, groups, dim),
        out_shape=jax.ShapeDtypeStruct((groups * rows, share), jnp.bfloat16),
        in_specs=[VMEM] * (groups + pieces),
        out_specs=VMEM,
        scratch_shapes=[pltpu.VMEM((pieces * block, 2 * share), jnp.bfloat16)],
        compiler_params=pltpu.CompilerParams(vmem_limit_bytes=24 * 1024 * 1024),
        cost_estimate=pl.CostEstimate(
            flops=4 * groups * rows * pieces * block * share,
            bytes_accessed=4 * pieces * block * share,
            transcendentals=groups * rows * pieces * block * share // dim,
        ),
    )(*queries, *kvs)


def project_kernel(members, places, att, *refs):
    ws = refs[: len(places)]
    outs = refs[len(places) : -1]
    wide = refs[-1]
    width = outs[0].shape[1]
    q = lax.axis_index("patch") % members
    side = lax.axis_index("groups") & 1
    for piece, (j, flip, left) in zip(ws, places):
        size = piece.shape[0]
        row = 0
        if j is not None:
            row = (q ^ j) * (size if flip is None else 2 * size)
            if flip is not None:
                row = row + (side ^ flip) * size
            row = pl.multiple_of(row, size)
        wide[pl.ds(row, size), :] = piece[:, left : left + width]
    tile = 256 if width % 256 == 0 else width
    for t in range(width // tile):
        cols = slice(t * tile, (t + 1) * tile)
        part = jnp.dot(att[...], wide[:, cols], preferred_element_type=jnp.float32)
        first = 0
        for out in outs:
            out[:, cols] = part[first : first + out.shape[0]].astype(out.dtype)
            first += out.shape[0]


def project(members, att, width, pieces, places, outs):
    share = att.shape[1]
    return pl.pallas_call(
        functools.partial(project_kernel, members, places),
        out_shape=[jax.ShapeDtypeStruct((count, width), kind) for count, kind in outs],
        in_specs=[VMEM] * (1 + len(pieces)),
        out_specs=[VMEM] * len(outs),
        scratch_shapes=[pltpu.VMEM((share, width), jnp.bfloat16)],
        compiler_params=pltpu.CompilerParams(vmem_limit_bytes=24 * 1024 * 1024),
        cost_estimate=pl.CostEstimate(
            flops=2 * att.shape[0] * share * width, bytes_accessed=2 * share * width, transcendentals=0
        ),
    )(att, *pieces)


def after(x, *others):
    if not others:
        return x
    return lax.optimization_barrier((x, *others))[0]


def per_device(parts, patch, query, key_new, value_new, key_stale, value_stale, exponents, w_out, gate):
    heads = exponents.shape[1] // 2
    rows, width = query.shape
    dim = width // heads
    groups = math.gcd(patch, heads)
    members = patch // groups
    share = width // groups
    depth, model = w_out.shape
    far = members // 2
    shared = parts % 2 == 0 and members == 4 and depth % 32 == 0
    first = model // 2

    def send(x, k, j):
        return lax.ppermute(x, "patch", [(p, ((p // members) ^ k) * members + (p % members) ^ j) for p in range(patch)])

    def swap(x):
        return lax.ppermute(x, "groups", [(g, g ^ 1) for g in range(parts)])

    def spread(pieces, bit):
        while bit:
            for j in list(pieces):
                pieces[j ^ bit] = send(pieces[j], 0, bit)
            bit //= 2
        return [pieces[j] for j in range(members)]

    if shared:
        w_part = share_rows(w_out)
        y_part = send(w_part, 0, far)
    own_query, fresh = prepare(groups, members, query, key_new, value_new, key_stale, value_stale, exponents.T)
    w_own = w_out
    order = range(groups - 1, 0, -1)
    arrived = [send(fresh[k], k, 0) for k in order]
    both = jnp.concatenate([x[:, share:] for x in arrived] + [fresh[0]], axis=0)
    if shared:
        both = after(both, y_part)
    kvs = spread({0: both}, far)
    blocks = dict(zip(order, arrived))
    blocks[0] = own_query
    line = [3, 1, 2, 0] if groups == 4 else [*order, 0]
    att = attend(groups, dim, [blocks[k] for k in line], kvs)

    jobs = []
    if shared:
        w_core = send(after(w_own, both), 0, 1)
        y_core = send(after(y_part, both), 0, 1)
        x_part = swap(y_part)
        edges = (0, first, model)
        for left, right in zip(edges, edges[1:]):
            x_core = send(after(x_part, kvs[far])[:, left:right], 0, 1)
            pieces = [w_own, w_core, y_part, x_part, y_core, x_core]
            places = [(0, None, left), (1, None, left), (2, 0, left), (2, 1, left), (3, 0, left), (3, 1, 0)]
            jobs.append((right - left, pieces, places))
    else:
        spots = (lax.axis_index("patch") % members) ^ jnp.arange(members)
        jobs.append((model, [jnp.stack(spread({0: w_own}, far))[spots].reshape(-1, model)], [(None, None, 0)]))
    half, full = jnp.bfloat16, jnp.float32

    def straight(att, width, pieces, places):
        sums = project(members, att, width, pieces, places, [(rows, half)] * (groups - 1) + [(rows, full)])
        total = sums[-1]
        taken = [send(part, k, 0) for k, part in sorted(zip(line, sums[:-1]), key=lambda x: -x[0])]
        for part in taken:
            total = total + part.astype(full)
        return sums, taken, total

    def paired(att, width, pieces, places):
        sums = project(members, att, width, pieces, places, [(2 * rows, half), (rows, full), (rows, full)])
        return sums, send(sums[0], 1, 0)

    def close(sums, near, gate_on):
        across = (sums[1] + near[:rows].astype(full)).astype(half)
        return sums[2] + near[rows:].astype(full) + send(after(across, *gate_on), 2, 0).astype(full)

    if len(jobs) == 2 and groups == 4:
        sums, near = paired(att, *jobs[0])
        _, taken, total = straight(after(att, *sums), *jobs[1])
        totals = [close(sums, near, []), total]
    else:
        totals = [straight(att, *job)[2] for job in jobs]
    return (jnp.concatenate(totals, axis=1) * gate[None, :]).astype(jnp.bfloat16)


def solution(mesh):
    return jax.shard_map(
        functools.partial(per_device, mesh.shape["groups"], mesh.shape["patch"]),
        mesh=mesh,
        in_specs=(
            P(("groups", "patch"), None),
            P(("groups", "patch"), None),
            P(("groups", "patch"), None),
            P("groups", None),
            P("groups", None),
            P("groups", None),
            P("patch", None),
            P("groups"),
        ),
        out_specs=P(("groups", "patch"), None),
        check_vma=False,
    )
```

```python
import functools
import math

import jax
import jax.numpy as jnp
from jax import lax
from jax.experimental import pallas as pl
from jax.experimental.pallas import tpu as pltpu
from jax.sharding import PartitionSpec as P

CLIP_LIMIT = 2.0
VMEM = pl.BlockSpec(memory_space=pltpu.VMEM)
HBM = pl.BlockSpec(memory_space=pltpu.HBM)


def prepare_kernel(groups, members, *refs):
    sources = refs[:6]
    outs = refs[6:]
    qout, kvout, fulls = outs[0], outs[1], outs[1 : 1 + groups]
    query, key_new, value_new, kst, vst, est, packed, sems = outs[1 + groups :]
    rows, width = query.shape
    me = lax.axis_index("patch")
    first = pl.multiple_of((me // 2) * (2 * rows), 2 * rows)
    pair = pl.ds(first, 2 * rows)
    views = [sources[0], sources[1], sources[2], sources[3].at[pair], sources[4].at[pair], sources[5]]
    order = (5, 3, 1, 4, 2, 0)
    copies = {
        i: pltpu.make_async_copy(views[i], (query, key_new, value_new, kst, vst, est)[i], sems.at[i]) for i in order
    }
    for i in order:
        copies[i].start()
    heads = est.shape[0] // 2
    dim = width // heads
    share = width // groups
    odd = me % 2 == 1
    copies[5].wait()
    spot = lax.broadcasted_iota(jnp.int32, (rows, est.shape[1]), 1) == me * rows + lax.broadcasted_iota(
        jnp.int32, (rows, est.shape[1]), 0
    )
    powers = lax.dot_general(
        spot.astype(jnp.float32).astype(jnp.bfloat16),
        est[...].astype(jnp.float32).astype(jnp.bfloat16),
        (((1,), (1,)), ((), ())),
        preferred_element_type=jnp.float32,
    )
    scale = jnp.exp2(powers)
    inverse = jnp.exp2(-powers)
    for side, (fresh, stale) in enumerate(((key_new, kst), (value_new, vst))):
        copies[1 + side].wait()
        copies[3 + side].wait()
        for h in range(heads):
            cols = slice(h * dim, (h + 1) * dim)
            col = side * heads + h
            both = stale[:, cols].astype(jnp.float32)
            base = jnp.where(odd, both[rows:], both[:rows])
            resid = fresh[:, cols].astype(jnp.float32) - base
            codes = jnp.clip(resid * inverse[:, col : col + 1], -CLIP_LIMIT, CLIP_LIMIT)
            codes = codes.astype(jnp.bfloat16).astype(jnp.float32)
            at = side * share + (h * dim) % share
            packed[h * dim // share, :, at : at + dim] = (base + scale[:, col : col + 1] * codes).astype(jnp.bfloat16)
    copies[0].wait()
    for k in range(groups):
        target = (me // members) ^ k
        wanted = query[:, pl.ds(pl.multiple_of(target * share, share), share)]
        if k == 0:
            qout[...] = wanted
            kvout[...] = packed[target]
        else:
            fulls[k][:, :share] = wanted
            fulls[k][:, share:] = packed[target]


def prepare(groups, members, query, key_new, value_new, key_stale, value_stale, powers):
    rows, width = query.shape
    share = width // groups
    outs = (
        [((rows, share), jnp.bfloat16), ((rows, 2 * share), jnp.bfloat16)]
        + [((rows, 3 * share), jnp.bfloat16)] * (groups - 1)
    )
    sources = (query, key_new, value_new, key_stale, value_stale, powers)
    result = pl.pallas_call(
        functools.partial(prepare_kernel, groups, members),
        out_shape=[jax.ShapeDtypeStruct(*o) for o in outs],
        in_specs=[HBM] * 6,
        out_specs=[VMEM] * len(outs),
        scratch_shapes=[pltpu.VMEM((rows, width), jnp.bfloat16)] * 3
        + [pltpu.VMEM((2 * rows, width), jnp.bfloat16)] * 2
        + [
            pltpu.VMEM(powers.shape, jnp.int32),
            pltpu.VMEM((groups, rows, 2 * share), jnp.bfloat16),
            pltpu.SemaphoreType.DMA((6,)),
        ],
        compiler_params=pltpu.CompilerParams(vmem_limit_bytes=24 * 1024 * 1024),
        cost_estimate=pl.CostEstimate(
            flops=10 * rows * width, bytes_accessed=14 * rows * width, transcendentals=0
        ),
    )(*(pltpu.with_memory_space_constraint(x, pltpu.HBM) for x in sources))
    return result[0], result[1:]


def share_kernel(w_ref, out_ref, sems):
    size, model = out_ref.shape
    top = (lax.axis_index("groups") & 1) * size
    copies = []
    for i in range(sems.shape[0]):
        cols = pl.ds(i * (model // sems.shape[0]), model // sems.shape[0])
        source = w_ref.at[pl.ds(pl.multiple_of(top, size), size), cols]
        copies.append(pltpu.make_async_copy(source, out_ref.at[:, cols], sems.at[i]))
    for c in copies:
        c.start()
    for c in copies:
        c.wait()


def share_rows(w_out):
    depth, model = w_out.shape
    return pl.pallas_call(
        share_kernel,
        out_shape=jax.ShapeDtypeStruct((depth // 2, model), w_out.dtype),
        in_specs=[HBM],
        out_specs=VMEM,
        scratch_shapes=[pltpu.SemaphoreType.DMA((4,))],
        compiler_params=pltpu.CompilerParams(vmem_limit_bytes=24 * 1024 * 1024),
        cost_estimate=pl.CostEstimate(flops=0, bytes_accessed=2 * depth * model, transcendentals=0),
    )(pltpu.with_memory_space_constraint(w_out, pltpu.HBM))


def attend_kernel(groups, dim, *refs):
    queries = refs[:groups]
    kvs = refs[groups:-2]
    att, kv = refs[-2:]
    share = att.shape[1]
    block = kvs[0].shape[0]
    for j in range(len(kvs)):
        kv[j * block : (j + 1) * block] = kvs[j][...]
    query = jnp.concatenate([q[:, :share].astype(jnp.float32) for q in queries], axis=0).astype(jnp.bfloat16)
    inverse = 1.0 / dim**0.5
    for h in range(share // dim):
        cols = slice(h * dim, (h + 1) * dim)
        scores = (
            lax.dot_general(query[:, cols], kv[:, cols], (((1,), (1,)), ((), ())), preferred_element_type=jnp.float32)
            * inverse
        )
        peak = jnp.max(scores, axis=1, keepdims=True)
        expo = jnp.exp(scores - peak)
        total = jnp.sum(expo, axis=1, keepdims=True)
        numer = jnp.dot(
            expo.astype(jnp.bfloat16),
            kv[:, share + h * dim : share + (h + 1) * dim],
            preferred_element_type=jnp.float32,
        )
        att[:, cols] = (numer / total).astype(jnp.bfloat16)


def attend(groups, dim, queries, kvs):
    rows = queries[0].shape[0]
    share = min(q.shape[1] for q in queries)
    block = kvs[0].shape[0]
    pieces = len(kvs)
    return pl.pallas_call(
        functools.partial(attend_kernel, groups, dim),
        out_shape=jax.ShapeDtypeStruct((groups * rows, share), jnp.bfloat16),
        in_specs=[VMEM] * (groups + pieces),
        out_specs=VMEM,
        scratch_shapes=[pltpu.VMEM((pieces * block, 2 * share), jnp.bfloat16)],
        compiler_params=pltpu.CompilerParams(vmem_limit_bytes=24 * 1024 * 1024),
        cost_estimate=pl.CostEstimate(
            flops=4 * groups * rows * pieces * block * share,
            bytes_accessed=4 * pieces * block * share,
            transcendentals=groups * rows * pieces * block * share // dim,
        ),
    )(*queries, *kvs)


def project_kernel(members, places, att, *refs):
    ws = refs[: len(places)]
    outs = refs[len(places) : -1]
    wide = refs[-1]
    width = outs[0].shape[1]
    q = lax.axis_index("patch") % members
    side = lax.axis_index("groups") & 1
    for piece, (j, flip, left) in zip(ws, places):
        size = piece.shape[0]
        row = 0
        if j is not None:
            row = (q ^ j) * (size if flip is None else 2 * size)
            if flip is not None:
                row = row + (side ^ flip) * size
            row = pl.multiple_of(row, size)
        wide[pl.ds(row, size), :] = piece[:, left : left + width]
    tile = 256 if width % 256 == 0 else width
    for t in range(width // tile):
        cols = slice(t * tile, (t + 1) * tile)
        part = jnp.dot(att[...], wide[:, cols], preferred_element_type=jnp.float32)
        first = 0
        for out in outs:
            out[:, cols] = part[first : first + out.shape[0]].astype(out.dtype)
            first += out.shape[0]


def project(members, att, width, pieces, places, outs):
    share = att.shape[1]
    return pl.pallas_call(
        functools.partial(project_kernel, members, places),
        out_shape=[jax.ShapeDtypeStruct((count, width), kind) for count, kind in outs],
        in_specs=[VMEM] * (1 + len(pieces)),
        out_specs=[VMEM] * len(outs),
        scratch_shapes=[pltpu.VMEM((share, width), jnp.bfloat16)],
        compiler_params=pltpu.CompilerParams(vmem_limit_bytes=24 * 1024 * 1024),
        cost_estimate=pl.CostEstimate(
            flops=2 * att.shape[0] * share * width, bytes_accessed=2 * share * width, transcendentals=0
        ),
    )(att, *pieces)


def after(x, *others):
    if not others:
        return x
    return lax.optimization_barrier((x, *others))[0]


def per_device(parts, patch, query, key_new, value_new, key_stale, value_stale, exponents, w_out, gate):
    heads = exponents.shape[1] // 2
    rows, width = query.shape
    dim = width // heads
    groups = math.gcd(patch, heads)
    members = patch // groups
    share = width // groups
    depth, model = w_out.shape
    far = members // 2
    shared = parts % 2 == 0 and members == 4 and depth % 32 == 0
    first = model * 2 // 3 // 256 * 256

    def send(x, k, j):
        return lax.ppermute(x, "patch", [(p, ((p // members) ^ k) * members + (p % members) ^ j) for p in range(patch)])

    def swap(x):
        return lax.ppermute(x, "groups", [(g, g ^ 1) for g in range(parts)])

    def spread(pieces, bit):
        while bit:
            for j in list(pieces):
                pieces[j ^ bit] = send(pieces[j], 0, bit)
            bit //= 2
        return [pieces[j] for j in range(members)]

    if shared:
        w_part = share_rows(w_out)
        y_part = send(w_part, 0, far)
    own_query, fresh = prepare(groups, members, query, key_new, value_new, key_stale, value_stale, exponents.T)
    w_own = w_out
    order = range(groups - 1, 0, -1)
    arrived = [send(fresh[k], k, 0) for k in order]
    both = jnp.concatenate([x[:, share:] for x in arrived] + [fresh[0]], axis=0)
    if shared:
        both = after(both, y_part)
    kvs = spread({0: both}, far)
    blocks = dict(zip(order, arrived))
    blocks[0] = own_query
    line = [3, 1, 2, 0] if groups == 4 else [*order, 0]
    att = attend(groups, dim, [blocks[k] for k in line], kvs)

    jobs = []
    if shared:
        w_core = send(after(w_own, both), 0, 1)
        y_core = send(after(y_part, both), 0, 1)
        x_part = swap(y_part)
        x_core = send(after(x_part, *kvs), 0, 1)
        edges = (0, first, model)
        for left, right in zip(edges, edges[1:]):
            pieces = [w_own, w_core, y_part, x_part, y_core, x_core]
            places = [(0, None, left), (1, None, left), (2, 0, left), (2, 1, left), (3, 0, left), (3, 1, left)]
            jobs.append((right - left, pieces, places))
    else:
        spots = (lax.axis_index("patch") % members) ^ jnp.arange(members)
        jobs.append((model, [jnp.stack(spread({0: w_own}, far))[spots].reshape(-1, model)], [(None, None, 0)]))
    half, full = jnp.bfloat16, jnp.float32

    def straight(att, width, pieces, places):
        sums = project(members, att, width, pieces, places, [(rows, half)] * (groups - 1) + [(rows, full)])
        total = sums[-1]
        taken = [send(part, k, 0) for k, part in sorted(zip(line, sums[:-1]), key=lambda x: -x[0])]
        for part in taken:
            total = total + part.astype(full)
        return sums, taken, total

    def paired(att, width, pieces, places):
        sums = project(members, att, width, pieces, places, [(2 * rows, half), (rows, full), (rows, full)])
        return sums, send(sums[0], 1, 0)

    def close(sums, near, gate_on):
        across = (sums[1] + near[:rows].astype(full)).astype(half)
        return sums[2] + near[rows:].astype(full) + send(after(across, *gate_on), 2, 0).astype(full)

    if len(jobs) == 2 and groups == 4:
        sums, near = paired(att, *jobs[0])
        _, taken, total = straight(after(att, *sums), *jobs[1])
        totals = [close(sums, near, []), total]
    else:
        totals = [straight(att, *job)[2] for job in jobs]
    return (jnp.concatenate(totals, axis=1) * gate[None, :]).astype(jnp.bfloat16)


def solution(mesh):
    return jax.shard_map(
        functools.partial(per_device, mesh.shape["groups"], mesh.shape["patch"]),
        mesh=mesh,
        in_specs=(
            P(("groups", "patch"), None),
            P(("groups", "patch"), None),
            P(("groups", "patch"), None),
            P("groups", None),
            P("groups", None),
            P("groups", None),
            P("patch", None),
            P("groups"),
        ),
        out_specs=P(("groups", "patch"), None),
        check_vma=False,
    )
```

```python
import functools
import math

import jax
import jax.numpy as jnp
from jax import lax
from jax.experimental import pallas as pl
from jax.experimental.pallas import tpu as pltpu
from jax.sharding import PartitionSpec as P

CLIP_LIMIT = 2.0
VMEM = pl.BlockSpec(memory_space=pltpu.VMEM)
HBM = pl.BlockSpec(memory_space=pltpu.HBM)


def prepare_kernel(groups, members, *refs):
    sources = refs[:6]
    outs = refs[6:]
    qout, kvout, fulls = outs[0], outs[1], outs[1 : 1 + groups]
    query, key_new, value_new, kst, vst, est, packed, sems = outs[1 + groups :]
    rows, width = query.shape
    me = lax.axis_index("patch")
    first = pl.multiple_of((me // 2) * (2 * rows), 2 * rows)
    pair = pl.ds(first, 2 * rows)
    views = [sources[0], sources[1], sources[2], sources[3].at[pair], sources[4].at[pair], sources[5]]
    order = (5, 3, 1, 4, 2, 0)
    copies = {
        i: pltpu.make_async_copy(views[i], (query, key_new, value_new, kst, vst, est)[i], sems.at[i]) for i in order
    }
    for i in order:
        copies[i].start()
    heads = est.shape[0] // 2
    dim = width // heads
    share = width // groups
    odd = me % 2 == 1
    copies[5].wait()
    spot = lax.broadcasted_iota(jnp.int32, (rows, est.shape[1]), 1) == me * rows + lax.broadcasted_iota(
        jnp.int32, (rows, est.shape[1]), 0
    )
    powers = lax.dot_general(
        spot.astype(jnp.float32).astype(jnp.bfloat16),
        est[...].astype(jnp.float32).astype(jnp.bfloat16),
        (((1,), (1,)), ((), ())),
        preferred_element_type=jnp.float32,
    )
    scale = jnp.exp2(powers)
    inverse = jnp.exp2(-powers)
    for side, (fresh, stale) in enumerate(((key_new, kst), (value_new, vst))):
        copies[1 + side].wait()
        copies[3 + side].wait()
        for h in range(heads):
            cols = slice(h * dim, (h + 1) * dim)
            col = side * heads + h
            both = stale[:, cols].astype(jnp.float32)
            base = jnp.where(odd, both[rows:], both[:rows])
            resid = fresh[:, cols].astype(jnp.float32) - base
            codes = jnp.clip(resid * inverse[:, col : col + 1], -CLIP_LIMIT, CLIP_LIMIT)
            codes = codes.astype(jnp.bfloat16).astype(jnp.float32)
            at = side * share + (h * dim) % share
            packed[h * dim // share, :, at : at + dim] = (base + scale[:, col : col + 1] * codes).astype(jnp.bfloat16)
    copies[0].wait()
    for k in range(groups):
        target = (me // members) ^ k
        wanted = query[:, pl.ds(pl.multiple_of(target * share, share), share)]
        if k == 0:
            qout[...] = wanted
            kvout[...] = packed[target]
        else:
            fulls[k][:, :share] = wanted
            fulls[k][:, share:] = packed[target]


def prepare(groups, members, query, key_new, value_new, key_stale, value_stale, powers):
    rows, width = query.shape
    share = width // groups
    outs = (
        [((rows, share), jnp.bfloat16), ((rows, 2 * share), jnp.bfloat16)]
        + [((rows, 3 * share), jnp.bfloat16)] * (groups - 1)
    )
    sources = (query, key_new, value_new, key_stale, value_stale, powers)
    result = pl.pallas_call(
        functools.partial(prepare_kernel, groups, members),
        out_shape=[jax.ShapeDtypeStruct(*o) for o in outs],
        in_specs=[HBM] * 6,
        out_specs=[VMEM] * len(outs),
        scratch_shapes=[pltpu.VMEM((rows, width), jnp.bfloat16)] * 3
        + [pltpu.VMEM((2 * rows, width), jnp.bfloat16)] * 2
        + [
            pltpu.VMEM(powers.shape, jnp.int32),
            pltpu.VMEM((groups, rows, 2 * share), jnp.bfloat16),
            pltpu.SemaphoreType.DMA((6,)),
        ],
        compiler_params=pltpu.CompilerParams(vmem_limit_bytes=24 * 1024 * 1024),
        cost_estimate=pl.CostEstimate(
            flops=10 * rows * width, bytes_accessed=14 * rows * width, transcendentals=0
        ),
    )(*(pltpu.with_memory_space_constraint(x, pltpu.HBM) for x in sources))
    return result[0], result[1:]


def share_kernel(w_ref, out_ref, sems):
    size, model = out_ref.shape
    top = (lax.axis_index("groups") & 1) * size
    copies = []
    for i in range(sems.shape[0]):
        cols = pl.ds(i * (model // sems.shape[0]), model // sems.shape[0])
        source = w_ref.at[pl.ds(pl.multiple_of(top, size), size), cols]
        copies.append(pltpu.make_async_copy(source, out_ref.at[:, cols], sems.at[i]))
    for c in copies:
        c.start()
    for c in copies:
        c.wait()


def share_rows(w_out):
    depth, model = w_out.shape
    return pl.pallas_call(
        share_kernel,
        out_shape=jax.ShapeDtypeStruct((depth // 2, model), w_out.dtype),
        in_specs=[HBM],
        out_specs=VMEM,
        scratch_shapes=[pltpu.SemaphoreType.DMA((4,))],
        compiler_params=pltpu.CompilerParams(vmem_limit_bytes=24 * 1024 * 1024),
        cost_estimate=pl.CostEstimate(flops=0, bytes_accessed=2 * depth * model, transcendentals=0),
    )(pltpu.with_memory_space_constraint(w_out, pltpu.HBM))


def attend_kernel(groups, dim, *refs):
    queries = refs[:groups]
    kvs = refs[groups:-2]
    att, kv = refs[-2:]
    share = att.shape[1]
    block = kvs[0].shape[0]
    for j in range(len(kvs)):
        kv[j * block : (j + 1) * block] = kvs[j][...]
    query = jnp.concatenate([q[:, :share].astype(jnp.float32) for q in queries], axis=0).astype(jnp.bfloat16)
    inverse = 1.0 / dim**0.5
    for h in range(share // dim):
        cols = slice(h * dim, (h + 1) * dim)
        scores = (
            lax.dot_general(query[:, cols], kv[:, cols], (((1,), (1,)), ((), ())), preferred_element_type=jnp.float32)
            * inverse
        )
        peak = jnp.max(scores, axis=1, keepdims=True)
        expo = jnp.exp(scores - peak)
        total = jnp.sum(expo, axis=1, keepdims=True)
        numer = jnp.dot(
            expo.astype(jnp.bfloat16),
            kv[:, share + h * dim : share + (h + 1) * dim],
            preferred_element_type=jnp.float32,
        )
        att[:, cols] = (numer / total).astype(jnp.bfloat16)


def attend(groups, dim, queries, kvs):
    rows = queries[0].shape[0]
    share = min(q.shape[1] for q in queries)
    block = kvs[0].shape[0]
    pieces = len(kvs)
    return pl.pallas_call(
        functools.partial(attend_kernel, groups, dim),
        out_shape=jax.ShapeDtypeStruct((groups * rows, share), jnp.bfloat16),
        in_specs=[VMEM] * (groups + pieces),
        out_specs=VMEM,
        scratch_shapes=[pltpu.VMEM((pieces * block, 2 * share), jnp.bfloat16)],
        compiler_params=pltpu.CompilerParams(vmem_limit_bytes=24 * 1024 * 1024),
        cost_estimate=pl.CostEstimate(
            flops=4 * groups * rows * pieces * block * share,
            bytes_accessed=4 * pieces * block * share,
            transcendentals=groups * rows * pieces * block * share // dim,
        ),
    )(*queries, *kvs)


def project_kernel(members, places, att, *refs):
    ws = refs[: len(places)]
    outs = refs[len(places) : -1]
    wide = refs[-1]
    width = outs[0].shape[1]
    q = lax.axis_index("patch") % members
    side = lax.axis_index("groups") & 1
    for piece, (j, flip, left) in zip(ws, places):
        size = piece.shape[0]
        row = 0
        if j is not None:
            row = (q ^ j) * (size if flip is None else 2 * size)
            if flip is not None:
                row = row + (side ^ flip) * size
            row = pl.multiple_of(row, size)
        wide[pl.ds(row, size), :] = piece[:, left : left + width]
    tile = 256 if width % 256 == 0 else width
    for t in range(width // tile):
        cols = slice(t * tile, (t + 1) * tile)
        part = jnp.dot(att[...], wide[:, cols], preferred_element_type=jnp.float32)
        first = 0
        for out in outs:
            out[:, cols] = part[first : first + out.shape[0]].astype(out.dtype)
            first += out.shape[0]


def project(members, att, width, pieces, places, outs):
    share = att.shape[1]
    return pl.pallas_call(
        functools.partial(project_kernel, members, places),
        out_shape=[jax.ShapeDtypeStruct((count, width), kind) for count, kind in outs],
        in_specs=[VMEM] * (1 + len(pieces)),
        out_specs=[VMEM] * len(outs),
        scratch_shapes=[pltpu.VMEM((share, width), jnp.bfloat16)],
        compiler_params=pltpu.CompilerParams(vmem_limit_bytes=24 * 1024 * 1024),
        cost_estimate=pl.CostEstimate(
            flops=2 * att.shape[0] * share * width, bytes_accessed=2 * share * width, transcendentals=0
        ),
    )(att, *pieces)


def after(x, *others):
    if not others:
        return x
    return lax.optimization_barrier((x, *others))[0]


def per_device(parts, patch, query, key_new, value_new, key_stale, value_stale, exponents, w_out, gate):
    heads = exponents.shape[1] // 2
    rows, width = query.shape
    dim = width // heads
    groups = math.gcd(patch, heads)
    members = patch // groups
    share = width // groups
    depth, model = w_out.shape
    far = members // 2
    shared = parts % 2 == 0 and members == 4 and depth % 32 == 0
    first = model // 2

    def send(x, k, j):
        return lax.ppermute(x, "patch", [(p, ((p // members) ^ k) * members + (p % members) ^ j) for p in range(patch)])

    def swap(x):
        return lax.ppermute(x, "groups", [(g, g ^ 1) for g in range(parts)])

    def spread(pieces, bit):
        while bit:
            for j in list(pieces):
                pieces[j ^ bit] = send(pieces[j], 0, bit)
            bit //= 2
        return [pieces[j] for j in range(members)]

    if shared:
        w_part = share_rows(w_out)
        y_part = send(w_part, 0, far)
    own_query, fresh = prepare(groups, members, query, key_new, value_new, key_stale, value_stale, exponents.T)
    w_own = w_out
    order = range(groups - 1, 0, -1)
    arrived = [send(fresh[k], k, 0) for k in order]
    both = jnp.concatenate([x[:, share:] for x in arrived] + [fresh[0]], axis=0)
    if shared:
        both = after(both, y_part)
    kvs = spread({0: both}, far)
    blocks = dict(zip(order, arrived))
    blocks[0] = own_query
    line = [3, 1, 2, 0] if groups == 4 else [*order, 0]
    att = attend(groups, dim, [blocks[k] for k in line], kvs)

    jobs = []
    if shared:
        w_core = send(after(w_own, both), 0, 1)
        y_core = send(after(y_part, both), 0, 1)
        x_part = swap(y_part)
        x_core = send(after(x_part, kvs[far]), 0, 1)
        edges = (0, first, model)
        for left, right in zip(edges, edges[1:]):
            pieces = [w_own, w_core, y_part, x_part, y_core, x_core]
            places = [(0, None, left), (1, None, left), (2, 0, left), (2, 1, left), (3, 0, left), (3, 1, left)]
            jobs.append((right - left, pieces, places))
    else:
        spots = (lax.axis_index("patch") % members) ^ jnp.arange(members)
        jobs.append((model, [jnp.stack(spread({0: w_own}, far))[spots].reshape(-1, model)], [(None, None, 0)]))
    half, full = jnp.bfloat16, jnp.float32

    def straight(att, width, pieces, places):
        sums = project(members, att, width, pieces, places, [(rows, half)] * (groups - 1) + [(rows, full)])
        total = sums[-1]
        taken = [send(part, k, 0) for k, part in sorted(zip(line, sums[:-1]), key=lambda x: -x[0])]
        for part in taken:
            total = total + part.astype(full)
        return sums, taken, total

    def paired(att, width, pieces, places):
        sums = project(members, att, width, pieces, places, [(2 * rows, half), (rows, full), (rows, full)])
        return sums, send(sums[0], 1, 0)

    def close(sums, near, gate_on):
        across = (sums[1] + near[:rows].astype(full)).astype(half)
        return sums[2] + near[rows:].astype(full) + send(after(across, *gate_on), 2, 0).astype(full)

    if len(jobs) == 2 and groups == 4:
        sums, near = paired(att, *jobs[0])
        _, taken, total = straight(after(att, *sums), *jobs[1])
        totals = [close(sums, near, []), total]
    else:
        totals = [straight(att, *job)[2] for job in jobs]
    return (jnp.concatenate(totals, axis=1) * gate[None, :]).astype(jnp.bfloat16)


def solution(mesh):
    return jax.shard_map(
        functools.partial(per_device, mesh.shape["groups"], mesh.shape["patch"]),
        mesh=mesh,
        in_specs=(
            P(("groups", "patch"), None),
            P(("groups", "patch"), None),
            P(("groups", "patch"), None),
            P("groups", None),
            P("groups", None),
            P("groups", None),
            P("patch", None),
            P("groups"),
        ),
        out_specs=P(("groups", "patch"), None),
        check_vma=False,
    )
```

```python
import functools
import math

import jax
import jax.numpy as jnp
from jax import lax
from jax.experimental import pallas as pl
from jax.experimental.pallas import tpu as pltpu
from jax.sharding import PartitionSpec as P

CLIP_LIMIT = 2.0
VMEM = pl.BlockSpec(memory_space=pltpu.VMEM)
HBM = pl.BlockSpec(memory_space=pltpu.HBM)


def prepare_kernel(groups, members, *refs):
    sources = refs[:6]
    outs = refs[6:]
    qout, kvout, fulls = outs[0], outs[1], outs[1 : 1 + groups]
    query, key_new, value_new, kst, vst, est, packed, sems = outs[1 + groups :]
    rows, width = query.shape
    me = lax.axis_index("patch")
    first = pl.multiple_of((me // 2) * (2 * rows), 2 * rows)
    pair = pl.ds(first, 2 * rows)
    views = [sources[0], sources[1], sources[2], sources[3].at[pair], sources[4].at[pair], sources[5]]
    order = (5, 3, 1, 4, 2, 0)
    copies = {
        i: pltpu.make_async_copy(views[i], (query, key_new, value_new, kst, vst, est)[i], sems.at[i]) for i in order
    }
    for i in order:
        copies[i].start()
    heads = est.shape[0] // 2
    dim = width // heads
    share = width // groups
    odd = me % 2 == 1
    copies[5].wait()
    spot = lax.broadcasted_iota(jnp.int32, (rows, est.shape[1]), 1) == me * rows + lax.broadcasted_iota(
        jnp.int32, (rows, est.shape[1]), 0
    )
    powers = lax.dot_general(
        spot.astype(jnp.float32).astype(jnp.bfloat16),
        est[...].astype(jnp.float32).astype(jnp.bfloat16),
        (((1,), (1,)), ((), ())),
        preferred_element_type=jnp.float32,
    )
    scale = jnp.exp2(powers)
    inverse = jnp.exp2(-powers)
    for side, (fresh, stale) in enumerate(((key_new, kst), (value_new, vst))):
        copies[1 + side].wait()
        copies[3 + side].wait()
        for h in range(heads):
            cols = slice(h * dim, (h + 1) * dim)
            col = side * heads + h
            both = stale[:, cols].astype(jnp.float32)
            base = jnp.where(odd, both[rows:], both[:rows])
            resid = fresh[:, cols].astype(jnp.float32) - base
            codes = jnp.clip(resid * inverse[:, col : col + 1], -CLIP_LIMIT, CLIP_LIMIT)
            codes = codes.astype(jnp.bfloat16).astype(jnp.float32)
            at = side * share + (h * dim) % share
            packed[h * dim // share, :, at : at + dim] = (base + scale[:, col : col + 1] * codes).astype(jnp.bfloat16)
    copies[0].wait()
    for k in range(groups):
        target = (me // members) ^ k
        wanted = query[:, pl.ds(pl.multiple_of(target * share, share), share)]
        if k == 0:
            qout[...] = wanted
            kvout[...] = packed[target]
        else:
            fulls[k][:, :share] = wanted
            fulls[k][:, share:] = packed[target]


def prepare(groups, members, query, key_new, value_new, key_stale, value_stale, powers):
    rows, width = query.shape
    share = width // groups
    outs = (
        [((rows, share), jnp.bfloat16), ((rows, 2 * share), jnp.bfloat16)]
        + [((rows, 3 * share), jnp.bfloat16)] * (groups - 1)
    )
    sources = (query, key_new, value_new, key_stale, value_stale, powers)
    result = pl.pallas_call(
        functools.partial(prepare_kernel, groups, members),
        out_shape=[jax.ShapeDtypeStruct(*o) for o in outs],
        in_specs=[HBM] * 6,
        out_specs=[VMEM] * len(outs),
        scratch_shapes=[pltpu.VMEM((rows, width), jnp.bfloat16)] * 3
        + [pltpu.VMEM((2 * rows, width), jnp.bfloat16)] * 2
        + [
            pltpu.VMEM(powers.shape, jnp.int32),
            pltpu.VMEM((groups, rows, 2 * share), jnp.bfloat16),
            pltpu.SemaphoreType.DMA((6,)),
        ],
        compiler_params=pltpu.CompilerParams(vmem_limit_bytes=24 * 1024 * 1024),
        cost_estimate=pl.CostEstimate(
            flops=10 * rows * width, bytes_accessed=14 * rows * width, transcendentals=0
        ),
    )(*(pltpu.with_memory_space_constraint(x, pltpu.HBM) for x in sources))
    return result[0], result[1:]


def share_kernel(w_ref, out_ref, sems):
    size, model = out_ref.shape
    top = (lax.axis_index("groups") & 1) * size
    copies = []
    for i in range(sems.shape[0]):
        cols = pl.ds(i * (model // sems.shape[0]), model // sems.shape[0])
        source = w_ref.at[pl.ds(pl.multiple_of(top, size), size), cols]
        copies.append(pltpu.make_async_copy(source, out_ref.at[:, cols], sems.at[i]))
    for c in copies:
        c.start()
    for c in copies:
        c.wait()


def share_rows(w_out):
    depth, model = w_out.shape
    return pl.pallas_call(
        share_kernel,
        out_shape=jax.ShapeDtypeStruct((depth // 2, model), w_out.dtype),
        in_specs=[HBM],
        out_specs=VMEM,
        scratch_shapes=[pltpu.SemaphoreType.DMA((4,))],
        compiler_params=pltpu.CompilerParams(vmem_limit_bytes=24 * 1024 * 1024),
        cost_estimate=pl.CostEstimate(flops=0, bytes_accessed=2 * depth * model, transcendentals=0),
    )(pltpu.with_memory_space_constraint(w_out, pltpu.HBM))


def attend_kernel(groups, dim, *refs):
    queries = refs[:groups]
    kvs = refs[groups:-2]
    att, kv = refs[-2:]
    share = att.shape[1]
    block = kvs[0].shape[0]
    for j in range(len(kvs)):
        kv[j * block : (j + 1) * block] = kvs[j][...]
    query = jnp.concatenate([q[:, :share].astype(jnp.float32) for q in queries], axis=0).astype(jnp.bfloat16)
    inverse = 1.0 / dim**0.5
    for h in range(share // dim):
        cols = slice(h * dim, (h + 1) * dim)
        scores = (
            lax.dot_general(query[:, cols], kv[:, cols], (((1,), (1,)), ((), ())), preferred_element_type=jnp.float32)
            * inverse
        )
        peak = jnp.max(scores, axis=1, keepdims=True)
        expo = jnp.exp(scores - peak)
        total = jnp.sum(expo, axis=1, keepdims=True)
        numer = jnp.dot(
            expo.astype(jnp.bfloat16),
            kv[:, share + h * dim : share + (h + 1) * dim],
            preferred_element_type=jnp.float32,
        )
        att[:, cols] = (numer / total).astype(jnp.bfloat16)


def attend(groups, dim, queries, kvs):
    rows = queries[0].shape[0]
    share = min(q.shape[1] for q in queries)
    block = kvs[0].shape[0]
    pieces = len(kvs)
    return pl.pallas_call(
        functools.partial(attend_kernel, groups, dim),
        out_shape=jax.ShapeDtypeStruct((groups * rows, share), jnp.bfloat16),
        in_specs=[VMEM] * (groups + pieces),
        out_specs=VMEM,
        scratch_shapes=[pltpu.VMEM((pieces * block, 2 * share), jnp.bfloat16)],
        compiler_params=pltpu.CompilerParams(vmem_limit_bytes=24 * 1024 * 1024),
        cost_estimate=pl.CostEstimate(
            flops=4 * groups * rows * pieces * block * share,
            bytes_accessed=4 * pieces * block * share,
            transcendentals=groups * rows * pieces * block * share // dim,
        ),
    )(*queries, *kvs)


def project_kernel(members, places, att, *refs):
    ws = refs[: len(places)]
    outs = refs[len(places) : -1]
    wide = refs[-1]
    width = outs[0].shape[1]
    q = lax.axis_index("patch") % members
    side = lax.axis_index("groups") & 1
    for piece, (j, flip, left) in zip(ws, places):
        size = piece.shape[0]
        row = 0
        if j is not None:
            row = (q ^ j) * (size if flip is None else 2 * size)
            if flip is not None:
                row = row + (side ^ flip) * size
            row = pl.multiple_of(row, size)
        wide[pl.ds(row, size), :] = piece[:, left : left + width]
    tile = 256 if width % 256 == 0 else width
    for t in range(width // tile):
        cols = slice(t * tile, (t + 1) * tile)
        part = jnp.dot(att[...], wide[:, cols], preferred_element_type=jnp.float32)
        first = 0
        for out in outs:
            out[:, cols] = part[first : first + out.shape[0]].astype(out.dtype)
            first += out.shape[0]


def project(members, att, width, pieces, places, outs):
    share = att.shape[1]
    return pl.pallas_call(
        functools.partial(project_kernel, members, places),
        out_shape=[jax.ShapeDtypeStruct((count, width), kind) for count, kind in outs],
        in_specs=[VMEM] * (1 + len(pieces)),
        out_specs=[VMEM] * len(outs),
        scratch_shapes=[pltpu.VMEM((share, width), jnp.bfloat16)],
        compiler_params=pltpu.CompilerParams(vmem_limit_bytes=24 * 1024 * 1024),
        cost_estimate=pl.CostEstimate(
            flops=2 * att.shape[0] * share * width, bytes_accessed=2 * share * width, transcendentals=0
        ),
    )(att, *pieces)


def after(x, *others):
    if not others:
        return x
    return lax.optimization_barrier((x, *others))[0]


def per_device(parts, patch, query, key_new, value_new, key_stale, value_stale, exponents, w_out, gate):
    heads = exponents.shape[1] // 2
    rows, width = query.shape
    dim = width // heads
    groups = math.gcd(patch, heads)
    members = patch // groups
    share = width // groups
    depth, model = w_out.shape
    far = members // 2
    shared = parts % 2 == 0 and members == 4 and depth % 32 == 0
    first = model // 2

    def send(x, k, j):
        return lax.ppermute(x, "patch", [(p, ((p // members) ^ k) * members + (p % members) ^ j) for p in range(patch)])

    def swap(x):
        return lax.ppermute(x, "groups", [(g, g ^ 1) for g in range(parts)])

    def spread(pieces, bit):
        while bit:
            for j in list(pieces):
                pieces[j ^ bit] = send(pieces[j], 0, bit)
            bit //= 2
        return [pieces[j] for j in range(members)]

    if shared:
        w_part = share_rows(w_out)
        y_part = send(w_part, 0, far)
    own_query, fresh = prepare(groups, members, query, key_new, value_new, key_stale, value_stale, exponents.T)
    w_own = w_out
    order = range(groups - 1, 0, -1)
    arrived = [send(fresh[k], k, 0) for k in order]
    both = jnp.concatenate([x[:, share:] for x in arrived] + [fresh[0]], axis=0)
    if shared:
        both = after(both, y_part)
    kvs = spread({0: both}, far)
    blocks = dict(zip(order, arrived))
    blocks[0] = own_query
    line = [3, 1, 2, 0] if groups == 4 else [*order, 0]
    att = attend(groups, dim, [blocks[k] for k in line], kvs)

    jobs = []
    if shared:
        w_core = send(after(w_own, both), 0, 1)
        y_core = send(after(y_part, both), 0, 1)
        x_part = swap(y_part)
        edges = (0, first, model)
        for left, right in zip(edges, edges[1:]):
            x_core = send(after(x_part, att if left else kvs[far])[:, left:right], 0, 1)
            pieces = [w_own, w_core, y_part, x_part, y_core, x_core]
            places = [(0, None, left), (1, None, left), (2, 0, left), (2, 1, left), (3, 0, left), (3, 1, 0)]
            jobs.append((right - left, pieces, places))
    else:
        spots = (lax.axis_index("patch") % members) ^ jnp.arange(members)
        jobs.append((model, [jnp.stack(spread({0: w_own}, far))[spots].reshape(-1, model)], [(None, None, 0)]))
    half, full = jnp.bfloat16, jnp.float32

    def straight(att, width, pieces, places):
        sums = project(members, att, width, pieces, places, [(rows, half)] * (groups - 1) + [(rows, full)])
        total = sums[-1]
        taken = [send(part, k, 0) for k, part in sorted(zip(line, sums[:-1]), key=lambda x: -x[0])]
        for part in taken:
            total = total + part.astype(full)
        return sums, taken, total

    def paired(att, width, pieces, places):
        sums = project(members, att, width, pieces, places, [(2 * rows, half), (rows, full), (rows, full)])
        return sums, send(sums[0], 1, 0)

    def close(sums, near, gate_on):
        across = (sums[1] + near[:rows].astype(full)).astype(half)
        return sums[2] + near[rows:].astype(full) + send(after(across, *gate_on), 2, 0).astype(full)

    if len(jobs) == 2 and groups == 4:
        sums, near = paired(att, *jobs[0])
        _, taken, total = straight(after(att, *sums), *jobs[1])
        totals = [close(sums, near, []), total]
    else:
        totals = [straight(att, *job)[2] for job in jobs]
    return (jnp.concatenate(totals, axis=1) * gate[None, :]).astype(jnp.bfloat16)


def solution(mesh):
    return jax.shard_map(
        functools.partial(per_device, mesh.shape["groups"], mesh.shape["patch"]),
        mesh=mesh,
        in_specs=(
            P(("groups", "patch"), None),
            P(("groups", "patch"), None),
            P(("groups", "patch"), None),
            P("groups", None),
            P("groups", None),
            P("groups", None),
            P("patch", None),
            P("groups"),
        ),
        out_specs=P(("groups", "patch"), None),
        check_vma=False,
    )
```
